512 devices in a mesh: loop: 128 (over z, x_hi, y), rep: 4 (over x_lo, core).
Axes of the slice: x: 4 (x_hi: 2, x_lo: 2; x = x_hi * 2 + x_lo), y: 4, z: 16, core: 2. Of those that a mesh axis runs over, the one named last changes fastest.
Arguments:
- node_features: bfloat16 [524288, 256], P(('loop', 'rep')), may hold values from -6 to 6
- cotangent: bfloat16 [524288, 256], P(('loop', 'rep')), may hold values from -6 to 6
- adjacency: bfloat16 [128, 4, 24, 128, 128], P('loop', 'rep'), may hold values from -0.44140625 to 0.44140625
- block_index: int32 [128, 4, 2, 24], P('loop', 'rep'), may hold values from 0 to 13, as said below
- block_count: int32 [128, 4], P('loop', 'rep'), may hold values from 14 to 24, as said below
- send_rows: int32 [128, 4, 6, 128], P('loop', 'rep'), may hold values from 0 to 1023, as said below
- row_counts: int32 [128, 4, 6], P('loop', 'rep'), may hold values from 64 to 128, as said below
- message_weight: bfloat16 [256, 256], replicated, may hold values from -0.375 to 0.375
- input_weight: bfloat16 [512, 256], replicated, may hold values from -0.25 to 0.25
- input_bias: float32 [256], replicated, may hold values from -4 to 4
- output_weight: bfloat16 [256, 256], replicated, may hold values from -0.375 to 0.375
- norm_gain: float32 [256], replicated, may hold values from 0.25 to 1.75
Outputs:
- new_features: bfloat16 [524288, 256], P(('loop', 'rep'))
- grad_features: bfloat16 [524288, 256], P(('loop', 'rep'))
- grad_message_weight: float32 [256, 256], P('rep')
- grad_input_weight: float32 [512, 256], P('rep')
- grad_input_bias: float32 [256], P('rep')
- grad_output_weight: float32 [256, 256], P('rep')
- grad_norm_gain: float32 [256], P('rep')
The draws below stay inside these ranges and needn't reach their ends.
Inputs may be any that keep to these rules, and one draw needn't show every extreme that they name: `block_index`: row 0 holds the destination row block (below 8) and row 1 the source block of the table of each slot. Among the live slots every row block of the partition is paired with its own block of the table, and every block of the table is a source. The live slots are the first block_count ones. `send_rows`: each list holds distinct rows of its partition; list 0 goes to loop index + 1, list 1 to loop index - 1, list 2 + q to rep index q of the same loop index. `row_counts`: in every draw some partition receives full lists from all its peers.
All inputs are finite; a program needn't handle non-finite values.
Results may differ from the reference program's by a relative error of at most 0.008.
Values may be sent and summed in bfloat16 or wider, within the bound.
A program may use at most 64 MiB of HBM per device.

```python
import math
import jax
import jax.numpy as jnp
from jax import lax

D = 256
BLOCK = 128
ROWS = 1024
SLOTS = 24
NODES = 524288
N_LOOP = 128
N_REP = 4


def draw_block_index(key, part):
    num_blocks = ROWS // BLOCK
    table_blocks = num_blocks + 2 + N_REP
    first_key, second_key, third_key = jax.random.split(key, 3)
    shape_all = (N_LOOP, N_REP, SLOTS)
    slot_ids = jnp.broadcast_to(jnp.arange(SLOTS, dtype=jnp.int32)[None, None, :], shape_all)
    random_dest = jax.random.randint(first_key, shape_all, 0, num_blocks)
    random_source = jax.random.randint(second_key, shape_all, 0, table_blocks)
    covering = slot_ids < table_blocks
    dest_part = jnp.where(slot_ids < num_blocks, slot_ids, random_dest)
    source_part = jnp.where(covering, slot_ids, random_source)
    scores = jax.random.randint(third_key, shape_all, 0, 1 << 16) * SLOTS + slot_ids
    scores = jnp.where(covering, scores, (1 << 28) + slot_ids)
    ordering = jnp.argsort(scores, axis=-1, stable=True)
    dest_part = jnp.take_along_axis(dest_part, ordering, axis=-1)
    source_part = jnp.take_along_axis(source_part, ordering, axis=-1)
    return jnp.stack([dest_part, source_part], axis=2).astype(jnp.int32)


def draw_block_count(key, part):
    table_blocks = ROWS // BLOCK + 2 + N_REP
    first_key, second_key = jax.random.split(key)
    counts = jax.random.randint(first_key, (N_LOOP * N_REP,), table_blocks, SLOTS + 1)
    chosen = jax.random.randint(second_key, (), 0, N_LOOP * N_REP)
    counts = counts.at[chosen].set(SLOTS)
    return counts.reshape(N_LOOP, N_REP).astype(jnp.int32)


def draw_send_rows(key, part):
    total_lists = N_LOOP * N_REP * (2 + N_REP)
    keys_all = jax.random.split(key, total_lists)
    permuted = jax.vmap(lambda single_key: jax.random.permutation(single_key, ROWS))(keys_all)
    return permuted[:, :BLOCK].reshape(N_LOOP, N_REP, 2 + N_REP, BLOCK).astype(jnp.int32)


def draw_row_counts(key, part):
    shape_all = (N_LOOP, N_REP, 2 + N_REP)
    first_key, second_key, third_key = jax.random.split(key, 3)
    counts = jax.random.randint(first_key, shape_all, BLOCK // 2, BLOCK + 1)
    chosen_loop = jax.random.randint(second_key, (), 0, N_LOOP)
    chosen_rep = jax.random.randint(third_key, (), 0, N_REP)
    loop_ids = jnp.arange(N_LOOP, dtype=jnp.int32)[:, None, None]
    rep_ids = jnp.arange(N_REP, dtype=jnp.int32)[None, :, None]
    list_ids = jnp.arange(2 + N_REP, dtype=jnp.int32)[None, None, :]
    from_below = (loop_ids == (chosen_loop + N_LOOP - 1) % N_LOOP) & (rep_ids == chosen_rep) & (list_ids == 0)
    from_above = (loop_ids == (chosen_loop + 1) % N_LOOP) & (rep_ids == chosen_rep) & (list_ids == 1)
    from_group = (loop_ids == chosen_loop) & (list_ids == 2 + chosen_rep)
    filled = from_below | from_above | from_group
    return jnp.where(filled, BLOCK, counts).astype(jnp.int32)


def block_scale(own_key, extent, shards, low, top_value):
    level, own = 1.0, jax.random.fold_in(own_key, 6)
    for position, parts in shards:
        steps = jnp.exp(jax.random.uniform(jax.random.fold_in(own, position), (parts,), jnp.float32, low / len(shards), top_value / len(shards)))
        level = level * jnp.repeat(steps, extent[position] // parts).reshape([-1 if axis == position else 1 for axis in range(len(extent))])
    return level


def bell_draw(stream_key, dims, scale, most, pieces=(), kind=jnp.bfloat16):
    values = scale * jax.random.normal(stream_key, dims, jnp.float32)
    if pieces:
        values = values * block_scale(stream_key, dims, pieces, -0.22, 0.18)
    return jnp.clip(values, -most, most).astype(kind)


def setup_inputs(seed: int = 0) -> dict:
    seeds = jax.random.split(jax.random.key(seed), 13)
    return {
        "node_features": bell_draw(seeds[0], (NODES, D), 1.0, 6.0, ((0, 512),)),
        "cotangent": bell_draw(seeds[1], (NODES, D), 1.0, 6.0, ((0, 512),)),
        "adjacency": bell_draw(seeds[2], (N_LOOP, N_REP, SLOTS, BLOCK, BLOCK), (1.0 / BLOCK ** 0.5), 0.44140625, ((0, 128), (1, 4))),
        "block_index": draw_block_index(jax.random.fold_in(seeds[12], 71), 0),
        "block_count": draw_block_count(jax.random.fold_in(seeds[12], 71), 0),
        "send_rows": draw_send_rows(jax.random.fold_in(seeds[12], 71), 0),
        "row_counts": draw_row_counts(jax.random.fold_in(seeds[12], 71), 0),
        "message_weight": bell_draw(seeds[7], (D, D), D ** -0.5, 0.375),
        "input_weight": bell_draw(seeds[8], (2 * D, D), (2 * D) ** -0.5, 0.25),
        "input_bias": bell_draw(seeds[9], (D,), 1.0, 4.0, (), jnp.float32),
        "output_weight": bell_draw(seeds[10], (D, D), D ** -0.5, 0.375),
        "norm_gain": jnp.clip(1.0 + 0.15 * jax.random.normal(seeds[11], (D,), jnp.float32), 0.25, 1.75),
    }


norm_eps = 1e-05

def silu_slope(argument):
    sigmoid_of = jax.nn.sigmoid(argument)
    return sigmoid_of * (1.0 + argument * (1.0 - sigmoid_of))

def layer_stats(values_in):
    centered = values_in - lax.optimization_barrier(jnp.mean(values_in, axis=-1, keepdims=True))
    inv_std = lax.rsqrt(lax.optimization_barrier(jnp.mean(centered * centered, axis=-1, keepdims=True)) + norm_eps)
    return (centered * inv_std, inv_std)

def inner_rows(left_side, right_side):
    return lax.dot_general(left_side, right_side, (((0,), (0,)), ((), ())), preferred_element_type=jnp.float32)

def gather_forward(table_dev, adj_dev, index_dev, count_dev):
    num_blocks = ROWS // BLOCK
    sources = jnp.take(table_dev, index_dev[1], axis=0)
    products = jnp.einsum('sij,sjd->sid', adj_dev.astype(jnp.float32), sources.astype(jnp.float32), precision=lax.Precision.HIGHEST)
    slot_live = (jnp.arange(SLOTS, dtype=jnp.int32) < count_dev).astype(jnp.float32)
    placing = (index_dev[0][None, :] == jnp.arange(num_blocks, dtype=jnp.int32)[:, None]).astype(jnp.float32) * slot_live[None, :]
    summed = jnp.einsum('bs,sid->bid', placing, products, precision=lax.Precision.HIGHEST)
    return summed.reshape(ROWS, -1).astype(jnp.bfloat16)

def scatter_backward(grad_dev, adj_dev, index_dev, count_dev):
    num_blocks = ROWS // BLOCK
    table_blocks = num_blocks + 2 + N_REP
    picked = jnp.take(grad_dev.reshape(num_blocks, BLOCK, -1), index_dev[0], axis=0)
    slot_live = (jnp.arange(SLOTS, dtype=jnp.int32) < count_dev).astype(jnp.float32)
    backs = jnp.einsum('sij,sid->sjd', adj_dev.astype(jnp.float32), picked.astype(jnp.float32), precision=lax.Precision.HIGHEST)
    backs = backs * slot_live[:, None, None]
    owning = (index_dev[1][None, :] == jnp.arange(table_blocks, dtype=jnp.int32)[:, None]).astype(jnp.float32)
    return jnp.einsum('ts,sjd->tjd', owning, backs, precision=lax.Precision.HIGHEST)

def reference(node_features, cotangent, adjacency, block_index, block_count, send_rows, row_counts, message_weight, input_weight, input_bias, output_weight, norm_gain):
    feat_width = node_features.shape[1]
    devices_all = N_LOOP * N_REP
    num_blocks = ROWS // BLOCK
    table_blocks = num_blocks + 2 + N_REP
    message_pre = jnp.dot(node_features, message_weight, preferred_element_type=jnp.float32)
    message = jax.nn.silu(message_pre).astype(jnp.bfloat16)
    base_rows = (jnp.arange(devices_all, dtype=jnp.int32) * ROWS).reshape(N_LOOP, N_REP, 1, 1)
    flat_index = (send_rows + base_rows).reshape(-1)
    row_keep = jnp.arange(BLOCK, dtype=jnp.int32)[None, None, None, :] < row_counts[:, :, :, None]
    outgoing = jnp.take(message, flat_index, axis=0).reshape(N_LOOP, N_REP, 2 + N_REP, BLOCK, feat_width)
    outgoing = jnp.where(row_keep[..., None], outgoing, jnp.zeros_like(outgoing))
    from_left = jnp.roll(outgoing[:, :, 0], 1, axis=0)
    from_right = jnp.roll(outgoing[:, :, 1], -1, axis=0)
    from_peers = jnp.swapaxes(outgoing[:, :, 2:], 1, 2).reshape(N_LOOP, N_REP, N_REP * BLOCK, feat_width)
    table = jnp.concatenate([message.reshape(N_LOOP, N_REP, ROWS, feat_width), from_left, from_right, from_peers], axis=2)
    table = table.reshape(devices_all, table_blocks, BLOCK, feat_width)
    adj_flat = adjacency.reshape(devices_all, SLOTS, BLOCK, BLOCK)
    index_flat = block_index.reshape(devices_all, 2, SLOTS)
    count_flat = block_count.reshape(devices_all)
    aggregate = lax.map(lambda packed: gather_forward(*packed), (table, adj_flat, index_flat, count_flat))
    aggregate = aggregate.reshape(-1, feat_width)
    joined = jnp.concatenate([node_features, aggregate], axis=1)
    pre_act = jnp.dot(joined, input_weight, preferred_element_type=jnp.float32) + input_bias
    hidden = jax.nn.silu(pre_act).astype(jnp.bfloat16)
    outer = jnp.dot(hidden, output_weight, preferred_element_type=jnp.float32)
    normed, inv_std = layer_stats(outer)
    new_features = (node_features.astype(jnp.float32) + normed * norm_gain).astype(jnp.bfloat16)
    grad_scale = 1.0 / math.sqrt(NODES)
    upstream = cotangent.astype(jnp.float32)
    gained = upstream * norm_gain
    outer_grad = ((gained - lax.optimization_barrier(jnp.mean(gained, axis=-1, keepdims=True)) - normed * lax.optimization_barrier(jnp.mean(gained * normed, axis=-1, keepdims=True))) * inv_std).astype(jnp.bfloat16)
    grad_norm_gain = grad_scale * lax.optimization_barrier(jnp.sum(upstream * normed, axis=0))
    grad_output_weight = grad_scale * inner_rows(hidden, outer_grad)
    pre_grad = (jnp.dot(outer_grad, output_weight.T, preferred_element_type=jnp.float32) * silu_slope(pre_act)).astype(jnp.bfloat16)
    grad_input_weight = grad_scale * inner_rows(joined, pre_grad)
    grad_input_bias = grad_scale * lax.optimization_barrier(jnp.sum(pre_grad.astype(jnp.float32), axis=0))
    joined_grad = jnp.dot(pre_grad, input_weight.T, preferred_element_type=jnp.float32)
    aggregate_grad = joined_grad[:, feat_width:].astype(jnp.bfloat16)
    table_grad = lax.map(lambda packed: scatter_backward(*packed), (aggregate_grad.reshape(devices_all, ROWS, feat_width), adj_flat, index_flat, count_flat))
    table_grad = table_grad.reshape(N_LOOP, N_REP, table_blocks, BLOCK, feat_width)
    own_part = table_grad[:, :, :num_blocks].reshape(-1, feat_width)
    back_up = jnp.roll(table_grad[:, :, num_blocks], -1, axis=0)
    back_down = jnp.roll(table_grad[:, :, num_blocks + 1], 1, axis=0)
    back_peers = jnp.swapaxes(table_grad[:, :, num_blocks + 2:], 1, 2)
    returned = jnp.concatenate([back_up[:, :, None], back_down[:, :, None], back_peers], axis=2)
    returned = jnp.where(row_keep[..., None], returned, jnp.zeros_like(returned))
    message_grad = own_part.at[flat_index].add(returned.reshape(-1, feat_width))
    message_pre_grad = (message_grad * silu_slope(message_pre)).astype(jnp.bfloat16)
    grad_message_weight = grad_scale * inner_rows(node_features, message_pre_grad)
    grad_features = (upstream + joined_grad[:, :feat_width] + jnp.dot(message_pre_grad, message_weight.T, preferred_element_type=jnp.float32)).astype(jnp.bfloat16)
    return (new_features, grad_features, grad_message_weight, grad_input_weight, grad_input_bias, grad_output_weight, grad_norm_gain)
```

```python
import functools
import math

import jax
import jax.numpy as jnp
from jax import lax
from jax.experimental import pallas as pl
from jax.experimental.pallas import tpu as pltpu
from jax.sharding import PartitionSpec as P

norm_eps = 1e-05
MESH = pl.DeviceIdType.MESH


def shifted(shard, axis, by):
    size = lax.axis_size(axis)
    return lax.ppermute(shard, axis, [(i, (i + by) % size) for i in range(size)])


def silu_slope(argument):
    sigmoid_of = jax.nn.sigmoid(argument)
    return sigmoid_of * (1.0 + argument * (1.0 - sigmoid_of))


def layer_stats(values_in):
    centered = values_in - jnp.mean(values_in, axis=-1, keepdims=True)
    inv_std = lax.rsqrt(jnp.mean(centered * centered, axis=-1, keepdims=True) + norm_eps)
    return (centered * inv_std, inv_std)


def inner_rows(left_side, right_side):
    return lax.dot_general(
        left_side, right_side, (((0,), (0,)), ((), ())), preferred_element_type=jnp.float32
    )


def plane_of(loop_size):
    plane = 8 if loop_size % 8 == 0 and loop_size > 8 else 2
    return plane, loop_size // plane


def reduce_kernel(
    plane, depth, reps, scale,
    mw_ref, iw_ref, ow_ref, vec_ref,
    out_mw, out_iw, out_ow, out_vec,
    stage, landed, zsend, zland, zpiece, zgather, gpiece, gather,
    send_sem, recv_sem,
):
    sub = 8 // plane
    loop_at, rep_at = lax.axis_index("loop"), lax.axis_index("rep")
    z_at, g_at = loop_at // plane, lax.rem(loop_at, plane)
    team = reps * plane
    team_at = rep_at * plane + g_at

    def mate(step):
        other = lax.rem(team_at + step, team)
        r_to, g_to = other // plane, lax.rem(other, plane)
        return other, {"loop": z_at * plane + g_to, "rep": r_to}

    def above(step):
        z_to = lax.rem(z_at + step, depth)
        return z_to, {"loop": z_to * plane + g_at, "rep": rep_at}

    barrier = pltpu.get_barrier_semaphore()

    @pl.loop(1, team)
    def _(step):
        pl.semaphore_signal(barrier, inc=1, device_id=mate(step)[1], device_id_type=MESH)

    @pl.loop(1, depth)
    def _(step):
        pl.semaphore_signal(barrier, inc=1, device_id=above(step)[1], device_id_type=MESH)

    for rep in range(reps):
        for tile in range(8):
            row, half = 16 * (tile // 2), 128 * (tile % 2)
            slot, place = rep * plane + tile // sub, 64 * (tile % sub)
            for first, source, tall in ((0, ow_ref, 1), (16, iw_ref, 2), (48, mw_ref, 1)):
                start = (64 * rep + row) * tall
                block = source[start : start + 16 * tall, half : half + 128]
                stage[slot, place + first : place + first + 16 * tall, :] = block.astype(jnp.bfloat16)
        for g in range(plane):
            stage[rep * plane + g, 64 * sub :, :] = jnp.broadcast_to(
                vec_ref[rep : rep + 1, :], (16, 128)
            ).astype(jnp.bfloat16)

    landed[team_at] = stage[team_at]
    pl.semaphore_wait(barrier, team + depth - 2)

    @pl.loop(1, team)
    def _(step):
        other, device = mate(step)
        pltpu.make_async_remote_copy(
            stage.at[other], landed.at[team_at], send_sem.at[0], recv_sem.at[0],
            device_id=device, device_id_type=MESH,
        ).start()

    pltpu.make_async_copy(landed.at[1:], landed.at[1:], recv_sem.at[0]).wait()
    total = landed[0].astype(jnp.float32)
    for slot in range(1, team):
        total = total + landed[slot].astype(jnp.float32)

    rows = 64 * sub // depth
    for z in range(depth):
        zsend[z, 0:rows, :] = total[z * rows : (z + 1) * rows]
        zsend[z, rows : rows + 1, :] = total[64 * sub : 64 * sub + 1]
        zsend[z, rows + 1 :, :] = jnp.zeros((zsend.shape[1] - rows - 1, 128), jnp.float32)
    zland[z_at] = zsend[z_at]

    @pl.loop(1, depth)
    def _(step):
        z_to, device = above(step)
        pltpu.make_async_remote_copy(
            zsend.at[z_to], zland.at[z_at], send_sem.at[1], recv_sem.at[1],
            device_id=device, device_id_type=MESH,
        ).start()

    pltpu.make_async_copy(zland.at[1:], zland.at[1:], recv_sem.at[1]).wait()
    total = zland[0]
    for z in range(1, depth):
        total = total + zland[z]
    total = total * scale
    out_vec[...] = total[rows : rows + 1]
    zpiece[...] = total[0:rows]
    zgather[z_at] = total[0:rows]

    @pl.loop(1, depth)
    def _(step):
        z_to, device = above(step)
        pltpu.make_async_remote_copy(
            zpiece, zgather.at[z_at], send_sem.at[2], recv_sem.at[2],
            device_id=device, device_id_type=MESH,
        ).start()

    pltpu.make_async_copy(zgather.at[1:], zgather.at[1:], recv_sem.at[2]).wait()
    piece = jnp.concatenate([zgather[z] for z in range(depth)], axis=0).astype(jnp.bfloat16)
    gpiece[...] = piece
    gather[g_at] = piece

    @pl.loop(1, plane)
    def _(step):
        g_to = lax.rem(g_at + step, plane)
        pltpu.make_async_remote_copy(
            gpiece, gather.at[g_at], send_sem.at[3], recv_sem.at[3],
            device_id={"loop": z_at * plane + g_to, "rep": rep_at}, device_id_type=MESH,
        ).start()

    pltpu.make_async_copy(gather.at[1:], gather.at[1:], recv_sem.at[3]).wait()
    for tile in range(8):
        row, half = 16 * (tile // 2), 128 * (tile % 2)
        slot, place = tile // sub, 64 * (tile % sub)
        for first, out, tall in ((0, out_ow, 1), (16, out_iw, 2), (48, out_mw, 1)):
            block = gather[slot, place + first : place + first + 16 * tall, :]
            out[row * tall : (row + 16) * tall, half : half + 128] = block.astype(jnp.float32)

    for sem, sent in ((0, landed.at[1:]), (1, zland.at[1:]), (2, zgather.at[1:]), (3, gather.at[1:])):
        pltpu.make_async_copy(sent, sent, send_sem.at[sem]).wait()


def reduce_all(mw, iw, ow, bias, gain, scale):
    loop_size, reps = lax.axis_size("loop"), lax.axis_size("rep")
    plane, depth = plane_of(loop_size)
    sub = 8 // plane
    tall = 64 * sub + 16
    rows = 64 * sub // depth
    zrows = -(-(rows + 1) // 8) * 8
    vec = jnp.concatenate([bias.reshape(reps, -1), gain.reshape(reps, -1)], axis=1)
    f32 = jnp.float32
    outs = pl.pallas_call(
        functools.partial(reduce_kernel, plane, depth, reps, scale),
        out_shape=(
            jax.ShapeDtypeStruct((mw.shape[0] // reps, 256), f32),
            jax.ShapeDtypeStruct((iw.shape[0] // reps, 256), f32),
            jax.ShapeDtypeStruct((ow.shape[0] // reps, 256), f32),
            jax.ShapeDtypeStruct((1, 128), f32),
        ),
        in_specs=[pl.BlockSpec(memory_space=pltpu.VMEM)] * 4,
        out_specs=[pl.BlockSpec(memory_space=pltpu.VMEM)] * 4,
        scratch_shapes=[
            pltpu.VMEM((reps * plane, tall, 128), jnp.bfloat16),
            pltpu.VMEM((reps * plane, tall, 128), jnp.bfloat16),
            pltpu.VMEM((depth, zrows, 128), f32),
            pltpu.VMEM((depth, zrows, 128), f32),
            pltpu.VMEM((rows, 128), f32),
            pltpu.VMEM((depth, rows, 128), f32),
            pltpu.VMEM((64 * sub, 128), jnp.bfloat16),
            pltpu.VMEM((plane, 64 * sub, 128), jnp.bfloat16),
            pltpu.SemaphoreType.DMA((4,)),
            pltpu.SemaphoreType.DMA((4,)),
        ],
        compiler_params=pltpu.CompilerParams(
            collective_id=0, has_side_effects=True, vmem_limit_bytes=32 * 1024 * 1024
        ),
        name="reduce_gradients",
    )(mw, iw, ow, vec)
    return outs[0], outs[1], outs[2], outs[3][0, :64], outs[3][0, 64:]


def shards(
    node_features,
    cotangent,
    adjacency,
    block_index,
    block_count,
    send_rows,
    row_counts,
    message_weight,
    input_weight,
    input_bias,
    output_weight,
    norm_gain,
):
    node_rows, feat_width = node_features.shape
    block_rows = adjacency.shape[-1]
    slot_total = adjacency.shape[2]
    peer_total = lax.axis_size("rep")
    num_blocks = node_rows // block_rows
    table_blocks = num_blocks + 2 + peer_total
    adj_local = adjacency[0, 0]
    dest_index = block_index[0, 0, 0]
    source_index = block_index[0, 0, 1]
    slot_live = (jnp.arange(slot_total, dtype=jnp.int32) < block_count[0, 0]).astype(jnp.float32)
    row_lists = send_rows[0, 0]
    row_keep = jnp.arange(block_rows, dtype=jnp.int32)[None, :] < row_counts[0, 0][:, None]
    message_pre = jnp.dot(node_features, message_weight, preferred_element_type=jnp.float32)
    message = jax.nn.silu(message_pre).astype(jnp.bfloat16)
    outgoing = jnp.take(message, row_lists.reshape(-1), axis=0).reshape(
        2 + peer_total, block_rows, feat_width
    )
    outgoing = jnp.where(row_keep[:, :, None], outgoing, jnp.zeros_like(outgoing))
    from_left = shifted(outgoing[0], "loop", 1)
    from_right = shifted(outgoing[1], "loop", -1)
    from_peers = lax.all_to_all(outgoing[2:], "rep", split_axis=0, concat_axis=0, tiled=True)
    table = jnp.concatenate(
        [message, from_left, from_right, from_peers.reshape(peer_total * block_rows, feat_width)],
        axis=0,
    )
    table = table.reshape(table_blocks, block_rows, feat_width)
    sources = jnp.take(table, source_index, axis=0)
    products = jnp.einsum("sij,sjd->sid", adj_local, sources, preferred_element_type=jnp.float32)
    placing = (dest_index[None, :] == jnp.arange(num_blocks, dtype=jnp.int32)[:, None]).astype(
        jnp.float32
    ) * slot_live[None, :]
    aggregate = jnp.einsum("bs,sid->bid", placing, products, precision=lax.Precision.HIGHEST)
    aggregate = aggregate.reshape(node_rows, feat_width).astype(jnp.bfloat16)
    joined = jnp.concatenate([node_features, aggregate], axis=1)
    pre_act = jnp.dot(joined, input_weight, preferred_element_type=jnp.float32) + input_bias
    hidden = jax.nn.silu(pre_act).astype(jnp.bfloat16)
    outer = jnp.dot(hidden, output_weight, preferred_element_type=jnp.float32)
    normed, inv_std = layer_stats(outer)
    new_features = (node_features.astype(jnp.float32) + normed * norm_gain).astype(jnp.bfloat16)
    upstream = cotangent.astype(jnp.float32)
    gained = upstream * norm_gain
    outer_grad = (
        (
            gained
            - jnp.mean(gained, axis=-1, keepdims=True)
            - normed * jnp.mean(gained * normed, axis=-1, keepdims=True)
        )
        * inv_std
    ).astype(jnp.bfloat16)
    pre_grad = (
        jnp.dot(outer_grad, output_weight.T, preferred_element_type=jnp.float32)
        * silu_slope(pre_act)
    ).astype(jnp.bfloat16)
    joined_grad = jnp.dot(pre_grad, input_weight.T, preferred_element_type=jnp.float32)
    aggregate_grad = joined_grad[:, feat_width:].astype(jnp.bfloat16)
    picked = jnp.take(
        aggregate_grad.reshape(num_blocks, block_rows, feat_width), dest_index, axis=0
    )
    backs = (
        jnp.einsum("sij,sid->sjd", adj_local, picked, preferred_element_type=jnp.float32)
        * slot_live[:, None, None]
    )
    owning = (source_index[None, :] == jnp.arange(table_blocks, dtype=jnp.int32)[:, None]).astype(
        jnp.float32
    )
    table_grad = jnp.einsum("ts,sjd->tjd", owning, backs, precision=lax.Precision.HIGHEST)
    own_part = table_grad[:num_blocks].reshape(node_rows, feat_width)
    back_up = shifted(table_grad[num_blocks], "loop", -1)
    back_down = shifted(table_grad[num_blocks + 1], "loop", 1)
    back_peers = lax.all_to_all(
        table_grad[num_blocks + 2 :], "rep", split_axis=0, concat_axis=0, tiled=True
    )
    returned = jnp.concatenate([back_up[None], back_down[None], back_peers], axis=0)
    returned = jnp.where(row_keep[:, :, None], returned, jnp.zeros_like(returned))
    message_grad = own_part.at[row_lists.reshape(-1)].add(returned.reshape(-1, feat_width))
    message_pre_grad = (message_grad * silu_slope(message_pre)).astype(jnp.bfloat16)
    grad_features = (
        upstream
        + joined_grad[:, :feat_width]
        + jnp.dot(message_pre_grad, message_weight.T, preferred_element_type=jnp.float32)
    ).astype(jnp.bfloat16)
    partials = (
        inner_rows(node_features, message_pre_grad),
        inner_rows(joined, pre_grad),
        jnp.sum(pre_grad.astype(jnp.float32), axis=0),
        inner_rows(hidden, outer_grad),
        jnp.sum(upstream * normed, axis=0),
    )
    grad_scale = 1.0 / math.sqrt(node_rows * lax.axis_size("loop") * peer_total)
    grad_mw, grad_iw, grad_ow, grad_bias, grad_gain = reduce_all(
        partials[0], partials[1], partials[3], partials[2], partials[4], grad_scale
    )
    return (new_features, grad_features, grad_mw, grad_iw, grad_bias, grad_ow, grad_gain)


def solution(mesh):
    in_specs = (
        P(("loop", "rep"), None),
        P(("loop", "rep"), None),
        P("loop", "rep", None, None, None),
        P("loop", "rep", None, None),
        P("loop", "rep"),
        P("loop", "rep", None, None),
        P("loop", "rep", None),
        P(),
        P(),
        P(),
        P(),
        P(),
    )
    out_specs = (
        P(("loop", "rep"), None),
        P(("loop", "rep"), None),
        P("rep", None),
        P("rep", None),
        P("rep"),
        P("rep", None),
        P("rep"),
    )
    return jax.shard_map(shards, mesh=mesh, in_specs=in_specs, out_specs=out_specs, check_vma=False)
```

```python
import functools
import math

import jax
import jax.numpy as jnp
from jax import lax
from jax.experimental import pallas as pl
from jax.experimental.pallas import tpu as pltpu
from jax.sharding import PartitionSpec as P

norm_eps = 1e-05
MESH = pl.DeviceIdType.MESH
BF16, F32 = jnp.bfloat16, jnp.float32


def dot(left, right):
    return jnp.dot(left, right, preferred_element_type=F32)


def dot_right_t(left, right):
    return lax.dot_general(left, right, (((1,), (1,)), ((), ())), preferred_element_type=F32)


def inner_rows(left, right):
    return lax.dot_general(left, right, (((0,), (0,)), ((), ())), preferred_element_type=F32)


def sigmoid(argument):
    return 0.5 * jnp.tanh(0.5 * argument) + 0.5


def row_mean(values):
    return jnp.sum(values, axis=-1, keepdims=True) * (1.0 / values.shape[-1])


def plane_of(loop_size):
    plane = 8 if loop_size % 8 == 0 and loop_size > 8 else 2
    return plane, loop_size // plane


def copy_all(buffer, sem):
    return pltpu.make_async_copy(buffer, buffer, sem)


def slot_order(key_col, key_row, cols):
    shape = (32, 128)
    slot = lax.broadcasted_iota(jnp.int32, shape, 0)
    lane = lax.broadcasted_iota(jnp.int32, shape, 1)
    ahead = (key_row < key_col) | ((key_row == key_col) & (lane < slot))
    rank = jnp.sum(jnp.where(ahead & (lane < 24), 1, 0), axis=1, keepdims=True)
    placed = (rank == lane) & (slot < 24)
    rows = [
        jnp.sum(jnp.where(placed, col, 0), axis=0, keepdims=True) for col in (slot, *cols, key_col)
    ]
    before = pltpu.roll(rows[-1], 1, 1)
    keep = jnp.where((rows[-1] == before) & (lane[:1] > 0), 1, 0)
    last = jnp.sum(jnp.where((key_col <= lane) & (slot < 24), 1, 0), axis=0, keepdims=True) - 1
    last = jnp.maximum(last, 0)
    return [*rows[:-1], keep, last]


def layer_kernel(
    plane, depth, reps, scale,
    nf_ref, cot_ref, adj_ref, index_ref, count_ref, rows_ref, kept_ref,
    wm_ref, wi_ref, bias_ref, wo_ref, gain_ref,
    out_new, out_grad, out_mw, out_iw, out_ow, out_vec,
    flat, meta_v, meta_s, hout, hin, rout, rin, spread, table, slope, pre_part, run,
    agg, hidden, outer_grad, pre_grad, agg_grad, base, own_grad, halo_grad,
    stage_e, land_e, stage_l, land_l, zsend, zland, zpiece, zgather, gpiece, gather,
    meta_sem, send_sem, recv_sem,
):
    sub = 8 // plane
    node_rows = nf_ref.shape[0]
    blocks = node_rows // 128
    peers = 2 + reps
    loop_size = plane * depth
    loop_at, rep_at = lax.axis_index("loop"), lax.axis_index("rep")
    z_at, g_at = loop_at // plane, lax.rem(loop_at, plane)
    team = reps * plane
    team_at = rep_at * plane + g_at
    loop_up = {"loop": lax.rem(loop_at + 1, loop_size), "rep": rep_at}
    loop_down = {"loop": lax.rem(loop_at + loop_size - 1, loop_size), "rep": rep_at}

    def mate(step):
        other = lax.rem(team_at + step, team)
        r_to, g_to = other // plane, lax.rem(other, plane)
        return other, {"loop": z_at * plane + g_to, "rep": r_to}

    def above(step):
        z_to = lax.rem(z_at + step, depth)
        return z_to, {"loop": z_to * plane + g_at, "rep": rep_at}

    def send(source, target, sem, device):
        pltpu.make_async_remote_copy(
            source, target, send_sem.at[sem], recv_sem.at[sem], device_id=device, device_id_type=MESH
        ).start()

    barrier = pltpu.get_barrier_semaphore()
    for device in (loop_up, loop_down):
        pl.semaphore_signal(barrier, inc=1, device_id=device, device_id_type=MESH)

    @pl.loop(1, team)
    def _(step):
        pl.semaphore_signal(barrier, inc=1, device_id=mate(step)[1], device_id_type=MESH)

    @pl.loop(1, depth)
    def _(step):
        pl.semaphore_signal(barrier, inc=1, device_id=above(step)[1], device_id_type=MESH)

    flat[...] = jnp.zeros(flat.shape, jnp.int32)
    flat[0:2, 0:24] = index_ref[...]
    flat[8 : 8 + peers, :] = rows_ref[...]
    turned = jnp.transpose(flat[...])
    lane_rows = lax.broadcasted_iota(jnp.int32, (128, node_rows), 1)
    sub_rows = lax.broadcasted_iota(jnp.int32, (128, node_rows), 0)
    for k in range(peers):
        named = turned[:, 8 + k : 9 + k]
        live = (lane_rows == named) & (sub_rows < kept_ref[0, k])
        picker = jnp.where(live, 1.0, 0.0).astype(BF16)
        hout[k] = dot(picker, nf_ref[...]).astype(BF16)
    hin[2 + rep_at] = hout[2 + rep_at]

    pl.semaphore_wait(barrier, team + depth)
    send(hout.at[0], hin.at[0], 0, loop_up)
    send(hout.at[1], hin.at[1], 0, loop_down)

    @pl.loop(1, reps)
    def _(step):
        r_to = lax.rem(rep_at + step, reps)
        send(hout.at[2 + r_to], hin.at[2 + rep_at], 0, {"loop": loop_at, "rep": r_to})

    live_total = count_ref[0, 0]
    slot_col = lax.broadcasted_iota(jnp.int32, (32, 1), 0)
    slot_row = lax.broadcasted_iota(jnp.int32, (1, 128), 1)
    dest_col, source_col = turned[0:32, 0:1], turned[0:32, 1:2]
    dest_row, source_row = flat[0:1, :], flat[1:2, :]

    def keyed(value, iota):
        return jnp.where(iota < live_total, value, 64)

    def halo_first(value):
        return jnp.where(value >= blocks, value - blocks, value + peers)

    forward = slot_order(
        keyed(dest_col, slot_col), keyed(dest_row, slot_row), (source_col,)
    )
    backward = slot_order(
        keyed(halo_first(source_col), slot_col), keyed(halo_first(source_row), slot_row),
        (dest_col,),
    )
    meta_v[...] = jnp.concatenate(forward + backward, axis=0)
    meta_copy = pltpu.make_async_copy(meta_v, meta_s, meta_sem)
    meta_copy.start()

    @pl.loop(0, node_rows // 256)
    def _(c):
        at = pl.ds(pl.multiple_of(c * 256, 256), 256)
        features = nf_ref[at, :]
        pre = dot(features, wm_ref[...])
        gate = sigmoid(pre)
        table[pl.ds(2 * c, 2)] = (pre * gate).astype(BF16).reshape(2, 128, 256)
        slope[at, :] = gate * (1.0 + pre * (1.0 - gate))
        pre_part[at, :] = dot(features, wi_ref[0:256, :]) + bias_ref[...]

    row_at = lax.broadcasted_iota(jnp.int32, (node_rows, 128), 0)
    lane_at = lax.broadcasted_iota(jnp.int32, (node_rows, 128), 1)
    for k in range(peers):
        live = (row_at == rows_ref[k : k + 1, :]) & (lane_at < kept_ref[0, k])
        spread[:, 128 * k : 128 * k + 128] = jnp.where(live, 1.0, 0.0).astype(BF16)

    meta_copy.wait()
    copy_all(hin.at[1:], recv_sem.at[0]).wait()
    copy_all(hin.at[1:], send_sem.at[0]).wait()

    @pl.loop(0, peers)
    def _(k):
        at = pl.ds(pl.multiple_of(node_rows + k * 128, 128), 128)
        pre = dot(hin[k], wm_ref[...])
        gate = sigmoid(pre)
        table[blocks + k] = (pre * gate).astype(BF16)
        slope[at, :] = gate * (1.0 + pre * (1.0 - gate))

    def forward_slots(c, total):
        for lap in range(4):
            i = c * 4 + lap
            product = dot(adj_ref[meta_s[0, i]], table[meta_s[1, i]])
            total = product + total * meta_s[2, i].astype(F32)
            run[i] = total
        return total

    lax.fori_loop(0, 6, forward_slots, jnp.zeros((128, 256), F32))

    def node_update(c, sums):
        at = pl.ds(pl.multiple_of(c * 256, 256), 256)
        gathered = jnp.concatenate(
            [run[meta_s[3, 2 * c]], run[meta_s[3, 2 * c + 1]]], axis=0
        ).astype(BF16)
        agg[at, :] = gathered
        pre = pre_part[at, :] + dot(gathered, wi_ref[256:512, :])
        gate = sigmoid(pre)
        hid = (pre * gate).astype(BF16)
        hidden[at, :] = hid
        outer = dot(hid, wo_ref[...])
        centered = outer - row_mean(outer)
        inv_std = lax.rsqrt(row_mean(centered * centered) + norm_eps)
        normed = centered * inv_std
        gain = gain_ref[...]
        out_new[at, :] = (nf_ref[at, :].astype(F32) + normed * gain).astype(BF16)
        upstream = cot_ref[at, :].astype(F32)
        gained = upstream * gain
        back = ((gained - row_mean(gained) - normed * row_mean(gained * normed)) * inv_std).astype(BF16)
        outer_grad[at, :] = back
        back = (dot_right_t(back, wo_ref[...]) * (gate * (1.0 + pre * (1.0 - gate)))).astype(BF16)
        pre_grad[at, :] = back
        base[at, :] = upstream + dot_right_t(back, wi_ref[0:256, :])
        agg_grad[pl.ds(2 * c, 2)] = dot_right_t(back, wi_ref[256:512, :]).astype(BF16).reshape(2, 128, 256)
        return (
            sums[0] + jnp.sum(back.astype(F32), axis=0, keepdims=True),
            sums[1] + jnp.sum(upstream * normed, axis=0, keepdims=True),
        )

    zero_row = jnp.zeros((1, 256), F32)
    bias_sum, gain_sum = lax.fori_loop(0, node_rows // 256, node_update, (zero_row, zero_row))

    def deal(stage, first, tall, value):
        for rep in range(reps):
            for tile in range(8):
                start, half = (64 * rep + 16 * (tile // 2)) * tall, 128 * (tile % 2)
                slot, place = rep * plane + tile // sub, stage.shape[1] // sub * (tile % sub)
                stage[slot, place + first : place + first + 16 * tall, :] = value[
                    start : start + 16 * tall, half : half + 128
                ].astype(BF16)

    deal(stage_e, 0, 1, inner_rows(hidden[...], outer_grad[...]))
    back_all = pre_grad[...]
    deal(
        stage_e, 16, 2,
        jnp.concatenate([inner_rows(nf_ref[...], back_all), inner_rows(agg[...], back_all)], axis=0),
    )
    low_lane = lax.broadcasted_iota(jnp.int32, (1, 128), 1) < 64
    for rep in range(reps):
        at = slice(128 * (rep // 2), 128 * (rep // 2) + 128)
        left, right = bias_sum[:, at], gain_sum[:, at]
        if rep % 2:
            left = pltpu.roll(left, 64, 1)
        else:
            right = pltpu.roll(right, 64, 1)
        both = jnp.broadcast_to(jnp.where(low_lane, left, right), (16, 128)).astype(BF16)
        for g in range(plane):
            stage_e[rep * plane + g, 48:64, :] = both
    land_e[team_at] = stage_e[team_at]

    @pl.loop(1, team)
    def _(step):
        other, device = mate(step)
        send(stage_e.at[other], land_e.at[team_at], 1, device)

    def backward_slots(c, total):
        for lap in range(4):
            i = c * 4 + lap
            product = inner_rows(adj_ref[meta_s[4, i]], agg_grad[meta_s[5, i]])
            total = product + total * meta_s[6, i].astype(F32)
            run[i] = total
        return total

    carried = lax.fori_loop(0, 4, backward_slots, jnp.zeros((128, 256), F32))

    @pl.loop(0, peers)
    def _(k):
        at = pl.ds(pl.multiple_of(node_rows + k * 128, 128), 128)
        back = (run[meta_s[7, k]] * slope[at, :]).astype(BF16)
        halo_grad[pl.ds(pl.multiple_of(k * 128, 128), 128), :] = back
        rout[k] = dot_right_t(back, wm_ref[...]).astype(BF16)

    rin[2 + rep_at] = rout[2 + rep_at]
    send(rout.at[0], rin.at[0], 2, loop_down)
    send(rout.at[1], rin.at[1], 2, loop_up)

    @pl.loop(1, reps)
    def _(step):
        r_to = lax.rem(rep_at + step, reps)
        send(rout.at[2 + r_to], rin.at[2 + rep_at], 2, {"loop": loop_at, "rep": r_to})

    lax.fori_loop(4, 6, backward_slots, carried)

    @pl.loop(0, blocks)
    def _(b):
        at = pl.ds(pl.multiple_of(b * 128, 128), 128)
        own_grad[at, :] = (run[meta_s[7, peers + b]] * slope[at, :]).astype(BF16)

    message_grad = inner_rows(nf_ref[...], own_grad[...])
    for k in range(peers):
        message_grad += inner_rows(hin[k], halo_grad[128 * k : 128 * k + 128, :])
    deal(stage_l, 0, 1, message_grad)
    land_l[team_at] = stage_l[team_at]

    @pl.loop(1, team)
    def _(step):
        other, device = mate(step)
        send(stage_l.at[other], land_l.at[team_at], 3, device)

    @pl.loop(0, node_rows // 256)
    def _(c):
        at = pl.ds(pl.multiple_of(c * 256, 256), 256)
        base[at, :] += dot_right_t(own_grad[at, :], wm_ref[...])

    copy_all(rin.at[1:], recv_sem.at[2]).wait()
    copy_all(rin.at[1:], send_sem.at[2]).wait()

    @pl.loop(0, node_rows // 256)
    def _(c):
        at = pl.ds(pl.multiple_of(c * 256, 256), 256)
        total = base[at, :]
        for k in range(peers):
            total += dot(spread[at, 128 * k : 128 * k + 128], rin[k])
        out_grad[at, :] = total.astype(BF16)

    copy_all(land_e.at[1:], recv_sem.at[1]).wait()
    copy_all(land_l.at[1:], recv_sem.at[3]).wait()
    total_e = lax.fori_loop(
        1, team, lambda slot, total: total + land_e[slot].astype(F32), land_e[0].astype(F32)
    )
    total_l = lax.fori_loop(
        1, team, lambda slot, total: total + land_l[slot].astype(F32), land_l[0].astype(F32)
    )
    parts = []
    for tile in range(sub):
        parts += [total_e[64 * tile : 64 * tile + 48], total_l[16 * tile : 16 * tile + 16]]
    total = jnp.concatenate(parts, axis=0)
    vec_row = total_e[48:49]
    rows = 64 * sub // depth
    for z in range(depth):
        zsend[z, 0:rows, :] = total[z * rows : (z + 1) * rows]
        zsend[z, rows : rows + 1, :] = vec_row
        zsend[z, rows + 1 :, :] = jnp.zeros((zsend.shape[1] - rows - 1, 128), F32)
    zland[z_at] = zsend[z_at]

    @pl.loop(1, depth)
    def _(step):
        z_to, device = above(step)
        send(zsend.at[z_to], zland.at[z_at], 4, device)

    copy_all(zland.at[1:], recv_sem.at[4]).wait()
    total = zland[0]
    for z in range(1, depth):
        total = total + zland[z]
    total = total * scale
    out_vec[...] = total[rows : rows + 1]
    zpiece[...] = total[0:rows]
    zgather[z_at] = total[0:rows]

    @pl.loop(1, depth)
    def _(step):
        send(zpiece, zgather.at[z_at], 5, above(step)[1])

    copy_all(zgather.at[1:], recv_sem.at[5]).wait()
    piece = jnp.concatenate([zgather[z] for z in range(depth)], axis=0).astype(BF16)
    gpiece[...] = piece
    gather[g_at] = piece

    @pl.loop(1, plane)
    def _(step):
        g_to = lax.rem(g_at + step, plane)
        send(gpiece, gather.at[g_at], 6, {"loop": z_at * plane + g_to, "rep": rep_at})

    copy_all(gather.at[1:], recv_sem.at[6]).wait()
    for tile in range(8):
        row, half = 16 * (tile // 2), 128 * (tile % 2)
        slot, place = tile // sub, 64 * (tile % sub)
        for first, out, tall in ((0, out_ow, 1), (16, out_iw, 2), (48, out_mw, 1)):
            block = gather[slot, place + first : place + first + 16 * tall, :]
            out[row * tall : (row + 16) * tall, half : half + 128] = block.astype(F32)

    for sem, sent in ((1, land_e), (3, land_l), (4, zland), (5, zgather), (6, gather)):
        copy_all(sent.at[1:], send_sem.at[sem]).wait()


def shards(
    node_features,
    cotangent,
    adjacency,
    block_index,
    block_count,
    send_rows,
    row_counts,
    message_weight,
    input_weight,
    input_bias,
    output_weight,
    norm_gain,
):
    loop_size, reps = lax.axis_size("loop"), lax.axis_size("rep")
    plane, depth = plane_of(loop_size)
    sub = 8 // plane
    peers = 2 + reps
    node_rows, width = node_features.shape
    slots = adjacency.shape[2]
    rows = 64 * sub // depth
    zrows = -(-(rows + 1) // 8) * 8
    scale = 1.0 / math.sqrt(node_rows * loop_size * reps)
    vmem, smem = pl.BlockSpec(memory_space=pltpu.VMEM), pl.BlockSpec(memory_space=pltpu.SMEM)
    shape = jax.ShapeDtypeStruct
    table_rows = node_rows + peers * 128
    halo = pltpu.VMEM((peers, 128, width), BF16)
    wide = pltpu.VMEM((node_rows, width), BF16)
    outs = pl.pallas_call(
        functools.partial(layer_kernel, plane, depth, reps, scale),
        out_shape=(
            shape((node_rows, width), BF16),
            shape((node_rows, width), BF16),
            shape((width // reps, width), F32),
            shape((2 * width // reps, width), F32),
            shape((width // reps, width), F32),
            shape((1, 128), F32),
        ),
        in_specs=[vmem, vmem, vmem, vmem, smem, vmem, smem, vmem, vmem, vmem, vmem, vmem],
        out_specs=[vmem] * 6,
        scratch_shapes=[
            pltpu.VMEM((128, 128), jnp.int32),
            pltpu.VMEM((8, 128), jnp.int32),
            pltpu.SMEM((8, 128), jnp.int32),
            halo, halo, halo, halo,
            pltpu.VMEM((node_rows, peers * 128), BF16),
            pltpu.VMEM((table_rows // 128, 128, width), BF16),
            pltpu.VMEM((table_rows, width), F32),
            pltpu.VMEM((node_rows, width), F32),
            pltpu.VMEM((slots, 128, width), F32),
            wide, wide, wide, wide,
            pltpu.VMEM((node_rows // 128, 128, width), BF16),
            pltpu.VMEM((node_rows, width), F32),
            wide,
            pltpu.VMEM((peers * 128, width), BF16),
            pltpu.VMEM((reps * plane, 64 * sub, 128), BF16),
            pltpu.VMEM((reps * plane, 64 * sub, 128), BF16),
            pltpu.VMEM((reps * plane, 16 * sub, 128), BF16),
            pltpu.VMEM((reps * plane, 16 * sub, 128), BF16),
            pltpu.VMEM((depth, zrows, 128), F32),
            pltpu.VMEM((depth, zrows, 128), F32),
            pltpu.VMEM((rows, 128), F32),
            pltpu.VMEM((depth, rows, 128), F32),
            pltpu.VMEM((64 * sub, 128), BF16),
            pltpu.VMEM((plane, 64 * sub, 128), BF16),
            pltpu.SemaphoreType.DMA,
            pltpu.SemaphoreType.DMA((7,)),
            pltpu.SemaphoreType.DMA((7,)),
        ],
        compiler_params=pltpu.CompilerParams(
            collective_id=0, has_side_effects=True, vmem_limit_bytes=48 * 1024 * 1024
        ),
        name="message_layer",
    )(
        node_features,
        cotangent,
        adjacency[0, 0],
        block_index[0, 0],
        block_count,
        send_rows[0, 0],
        row_counts[0],
        message_weight,
        input_weight,
        input_bias[None, :],
        output_weight,
        norm_gain[None, :],
    )
    new_features, grad_features, grad_mw, grad_iw, grad_ow, vec = outs
    half = width // reps
    return new_features, grad_features, grad_mw, grad_iw, vec[0, :half], grad_ow, vec[0, half:]


def solution(mesh):
    in_specs = (
        P(("loop", "rep"), None),
        P(("loop", "rep"), None),
        P("loop", "rep", None, None, None),
        P("loop", "rep", None, None),
        P("loop", "rep"),
        P("loop", "rep", None, None),
        P("loop", "rep", None),
        P(),
        P(),
        P(),
        P(),
        P(),
    )
    out_specs = (
        P(("loop", "rep"), None),
        P(("loop", "rep"), None),
        P("rep", None),
        P("rep", None),
        P("rep"),
        P("rep", None),
        P("rep"),
    )
    return jax.shard_map(shards, mesh=mesh, in_specs=in_specs, out_specs=out_specs, check_vma=False)
```

```python
import functools
import math

import jax
import jax.numpy as jnp
from jax import lax
from jax.experimental import pallas as pl
from jax.experimental.pallas import tpu as pltpu
from jax.sharding import PartitionSpec as P

norm_eps = 1e-05
MESH = pl.DeviceIdType.MESH
BF16, F32 = jnp.bfloat16, jnp.float32


def dot(left, right):
    return jnp.dot(left, right, preferred_element_type=F32)


def dot_right_t(left, right):
    return lax.dot_general(left, right, (((1,), (1,)), ((), ())), preferred_element_type=F32)


def inner_rows(left, right):
    return lax.dot_general(left, right, (((0,), (0,)), ((), ())), preferred_element_type=F32)


def sigmoid(argument):
    return 0.5 * jnp.tanh(0.5 * argument) + 0.5


def row_mean(values):
    return jnp.sum(values, axis=-1, keepdims=True) * (1.0 / values.shape[-1])


def plane_of(loop_size):
    plane = 8 if loop_size % 8 == 0 and loop_size > 8 else 2
    return plane, loop_size // plane


def copy_all(buffer, sem):
    return pltpu.make_async_copy(buffer, buffer, sem)


def slot_order(key_col, key_row, cols):
    shape = (32, 128)
    slot = lax.broadcasted_iota(jnp.int32, shape, 0)
    lane = lax.broadcasted_iota(jnp.int32, shape, 1)
    ahead = (key_row < key_col) | ((key_row == key_col) & (lane < slot))
    rank = jnp.sum(jnp.where(ahead & (lane < 24), 1, 0), axis=1, keepdims=True)
    placed = (rank == lane) & (slot < 24)
    rows = [
        jnp.sum(jnp.where(placed, col, 0), axis=0, keepdims=True) for col in (slot, *cols, key_col)
    ]
    before = pltpu.roll(rows[-1], 1, 1)
    keep = jnp.where((rows[-1] == before) & (lane[:1] > 0), 1, 0)
    last = jnp.sum(jnp.where((key_col <= lane) & (slot < 24), 1, 0), axis=0, keepdims=True) - 1
    last = jnp.maximum(last, 0)
    return [*rows[:-1], keep, last]


def silu_and_slope(pre):
    gate = sigmoid(pre)
    return (pre * gate).astype(BF16), gate * (1.0 + pre * (1.0 - gate))


def remote(source, target, send_sem, recv_sem, device):
    pltpu.make_async_remote_copy(
        source, target, send_sem, recv_sem, device_id=device, device_id_type=MESH
    ).start()


def greet(device):
    pl.semaphore_signal(pltpu.get_barrier_semaphore(), inc=1, device_id=device, device_id_type=MESH)


def halo_kernel(
    reps, loop_size,
    nf_hbm, index_ref, count_ref, rows_ref, kept_ref,
    hin, meta,
    nf_ref, flat, hout, load_sem, send_sem, recv_sem,
):
    node_rows = nf_ref.shape[0]
    blocks = node_rows // 128
    peers = 2 + reps
    loop_at, rep_at = lax.axis_index("loop"), lax.axis_index("rep")
    loop_up = {"loop": lax.rem(loop_at + 1, loop_size), "rep": rep_at}
    loop_down = {"loop": lax.rem(loop_at + loop_size - 1, loop_size), "rep": rep_at}

    load = pltpu.make_async_copy(nf_hbm, nf_ref, load_sem)
    load.start()
    greet(loop_up)
    greet(loop_down)
    for step in range(1, reps):
        greet({"loop": loop_at, "rep": lax.rem(rep_at + step, reps)})
    flat[...] = jnp.zeros(flat.shape, jnp.int32)
    flat[0:2, 0:24] = index_ref[...]
    for k in range(peers):
        flat[8 + k : 9 + k, :] = rows_ref[k]
    turned = jnp.transpose(flat[...])
    lane_rows = lax.broadcasted_iota(jnp.int32, (128, node_rows), 1)
    sub_rows = lax.broadcasted_iota(jnp.int32, (128, node_rows), 0)
    load.wait()
    for k in range(peers):
        live = (lane_rows == turned[:, 8 + k : 9 + k]) & (sub_rows < kept_ref[0, k])
        picker = jnp.where(live, 1.0, 0.0).astype(BF16)
        hout[k] = dot(picker, nf_ref[...]).astype(BF16)

    pl.semaphore_wait(pltpu.get_barrier_semaphore(), 1 + reps)
    remote(hout.at[0], hin.at[0], send_sem, recv_sem, loop_up)
    remote(hout.at[1], hin.at[1], send_sem, recv_sem, loop_down)
    for step in range(1, reps):
        r_to = lax.rem(rep_at + step, reps)
        remote(
            hout.at[2 + r_to], hin.at[2 + rep_at], send_sem, recv_sem, {"loop": loop_at, "rep": r_to}
        )
    own = pltpu.make_async_copy(hout.at[2 + rep_at], hin.at[2 + rep_at], load_sem)
    own.start()

    live_total = count_ref[0, 0]
    slot_col = lax.broadcasted_iota(jnp.int32, (32, 1), 0)
    slot_row = lax.broadcasted_iota(jnp.int32, (1, 128), 1)
    dest_col, source_col = turned[0:32, 0:1], turned[0:32, 1:2]
    dest_row, source_row = flat[0:1, :], flat[1:2, :]

    def keyed(value, iota):
        return jnp.where(iota < live_total, value, 64)

    def halo_first(value):
        return jnp.where(value >= blocks, value - blocks, value + peers)

    forward = slot_order(keyed(dest_col, slot_col), keyed(dest_row, slot_row), (source_col,))
    backward = slot_order(
        keyed(halo_first(source_col), slot_col), keyed(halo_first(source_row), slot_row), (dest_col,)
    )
    meta[...] = jnp.concatenate(forward + backward, axis=0)

    own.wait()
    copy_all(hin.at[1:], recv_sem).wait()
    copy_all(hin.at[1:], send_sem).wait()


def layer_kernel(
    plane, depth, reps, scale,
    nf_hbm, wm_hbm, hin_hbm, wi_hbm, meta_hbm, adj_hbm, cot_hbm, wo_hbm,
    rows_ref, kept_ref, bias_ref, gain_ref,
    new_hbm, grad_hbm, mw_hbm, iw_hbm, grad_bias_hbm, ow_hbm, grad_gain_hbm,
    nf_ref, wm_ref, hin, wi_ref, meta_s, adj_ref, cot_ref, wo_ref,
    out_new, out_grad, out_mw, out_iw, out_bias, out_ow, out_gain,
    rout, rin, table, own_slope, halo_slope, pre_part, spread, run,
    agg, hidden, outer_grad, pre_grad, agg_grad, base, own_grad, halo_grad,
    stage_e, land_e, zsend, zland, zpiece, zgather, gpiece_e, gather_e,
    stage_l, land_l, lpiece, lland, gpiece_l, gather_l,
    load_sem, store_sem, send_sem, recv_sem,
):
    sub = 8 // plane
    node_rows = nf_ref.shape[0]
    blocks = node_rows // 128
    peers = 2 + reps
    loop_size = plane * depth
    loop_at, rep_at = lax.axis_index("loop"), lax.axis_index("rep")
    z_at, g_at = loop_at // plane, lax.rem(loop_at, plane)
    team = reps * plane
    team_at = rep_at * plane + g_at
    loop_up = {"loop": lax.rem(loop_at + 1, loop_size), "rep": rep_at}
    loop_down = {"loop": lax.rem(loop_at + loop_size - 1, loop_size), "rep": rep_at}

    def mate(step):
        other = lax.rem(team_at + step, team)
        r_to, g_to = other // plane, lax.rem(other, plane)
        return other, {"loop": z_at * plane + g_to, "rep": r_to}

    def above(step):
        z_to = lax.rem(z_at + step, depth)
        return z_to, {"loop": z_to * plane + g_at, "rep": rep_at}

    def send(source, target, sem, device):
        remote(source, target, send_sem.at[sem], recv_sem.at[sem], device)

    def to_team(stage, land, sem):
        land[team_at] = stage[team_at]

        @pl.loop(1, team)
        def _(step):
            other, device = mate(step)
            send(stage.at[other], land.at[team_at], sem, device)

    def to_plane(piece, gather, sem):
        gather[g_at] = piece[...]

        @pl.loop(1, plane)
        def _(step):
            g_to = lax.rem(g_at + step, plane)
            send(piece, gather.at[g_at], sem, {"loop": z_at * plane + g_to, "rep": rep_at})

    def arrived(land, sem):
        copy_all(land.at[1:], recv_sem.at[sem]).wait()

    def added(land, count):
        total = land[0].astype(F32)
        return lax.fori_loop(1, count, lambda slot, total: total + land[slot].astype(F32), total)

    loads = [
        pltpu.make_async_copy(source, target, load_sem.at[i])
        for i, (source, target) in enumerate(
            (
                (nf_hbm, nf_ref), (wm_hbm, wm_ref), (hin_hbm, hin), (wi_hbm, wi_ref),
                (meta_hbm, meta_s), (adj_hbm, adj_ref), (cot_hbm, cot_ref), (wo_hbm, wo_ref),
            )
        )
    ]
    for load in loads:
        load.start()
    stores = [
        pltpu.make_async_copy(source, target, store_sem.at[i])
        for i, (source, target) in enumerate(
            (
                (out_new, new_hbm), (out_grad, grad_hbm), (out_mw, mw_hbm), (out_iw, iw_hbm),
                (out_bias, grad_bias_hbm), (out_ow, ow_hbm), (out_gain, grad_gain_hbm),
            )
        )
    ]

    @pl.loop(1, depth)
    def _(step):
        greet(above(step)[1])

    @pl.loop(1, team)
    def _(step):
        greet(mate(step)[1])

    greet(loop_up)
    greet(loop_down)

    for load in loads[:4]:
        load.wait()

    @pl.loop(0, node_rows // 256)
    def _(c):
        at = pl.ds(pl.multiple_of(c * 256, 256), 256)
        features = nf_ref[at, :]
        message, own_slope[at, :] = silu_and_slope(dot(features, wm_ref[...]))
        table[pl.ds(2 * c, 2)] = message.reshape(2, 128, 256)
        pre_part[at, :] = dot(features, wi_ref[0:256, :]) + bias_ref[...]

    @pl.loop(0, peers)
    def _(k):
        table[blocks + k], halo_slope[k] = silu_and_slope(dot(hin[k], wm_ref[...]))

    for load in loads[4:]:
        load.wait()

    def forward_slots(c, total):
        for lap in range(4):
            i = c * 4 + lap
            product = dot(adj_ref[meta_s[0, i]], table[meta_s[1, i]])
            total = product + total * meta_s[2, i].astype(F32)
            run[i] = total
        return total

    lax.fori_loop(0, 6, forward_slots, jnp.zeros((128, 256), F32))

    def node_update(c, sums):
        at = pl.ds(pl.multiple_of(c * 256, 256), 256)
        gathered = jnp.concatenate(
            [run[meta_s[3, 2 * c]], run[meta_s[3, 2 * c + 1]]], axis=0
        ).astype(BF16)
        agg[at, :] = gathered
        hid, hid_slope = silu_and_slope(pre_part[at, :] + dot(gathered, wi_ref[256:512, :]))
        hidden[at, :] = hid
        outer = dot(hid, wo_ref[...])
        centered = outer - row_mean(outer)
        inv_std = lax.rsqrt(row_mean(centered * centered) + norm_eps)
        normed = centered * inv_std
        gain = gain_ref[...]
        out_new[at, :] = (nf_ref[at, :].astype(F32) + normed * gain).astype(BF16)
        upstream = cot_ref[at, :].astype(F32)
        gained = upstream * gain
        back = ((gained - row_mean(gained) - normed * row_mean(gained * normed)) * inv_std).astype(BF16)
        outer_grad[at, :] = back
        back = (dot_right_t(back, wo_ref[...]) * hid_slope).astype(BF16)
        pre_grad[at, :] = back
        base[at, :] = upstream + dot_right_t(back, wi_ref[0:256, :])
        agg_grad[pl.ds(2 * c, 2)] = dot_right_t(back, wi_ref[256:512, :]).astype(BF16).reshape(2, 128, 256)
        return (
            sums[0] + jnp.sum(back.astype(F32), axis=0, keepdims=True),
            sums[1] + jnp.sum(upstream * normed, axis=0, keepdims=True),
        )

    zero_row = jnp.zeros((1, 256), F32)
    bias_sum, gain_sum = lax.fori_loop(0, node_rows // 256, node_update, (zero_row, zero_row))

    stores[0].start()

    def deal(stage, first, tall, value):
        for rep in range(reps):
            for tile in range(8):
                start, half = (64 * rep + 16 * (tile // 2)) * tall, 128 * (tile % 2)
                slot, place = rep * plane + tile // sub, stage.shape[1] // sub * (tile % sub)
                stage[slot, place + first : place + first + 16 * tall, :] = value[
                    start : start + 16 * tall, half : half + 128
                ].astype(BF16)

    deal(stage_e, 0, 1, inner_rows(hidden[...], outer_grad[...]))
    back_all = pre_grad[...]
    deal(
        stage_e, 16, 2,
        jnp.concatenate([inner_rows(nf_ref[...], back_all), inner_rows(agg[...], back_all)], axis=0),
    )
    low_lane = lax.broadcasted_iota(jnp.int32, (1, 128), 1) < 64
    for rep in range(reps):
        at = slice(128 * (rep // 2), 128 * (rep // 2) + 128)
        left, right = bias_sum[:, at], gain_sum[:, at]
        if rep % 2:
            left = pltpu.roll(left, 64, 1)
        else:
            right = pltpu.roll(right, 64, 1)
        both = jnp.broadcast_to(jnp.where(low_lane, left, right), (16, 128)).astype(BF16)
        for g in range(plane):
            stage_e[rep * plane + g, 48:64, :] = both

    pl.semaphore_wait(pltpu.get_barrier_semaphore(), team + depth)
    to_team(stage_e, land_e, 0)

    def backward_slots(c, total):
        for lap in range(4):
            i = c * 4 + lap
            product = inner_rows(adj_ref[meta_s[4, i]], agg_grad[meta_s[5, i]])
            total = product + total * meta_s[6, i].astype(F32)
            run[i] = total
        return total

    carried = lax.fori_loop(0, 4, backward_slots, jnp.zeros((128, 256), F32))

    @pl.loop(0, peers)
    def _(k):
        back = (run[meta_s[7, k]] * halo_slope[k]).astype(BF16)
        halo_grad[k] = back
        rout[k] = dot_right_t(back, wm_ref[...]).astype(BF16)

    rin[2 + rep_at] = rout[2 + rep_at]
    send(rout.at[0], rin.at[0], 1, loop_down)
    send(rout.at[1], rin.at[1], 1, loop_up)
    for step in range(1, reps):
        r_to = lax.rem(rep_at + step, reps)
        send(rout.at[2 + r_to], rin.at[2 + rep_at], 1, {"loop": loop_at, "rep": r_to})

    lax.fori_loop(4, 6, backward_slots, carried)

    @pl.loop(0, blocks)
    def _(b):
        at = pl.ds(pl.multiple_of(b * 128, 128), 128)
        own_grad[at, :] = (run[meta_s[7, peers + b]] * own_slope[at, :]).astype(BF16)

    message_grad = inner_rows(nf_ref[...], own_grad[...])
    for k in range(peers):
        message_grad += inner_rows(hin[k], halo_grad[k])
    deal(stage_l, 0, 1, message_grad)
    to_team(stage_l, land_l, 2)

    @pl.loop(0, node_rows // 256)
    def _(c):
        at = pl.ds(pl.multiple_of(c * 256, 256), 256)
        base[at, :] += dot_right_t(own_grad[at, :], wm_ref[...])

    row_at = lax.broadcasted_iota(jnp.int32, (node_rows, 128), 0)
    lane_at = lax.broadcasted_iota(jnp.int32, (node_rows, 128), 1)
    for k in range(peers):
        live = (row_at == rows_ref[k]) & (lane_at < kept_ref[0, k])
        spread[:, 128 * k : 128 * k + 128] = jnp.where(live, 1.0, 0.0).astype(BF16)

    arrived(land_e, 0)
    total = added(land_e, team)
    vec_row = total[48:49]
    total = jnp.concatenate([total[64 * tile : 64 * tile + 48] for tile in range(sub)], axis=0)
    rows = 48 * sub // depth
    for z in range(depth):
        zsend[z, 0:rows, :] = total[z * rows : (z + 1) * rows]
        zsend[z, rows : rows + 1, :] = vec_row
    zland[z_at] = zsend[z_at]

    @pl.loop(1, depth)
    def _(step):
        z_to, device = above(step)
        send(zsend.at[z_to], zland.at[z_at], 3, device)

    arrived(land_l, 2)
    lpiece[...] = added(land_l, team).astype(BF16)
    lland[z_at] = lpiece[...]

    @pl.loop(1, depth)
    def _(step):
        send(lpiece, lland.at[z_at], 4, above(step)[1])

    arrived(rin, 1)

    @pl.loop(0, node_rows // 256)
    def _(c):
        at = pl.ds(pl.multiple_of(c * 256, 256), 256)
        total = base[at, :]
        for k in range(peers):
            total += dot(spread[at, 128 * k : 128 * k + 128], rin[k])
        out_grad[at, :] = total.astype(BF16)

    stores[1].start()
    arrived(zland, 3)
    total = added(zland, depth) * scale
    vec_row = total[rows : rows + 1]
    half = out_bias.shape[1]
    out_bias[...] = vec_row[:, 0:half]
    out_gain[...] = pltpu.roll(vec_row, half, 1)[:, 0:half]
    stores[4].start()
    stores[6].start()
    zpiece[...] = total
    zgather[z_at] = total

    @pl.loop(1, depth)
    def _(step):
        send(zpiece, zgather.at[z_at], 5, above(step)[1])

    arrived(lland, 4)
    gpiece_l[...] = (added(lland, depth) * scale).astype(BF16)
    to_plane(gpiece_l, gather_l, 6)

    arrived(zgather, 5)
    gpiece_e[...] = jnp.concatenate([zgather[z, 0:rows, :] for z in range(depth)], axis=0).astype(BF16)
    to_plane(gpiece_e, gather_e, 7)

    def collect(out, gather, first, tall):
        for tile in range(8):
            row, half = 16 * tall * (tile // 2), 128 * (tile % 2)
            slot, place = tile // sub, gather.shape[1] // sub * (tile % sub)
            block = gather[slot, place + first : place + first + 16 * tall, :]
            out[row : row + 16 * tall, half : half + 128] = block.astype(F32)

    arrived(gather_l, 6)
    collect(out_mw, gather_l, 0, 1)
    stores[2].start()
    arrived(gather_e, 7)
    collect(out_ow, gather_e, 0, 1)
    stores[5].start()
    collect(out_iw, gather_e, 16, 2)
    stores[3].start()

    sent = (land_e, rin, land_l, zland, lland, zgather, gather_l, gather_e)
    for sem, land in enumerate(sent):
        copy_all(land.at[1:], send_sem.at[sem]).wait()
    for store in stores:
        store.wait()


def finish_kernel(*refs):
    sem = refs[-1]
    copies = [
        pltpu.make_async_copy(source, target, sem.at[i])
        for i, (source, target) in enumerate(zip(refs[:7], refs[7:14]))
    ]
    for copy in copies:
        copy.start()
    for copy in copies:
        copy.wait()


def shards(
    node_features,
    cotangent,
    adjacency,
    block_index,
    block_count,
    send_rows,
    row_counts,
    message_weight,
    input_weight,
    input_bias,
    output_weight,
    norm_gain,
):
    loop_size, reps = lax.axis_size("loop"), lax.axis_size("rep")
    plane, depth = plane_of(loop_size)
    sub = 8 // plane
    peers = 2 + reps
    node_rows, width = node_features.shape
    blocks = node_rows // 128
    slots = adjacency.shape[2]
    rows = 48 * sub // depth + 1
    zrows = rows if rows <= 4 else -(-rows // 8) * 8
    scale = 1.0 / math.sqrt(node_rows * loop_size * reps)
    vmem, smem = pl.BlockSpec(memory_space=pltpu.VMEM), pl.BlockSpec(memory_space=pltpu.SMEM)
    hbm = pl.BlockSpec(memory_space=pltpu.HBM)
    shape = jax.ShapeDtypeStruct
    wide = (node_rows, width)
    mega = 1024 * 1024
    rows_in = send_rows.reshape(peers, 1, 128)
    hin, meta = pl.pallas_call(
        functools.partial(halo_kernel, reps, loop_size),
        out_shape=(shape((peers, 128, width), BF16), shape((8, 128), jnp.int32)),
        in_specs=[hbm, vmem, smem, vmem, smem],
        out_specs=[hbm, vmem],
        scratch_shapes=[
            pltpu.VMEM(wide, BF16),
            pltpu.VMEM((128, 128), jnp.int32),
            pltpu.VMEM((peers, 128, width), BF16),
            pltpu.SemaphoreType.DMA,
            pltpu.SemaphoreType.DMA,
            pltpu.SemaphoreType.DMA,
        ],
        compiler_params=pltpu.CompilerParams(
            collective_id=0, has_side_effects=True, vmem_limit_bytes=56 * mega
        ),
        name="halo_rows",
    )(node_features, block_index[0, 0], block_count, rows_in, row_counts[0])
    small = pltpu.VMEM(wide, BF16)
    half = width // reps
    results = (
        shape(wide, BF16),
        shape(wide, BF16),
        shape((half, width), F32),
        shape((2 * half, width), F32),
        shape((1, half), F32),
        shape((half, width), F32),
        shape((1, half), F32),
    )
    outs = pl.pallas_call(
        functools.partial(layer_kernel, plane, depth, reps, scale),
        out_shape=results,
        in_specs=[hbm] * 8 + [vmem, smem, vmem, vmem],
        out_specs=[hbm] * 7,
        scratch_shapes=[
            small,
            pltpu.VMEM((width, width), BF16),
            pltpu.VMEM((peers, 128, width), BF16),
            pltpu.VMEM((2 * width, width), BF16),
            pltpu.SMEM((8, 128), jnp.int32),
            pltpu.VMEM((slots, 128, 128), BF16),
            small,
            pltpu.VMEM((width, width), BF16),
            *(pltpu.VMEM(result.shape, result.dtype) for result in results),
            pltpu.VMEM((peers, 128, width), BF16),
            pltpu.VMEM((peers, 128, width), BF16),
            pltpu.VMEM((blocks + peers, 128, width), BF16),
            pltpu.VMEM(wide, F32),
            pltpu.VMEM((peers, 128, width), F32),
            pltpu.VMEM(wide, F32),
            pltpu.VMEM((node_rows, peers * 128), BF16),
            pltpu.VMEM((slots, 128, width), F32),
            small, small, small, small,
            pltpu.VMEM((blocks, 128, width), BF16),
            pltpu.VMEM(wide, F32),
            small,
            pltpu.VMEM((peers, 128, width), BF16),
            pltpu.VMEM((reps * plane, 64 * sub, 128), BF16),
            pltpu.VMEM((reps * plane, 64 * sub, 128), BF16),
            pltpu.VMEM((depth, zrows, 128), F32),
            pltpu.VMEM((depth, zrows, 128), F32),
            pltpu.VMEM((zrows, 128), F32),
            pltpu.VMEM((depth, zrows, 128), F32),
            pltpu.VMEM((48 * sub, 128), BF16),
            pltpu.VMEM((plane, 48 * sub, 128), BF16),
            pltpu.VMEM((reps * plane, 16 * sub, 128), BF16),
            pltpu.VMEM((reps * plane, 16 * sub, 128), BF16),
            pltpu.VMEM((16 * sub, 128), BF16),
            pltpu.VMEM((depth, 16 * sub, 128), BF16),
            pltpu.VMEM((16 * sub, 128), BF16),
            pltpu.VMEM((plane, 16 * sub, 128), BF16),
            pltpu.SemaphoreType.DMA((8,)),
            pltpu.SemaphoreType.DMA((7,)),
            pltpu.SemaphoreType.DMA((8,)),
            pltpu.SemaphoreType.DMA((8,)),
        ],
        compiler_params=pltpu.CompilerParams(
            collective_id=1, has_side_effects=True, vmem_limit_bytes=56 * mega
        ),
        name="message_layer",
    )(
        node_features,
        message_weight,
        hin,
        input_weight,
        meta,
        adjacency[0, 0],
        cotangent,
        output_weight,
        rows_in,
        row_counts[0],
        input_bias[None, :],
        norm_gain[None, :],
    )
    new_features, grad_features, grad_mw, grad_iw, grad_bias, grad_ow, grad_gain = pl.pallas_call(
        finish_kernel,
        out_shape=results,
        in_specs=[hbm] * 7,
        out_specs=[hbm] * 7,
        scratch_shapes=[pltpu.SemaphoreType.DMA((7,))],
        compiler_params=pltpu.CompilerParams(has_side_effects=True, vmem_limit_bytes=56 * mega),
        name="write_results",
    )(*outs)
    return (
        new_features, grad_features, grad_mw, grad_iw,
        grad_bias.reshape(half), grad_ow, grad_gain.reshape(half),
    )


def solution(mesh):
    in_specs = (
        P(("loop", "rep"), None),
        P(("loop", "rep"), None),
        P("loop", "rep", None, None, None),
        P("loop", "rep", None, None),
        P("loop", "rep"),
        P("loop", "rep", None, None),
        P("loop", "rep", None),
        P(),
        P(),
        P(),
        P(),
        P(),
    )
    out_specs = (
        P(("loop", "rep"), None),
        P(("loop", "rep"), None),
        P("rep", None),
        P("rep", None),
        P("rep"),
        P("rep", None),
        P("rep"),
    )
    return jax.shard_map(shards, mesh=mesh, in_specs=in_specs, out_specs=out_specs, check_vma=False)
```

```python
import functools
import math

import jax
import jax.numpy as jnp
from jax import lax
from jax.experimental import pallas as pl
from jax.experimental.pallas import tpu as pltpu
from jax.sharding import PartitionSpec as P

norm_eps = 1e-05
MESH = pl.DeviceIdType.MESH
BF16, F32 = jnp.bfloat16, jnp.float32


def dot(left, right):
    return jnp.dot(left, right, preferred_element_type=F32)


def dot_right_t(left, right):
    return lax.dot_general(left, right, (((1,), (1,)), ((), ())), preferred_element_type=F32)


def inner_rows(left, right):
    return lax.dot_general(left, right, (((0,), (0,)), ((), ())), preferred_element_type=F32)


def sigmoid(argument):
    return 0.5 * jnp.tanh(0.5 * argument) + 0.5


def row_mean(values):
    return jnp.sum(values, axis=-1, keepdims=True) * (1.0 / values.shape[-1])


def plane_of(loop_size):
    plane = 8 if loop_size % 8 == 0 and loop_size > 8 else 2
    return plane, loop_size // plane


def copy_all(buffer, sem):
    return pltpu.make_async_copy(buffer, buffer, sem)


def slot_order(key_col, key_row, cols):
    shape = (32, 128)
    slot = lax.broadcasted_iota(jnp.int32, shape, 0)
    lane = lax.broadcasted_iota(jnp.int32, shape, 1)
    ahead = (key_row < key_col) | ((key_row == key_col) & (lane < slot))
    rank = jnp.sum(jnp.where(ahead & (lane < 24), 1, 0), axis=1, keepdims=True)
    placed = (rank == lane) & (slot < 24)
    rows = [
        jnp.sum(jnp.where(placed, col, 0), axis=0, keepdims=True) for col in (slot, *cols, key_col)
    ]
    before = pltpu.roll(rows[-1], 1, 1)
    keep = jnp.where((rows[-1] == before) & (lane[:1] > 0), 1, 0)
    last = jnp.sum(jnp.where((key_col <= lane) & (slot < 24), 1, 0), axis=0, keepdims=True) - 1
    last = jnp.maximum(last, 0)
    return [*rows[:-1], keep, last]


def silu_and_slope(pre):
    gate = sigmoid(pre)
    return (pre * gate).astype(BF16), gate * (1.0 + pre * (1.0 - gate))


def remote(source, target, send_sem, recv_sem, device):
    pltpu.make_async_remote_copy(
        source, target, send_sem, recv_sem, device_id=device, device_id_type=MESH
    ).start()


def greet(device):
    pl.semaphore_signal(pltpu.get_barrier_semaphore(), inc=1, device_id=device, device_id_type=MESH)


def halo_kernel(
    reps, loop_size,
    nf_hbm, index_ref, count_ref, rows_ref, kept_ref,
    hin, meta,
    nf_ref, flat, hout, load_sem, send_sem, recv_sem,
):
    node_rows = nf_ref.shape[0]
    blocks = node_rows // 128
    peers = 2 + reps
    loop_at, rep_at = lax.axis_index("loop"), lax.axis_index("rep")
    loop_up = {"loop": lax.rem(loop_at + 1, loop_size), "rep": rep_at}
    loop_down = {"loop": lax.rem(loop_at + loop_size - 1, loop_size), "rep": rep_at}

    load = pltpu.make_async_copy(nf_hbm, nf_ref, load_sem)
    load.start()
    greet(loop_up)
    greet(loop_down)
    for step in range(1, reps):
        greet({"loop": loop_at, "rep": lax.rem(rep_at + step, reps)})
    flat[...] = jnp.zeros(flat.shape, jnp.int32)
    flat[0:2, 0:24] = index_ref[...]
    for k in range(peers):
        flat[8 + k : 9 + k, :] = rows_ref[k]
    turned = jnp.transpose(flat[...])
    lane_rows = lax.broadcasted_iota(jnp.int32, (128, node_rows), 1)
    sub_rows = lax.broadcasted_iota(jnp.int32, (128, node_rows), 0)
    load.wait()

    def pick(k):
        live = (lane_rows == turned[:, 8 + k : 9 + k]) & (sub_rows < kept_ref[0, k])
        picker = jnp.where(live, 1.0, 0.0).astype(BF16)
        hout[k] = dot(picker, nf_ref[...]).astype(BF16)

    pick(0)
    pick(1)
    pl.semaphore_wait(pltpu.get_barrier_semaphore(), 1 + reps)
    remote(hout.at[0], hin.at[0], send_sem, recv_sem, loop_up)
    remote(hout.at[1], hin.at[1], send_sem, recv_sem, loop_down)
    for k in range(2, peers):
        pick(k)
    for step in range(1, reps):
        r_to = lax.rem(rep_at + step, reps)
        remote(
            hout.at[2 + r_to], hin.at[2 + rep_at], send_sem, recv_sem, {"loop": loop_at, "rep": r_to}
        )
    own = pltpu.make_async_copy(hout.at[2 + rep_at], hin.at[2 + rep_at], load_sem)
    own.start()

    live_total = count_ref[0, 0]
    slot_col = lax.broadcasted_iota(jnp.int32, (32, 1), 0)
    slot_row = lax.broadcasted_iota(jnp.int32, (1, 128), 1)
    dest_col, source_col = turned[0:32, 0:1], turned[0:32, 1:2]
    dest_row, source_row = flat[0:1, :], flat[1:2, :]

    def keyed(value, iota):
        return jnp.where(iota < live_total, value, 64)

    def halo_first(value):
        return jnp.where(value >= blocks, value - blocks, value + peers)

    forward = slot_order(keyed(dest_col, slot_col), keyed(dest_row, slot_row), (source_col,))
    backward = slot_order(
        keyed(halo_first(source_col), slot_col), keyed(halo_first(source_row), slot_row), (dest_col,)
    )
    meta[...] = jnp.concatenate(forward + backward, axis=0)

    own.wait()
    copy_all(hin.at[1:], recv_sem).wait()
    copy_all(hin.at[1:], send_sem).wait()


def layer_kernel(
    plane, depth, reps, scale,
    nf_hbm, wm_hbm, wi_hbm, hin_hbm, meta_hbm, adj_hbm, cot_hbm, wo_hbm,
    rows_ref, kept_ref, bias_ref, gain_ref,
    new_hbm, grad_hbm, mw_hbm, iw_hbm, grad_bias_hbm, ow_hbm, grad_gain_hbm,
    nf_ref, wm_ref, wi_ref, hin, meta_s, adj_ref, cot_ref, wo_ref,
    out_new, out_grad, out_mw, out_iw, out_bias, out_ow, out_gain,
    rout, rin, table, own_slope, halo_slope, pre_part, spread, run,
    agg, hidden, outer_grad, pre_grad, agg_grad, base, own_grad, halo_grad,
    stage_e, land_e, psend, pland, epiece, eland, gpiece_e, gather_e,
    stage_l, land_l, lpiece, lland, gpiece_l, gather_l,
    load_sem, store_sem, send_sem, recv_sem,
):
    sub = 8 // plane
    node_rows = nf_ref.shape[0]
    blocks = node_rows // 128
    peers = 2 + reps
    loop_size = plane * depth
    loop_at, rep_at = lax.axis_index("loop"), lax.axis_index("rep")
    z_at, g_at = loop_at // plane, lax.rem(loop_at, plane)
    team = reps * plane
    team_at = rep_at * plane + g_at
    loop_up = {"loop": lax.rem(loop_at + 1, loop_size), "rep": rep_at}
    loop_down = {"loop": lax.rem(loop_at + loop_size - 1, loop_size), "rep": rep_at}

    def mate(step):
        other = lax.rem(team_at + step, team)
        r_to, g_to = other // plane, lax.rem(other, plane)
        return other, {"loop": z_at * plane + g_to, "rep": r_to}

    def above(step):
        z_to = lax.rem(z_at + step, depth)
        return z_to, {"loop": z_to * plane + g_at, "rep": rep_at}

    parity = lax.rem(z_at, 2)
    z_pair = z_at + 1 - 2 * parity

    def twin(step):
        other = lax.rem(parity * plane + g_at + step, 2 * plane)
        z_to, g_to = z_at - parity + other // plane, lax.rem(other, plane)
        return {"loop": z_to * plane + g_to, "rep": rep_at}

    def send(source, target, sem, device):
        remote(source, target, send_sem.at[sem], recv_sem.at[sem], device)

    def to_team(stage, land, sem):
        land[team_at] = stage[team_at]

        @pl.loop(1, team)
        def _(step):
            other, device = mate(step)
            send(stage.at[other], land.at[team_at], sem, device)

    def to_plane(piece, gather, sem):
        gather[g_at] = piece[...]

        @pl.loop(1, plane)
        def _(step):
            g_to = lax.rem(g_at + step, plane)
            send(piece, gather.at[g_at], sem, {"loop": z_at * plane + g_to, "rep": rep_at})

    def arrived(land, sem):
        if land.shape[0] > 1:
            copy_all(land.at[1:], recv_sem.at[sem]).wait()

    def added(land, count):
        total = land[0].astype(F32)
        return lax.fori_loop(1, count, lambda slot, total: total + land[slot].astype(F32), total)

    loads = [
        pltpu.make_async_copy(source, target, load_sem.at[i])
        for i, (source, target) in enumerate(
            (
                (nf_hbm, nf_ref), (wm_hbm, wm_ref), (wi_hbm, wi_ref), (hin_hbm, hin),
                (meta_hbm, meta_s), (adj_hbm, adj_ref), (cot_hbm, cot_ref), (wo_hbm, wo_ref),
            )
        )
    ]
    for load in loads:
        load.start()
    stores = [
        pltpu.make_async_copy(source, target, store_sem.at[i])
        for i, (source, target) in enumerate(
            (
                (out_new, new_hbm), (out_grad, grad_hbm), (out_mw, mw_hbm), (out_iw, iw_hbm),
                (out_bias, grad_bias_hbm), (out_ow, ow_hbm), (out_gain, grad_gain_hbm),
            )
        )
    ]

    @pl.loop(1, depth)
    def _(step):
        greet(above(step)[1])

    @pl.loop(1, team)
    def _(step):
        greet(mate(step)[1])

    @pl.loop(1, plane)
    def _(step):
        greet({"loop": z_pair * plane + lax.rem(g_at + step, plane), "rep": rep_at})

    greet(loop_up)
    greet(loop_down)

    for load in loads[:3]:
        load.wait()

    @pl.loop(0, node_rows // 256)
    def _(c):
        at = pl.ds(pl.multiple_of(c * 256, 256), 256)
        features = nf_ref[at, :]
        message, own_slope[at, :] = silu_and_slope(dot(features, wm_ref[...]))
        table[pl.ds(2 * c, 2)] = message.reshape(2, 128, 256)
        pre_part[at, :] = dot(features, wi_ref[0:256, :]) + bias_ref[...]

    loads[3].wait()
    half_peers = peers // 2
    for first in range(0, peers, half_peers):
        some = slice(first, first + half_peers)
        message, gate = silu_and_slope(dot(hin[some].reshape(half_peers * 128, 256), wm_ref[...]))
        table[blocks + first : blocks + first + half_peers] = message.reshape(half_peers, 128, 256)
        halo_slope[some] = gate.reshape(half_peers, 128, 256)

    loads[4].wait()
    loads[5].wait()

    def forward_slots(c, total):
        for lap in range(4):
            i = c * 4 + lap
            product = dot(adj_ref[meta_s[0, i]], table[meta_s[1, i]])
            total = product + total * meta_s[2, i].astype(F32)
            run[i] = total
        return total

    lax.fori_loop(0, 6, forward_slots, jnp.zeros((128, 256), F32))

    loads[6].wait()
    loads[7].wait()

    def node_update(c, sums):
        at = pl.ds(pl.multiple_of(c * 256, 256), 256)
        gathered = jnp.concatenate(
            [run[meta_s[3, 2 * c]], run[meta_s[3, 2 * c + 1]]], axis=0
        ).astype(BF16)
        agg[at, :] = gathered
        hid, hid_slope = silu_and_slope(pre_part[at, :] + dot(gathered, wi_ref[256:512, :]))
        hidden[at, :] = hid
        outer = dot(hid, wo_ref[...])
        centered = outer - row_mean(outer)
        inv_std = lax.rsqrt(row_mean(centered * centered) + norm_eps)
        normed = centered * inv_std
        gain = gain_ref[...]
        out_new[at, :] = (nf_ref[at, :].astype(F32) + normed * gain).astype(BF16)
        upstream = cot_ref[at, :].astype(F32)
        gained = upstream * gain
        back = ((gained - row_mean(gained) - normed * row_mean(gained * normed)) * inv_std).astype(BF16)
        outer_grad[at, :] = back
        back = (dot_right_t(back, wo_ref[...]) * hid_slope).astype(BF16)
        pre_grad[at, :] = back
        base[at, :] = upstream + dot_right_t(back, wi_ref[0:256, :])
        agg_grad[pl.ds(2 * c, 2)] = dot_right_t(back, wi_ref[256:512, :]).astype(BF16).reshape(2, 128, 256)
        return (
            sums[0] + jnp.sum(back.astype(F32), axis=0, keepdims=True),
            sums[1] + jnp.sum(upstream * normed, axis=0, keepdims=True),
        )

    zero_row = jnp.zeros((1, 256), F32)
    bias_sum, gain_sum = lax.fori_loop(
        0, node_rows // 256, node_update, (zero_row, zero_row), unroll=2
    )

    stores[0].start()

    def deal(stage, first, tall, value):
        for rep in range(reps):
            for tile in range(8):
                start, half = (64 * rep + 16 * (tile // 2)) * tall, 128 * (tile % 2)
                slot, place = rep * plane + tile // sub, stage.shape[1] // sub * (tile % sub)
                stage[slot, place + first : place + first + 16 * tall, :] = value[
                    start : start + 16 * tall, half : half + 128
                ].astype(BF16)

    deal(stage_e, 0, 1, inner_rows(hidden[...], outer_grad[...]))
    back_all = pre_grad[...]
    deal(
        stage_e, 16, 2,
        jnp.concatenate([inner_rows(nf_ref[...], back_all), inner_rows(agg[...], back_all)], axis=0),
    )
    low_lane = lax.broadcasted_iota(jnp.int32, (1, 128), 1) < 64
    for rep in range(reps):
        at = slice(128 * (rep // 2), 128 * (rep // 2) + 128)
        left, right = bias_sum[:, at], gain_sum[:, at]
        if rep % 2:
            left = pltpu.roll(left, 64, 1)
        else:
            right = pltpu.roll(right, 64, 1)
        both = jnp.broadcast_to(jnp.where(low_lane, left, right), (16, 128)).astype(BF16)
        for g in range(plane):
            stage_e[rep * plane + g, 48:64, :] = both

    pl.semaphore_wait(pltpu.get_barrier_semaphore(), team + depth + plane - 1)
    to_team(stage_e, land_e, 0)

    def backward_slots(c, total):
        for lap in range(4):
            i = c * 4 + lap
            product = inner_rows(adj_ref[meta_s[4, i]], agg_grad[meta_s[5, i]])
            total = product + total * meta_s[6, i].astype(F32)
            run[i] = total
        return total

    carried = lax.fori_loop(0, 4, backward_slots, jnp.zeros((128, 256), F32))

    for k in range(peers):
        halo_grad[k] = (run[meta_s[7, k]] * halo_slope[k]).astype(BF16)
    halo_back = halo_grad[...].reshape(peers * 128, 256)
    rout[...] = dot_right_t(halo_back, wm_ref[...]).astype(BF16).reshape(peers, 128, 256)

    rin[2 + rep_at] = rout[2 + rep_at]
    send(rout.at[0], rin.at[0], 1, loop_down)
    send(rout.at[1], rin.at[1], 1, loop_up)
    for step in range(1, reps):
        r_to = lax.rem(rep_at + step, reps)
        send(rout.at[2 + r_to], rin.at[2 + rep_at], 1, {"loop": loop_at, "rep": r_to})

    lax.fori_loop(4, 6, backward_slots, carried)

    @pl.loop(0, blocks)
    def _(b):
        at = pl.ds(pl.multiple_of(b * 128, 128), 128)
        own_grad[at, :] = (run[meta_s[7, peers + b]] * own_slope[at, :]).astype(BF16)

    message_grad = inner_rows(nf_ref[...], own_grad[...])
    message_grad += inner_rows(hin[...].reshape(peers * 128, 256), halo_grad[...].reshape(peers * 128, 256))
    deal(stage_l, 0, 1, message_grad)
    to_team(stage_l, land_l, 2)

    @pl.loop(0, node_rows // 256)
    def _(c):
        at = pl.ds(pl.multiple_of(c * 256, 256), 256)
        base[at, :] += dot_right_t(own_grad[at, :], wm_ref[...])

    row_at = lax.broadcasted_iota(jnp.int32, (node_rows, 128), 0)
    lane_at = lax.broadcasted_iota(jnp.int32, (node_rows, 128), 1)
    for k in range(peers):
        live = (row_at == rows_ref[k]) & (lane_at < kept_ref[0, k])
        spread[:, 128 * k : 128 * k + 128] = jnp.where(live, 1.0, 0.0).astype(BF16)

    arrived(land_e, 0)
    total = added(land_e, team)
    vec_rows = jnp.broadcast_to(total[48:49], (8, 128))
    total = jnp.concatenate([total[64 * tile : 64 * tile + 48] for tile in range(sub)], axis=0)
    rows = 24 * sub
    for part in range(2):
        psend[part, 0:rows, :] = total[part * rows : (part + 1) * rows]
        psend[part, rows:, :] = vec_rows
    send(psend.at[1 - parity], pland, 3, {"loop": z_pair * plane + g_at, "rep": rep_at})

    arrived(land_l, 2)
    lpiece[...] = added(land_l, team).astype(BF16)
    lland[z_at] = lpiece[...]

    @pl.loop(1, depth)
    def _(step):
        send(lpiece, lland.at[z_at], 5, above(step)[1])

    copy_all(pland, recv_sem.at[3]).wait()
    total = psend[parity] + pland[...]
    filler = jnp.zeros((epiece.shape[0] - total.shape[0], 128), F32)
    epiece[...] = (jnp.concatenate([total, filler], axis=0) if filler.shape[0] else total).astype(BF16)
    eland[z_at // 2] = epiece[...]

    @pl.loop(1, depth // 2)
    def _(step):
        send(epiece, eland.at[z_at // 2], 4, above(2 * step)[1])

    arrived(rin, 1)
    returned = rin[...].reshape(peers * 128, 256)

    @pl.loop(0, node_rows // 256)
    def _(c):
        at = pl.ds(pl.multiple_of(c * 256, 256), 256)
        out_grad[at, :] = (base[at, :] + dot(spread[at, :], returned)).astype(BF16)

    stores[1].start()

    arrived(lland, 5)
    gpiece_l[...] = (added(lland, depth) * scale).astype(BF16)
    to_plane(gpiece_l, gather_l, 6)

    arrived(eland, 4)
    total = added(eland, depth // 2) * scale
    vec_row = total[rows : rows + 1]
    half = out_bias.shape[1]
    out_bias[...] = vec_row[:, 0:half]
    out_gain[...] = pltpu.roll(vec_row, half, 1)[:, 0:half]
    stores[4].start()
    stores[6].start()
    gpiece_e[...] = total.astype(BF16)
    gather_e[parity * plane + g_at] = gpiece_e[...]

    @pl.loop(1, 2 * plane)
    def _(step):
        send(gpiece_e, gather_e.at[parity * plane + g_at], 7, twin(step))

    def collect(out, owned, first, tall):
        for tile in range(8):
            row, half = 16 * tall * (tile // 2), 128 * (tile % 2)
            block = owned[tile // sub]
            place = block.shape[0] // sub * (tile % sub) + first
            out[row : row + 16 * tall, half : half + 128] = block[place : place + 16 * tall]

    arrived(gather_l, 6)
    collect(out_mw, [gather_l[g].astype(F32) for g in range(plane)], 0, 1)
    stores[2].start()
    arrived(gather_e, 7)
    owned = [
        jnp.concatenate([gather_e[part * plane + g].astype(F32)[0:rows] for part in range(2)], axis=0)
        for g in range(plane)
    ]
    collect(out_ow, owned, 0, 1)
    stores[5].start()
    collect(out_iw, owned, 16, 2)
    stores[3].start()

    for sem, land in ((0, land_e), (1, rin), (2, land_l), (4, eland), (5, lland), (6, gather_l), (7, gather_e)):
        if land.shape[0] > 1:
            copy_all(land.at[1:], send_sem.at[sem]).wait()
    copy_all(pland, send_sem.at[3]).wait()
    for store in stores:
        store.wait()


def finish_kernel(*refs):
    sources, targets, held, (load_sem, store_sem) = refs[:7], refs[7:14], refs[14:21], refs[21:]
    pieces = []
    for source, target, buffer in zip(sources, targets, held):
        step = min(256, source.shape[0])
        for first in range(0, source.shape[0], step):
            at = pl.ds(first, step)
            i = len(pieces)
            pieces.append(
                (
                    pltpu.make_async_copy(source.at[at], buffer.at[at], load_sem.at[i]),
                    pltpu.make_async_copy(buffer.at[at], target.at[at], store_sem.at[i]),
                )
            )
    for load, _ in pieces:
        load.start()
    for load, store in pieces:
        load.wait()
        store.start()
    for _, store in pieces:
        store.wait()


def shards(
    node_features,
    cotangent,
    adjacency,
    block_index,
    block_count,
    send_rows,
    row_counts,
    message_weight,
    input_weight,
    input_bias,
    output_weight,
    norm_gain,
):
    loop_size, reps = lax.axis_size("loop"), lax.axis_size("rep")
    plane, depth = plane_of(loop_size)
    sub = 8 // plane
    peers = 2 + reps
    node_rows, width = node_features.shape
    blocks = node_rows // 128
    slots = adjacency.shape[2]
    half_rows = -(-(24 * sub + 8) // 16) * 16
    scale = 1.0 / math.sqrt(node_rows * loop_size * reps)
    vmem, smem = pl.BlockSpec(memory_space=pltpu.VMEM), pl.BlockSpec(memory_space=pltpu.SMEM)
    hbm = pl.BlockSpec(memory_space=pltpu.HBM)
    shape = jax.ShapeDtypeStruct
    wide = (node_rows, width)
    mega = 1024 * 1024
    rows_in = send_rows.reshape(peers, 1, 128)
    hin, meta = pl.pallas_call(
        functools.partial(halo_kernel, reps, loop_size),
        out_shape=(shape((peers, 128, width), BF16), shape((8, 128), jnp.int32)),
        in_specs=[hbm, vmem, smem, vmem, smem],
        out_specs=[hbm, vmem],
        scratch_shapes=[
            pltpu.VMEM(wide, BF16),
            pltpu.VMEM((128, 128), jnp.int32),
            pltpu.VMEM((peers, 128, width), BF16),
            pltpu.SemaphoreType.DMA,
            pltpu.SemaphoreType.DMA,
            pltpu.SemaphoreType.DMA,
        ],
        compiler_params=pltpu.CompilerParams(
            collective_id=0, has_side_effects=True, vmem_limit_bytes=56 * mega
        ),
        name="halo_rows",
    )(node_features, block_index[0, 0], block_count, rows_in, row_counts[0])
    small = pltpu.VMEM(wide, BF16)
    half = width // reps
    results = (
        shape(wide, BF16),
        shape(wide, BF16),
        shape((half, width), F32),
        shape((2 * half, width), F32),
        shape((1, half), F32),
        shape((half, width), F32),
        shape((1, half), F32),
    )
    outs = pl.pallas_call(
        functools.partial(layer_kernel, plane, depth, reps, scale),
        out_shape=results,
        in_specs=[hbm] * 8 + [vmem, smem, vmem, vmem],
        out_specs=[hbm] * 7,
        scratch_shapes=[
            small,
            pltpu.VMEM((width, width), BF16),
            pltpu.VMEM((2 * width, width), BF16),
            pltpu.VMEM((peers, 128, width), BF16),
            pltpu.SMEM((8, 128), jnp.int32),
            pltpu.VMEM((slots, 128, 128), BF16),
            small,
            pltpu.VMEM((width, width), BF16),
            *(pltpu.VMEM(result.shape, result.dtype) for result in results),
            pltpu.VMEM((peers, 128, width), BF16),
            pltpu.VMEM((peers, 128, width), BF16),
            pltpu.VMEM((blocks + peers, 128, width), BF16),
            pltpu.VMEM(wide, F32),
            pltpu.VMEM((peers, 128, width), F32),
            pltpu.VMEM(wide, F32),
            pltpu.VMEM((node_rows, peers * 128), BF16),
            pltpu.VMEM((slots, 128, width), F32),
            small, small, small, small,
            pltpu.VMEM((blocks, 128, width), BF16),
            pltpu.VMEM(wide, F32),
            small,
            pltpu.VMEM((peers, 128, width), BF16),
            pltpu.VMEM((reps * plane, 64 * sub, 128), BF16),
            pltpu.VMEM((reps * plane, 64 * sub, 128), BF16),
            pltpu.VMEM((2, 24 * sub + 8, 128), F32),
            pltpu.VMEM((24 * sub + 8, 128), F32),
            pltpu.VMEM((half_rows, 128), BF16),
            pltpu.VMEM((depth // 2, half_rows, 128), BF16),
            pltpu.VMEM((half_rows, 128), BF16),
            pltpu.VMEM((2 * plane, half_rows, 128), BF16),
            pltpu.VMEM((reps * plane, 16 * sub, 128), BF16),
            pltpu.VMEM((reps * plane, 16 * sub, 128), BF16),
            pltpu.VMEM((16 * sub, 128), BF16),
            pltpu.VMEM((depth, 16 * sub, 128), BF16),
            pltpu.VMEM((16 * sub, 128), BF16),
            pltpu.VMEM((plane, 16 * sub, 128), BF16),
            pltpu.SemaphoreType.DMA((8,)),
            pltpu.SemaphoreType.DMA((7,)),
            pltpu.SemaphoreType.DMA((8,)),
            pltpu.SemaphoreType.DMA((8,)),
        ],
        compiler_params=pltpu.CompilerParams(
            collective_id=1, has_side_effects=True, vmem_limit_bytes=56 * mega
        ),
        name="message_layer",
    )(
        node_features,
        message_weight,
        input_weight,
        hin,
        meta,
        adjacency[0, 0],
        cotangent,
        output_weight,
        rows_in,
        row_counts[0],
        input_bias[None, :],
        norm_gain[None, :],
    )
    new_features, grad_features, grad_mw, grad_iw, grad_bias, grad_ow, grad_gain = pl.pallas_call(
        finish_kernel,
        out_shape=results,
        in_specs=[hbm] * 7,
        out_specs=[hbm] * 7,
        scratch_shapes=[
            *(pltpu.VMEM(result.shape, result.dtype) for result in results),
            pltpu.SemaphoreType.DMA((16,)),
            pltpu.SemaphoreType.DMA((16,)),
        ],
        compiler_params=pltpu.CompilerParams(has_side_effects=True, vmem_limit_bytes=56 * mega),
        name="write_results",
    )(*outs)
    return (
        new_features, grad_features, grad_mw, grad_iw,
        grad_bias.reshape(half), grad_ow, grad_gain.reshape(half),
    )


def solution(mesh):
    in_specs = (
        P(("loop", "rep"), None),
        P(("loop", "rep"), None),
        P("loop", "rep", None, None, None),
        P("loop", "rep", None, None),
        P("loop", "rep"),
        P("loop", "rep", None, None),
        P("loop", "rep", None),
        P(),
        P(),
        P(),
        P(),
        P(),
    )
    out_specs = (
        P(("loop", "rep"), None),
        P(("loop", "rep"), None),
        P("rep", None),
        P("rep", None),
        P("rep"),
        P("rep", None),
        P("rep"),
    )
    return jax.shard_map(shards, mesh=mesh, in_specs=in_specs, out_specs=out_specs, check_vma=False)
```

```python
import functools
import math

import jax
import jax.numpy as jnp
from jax import lax
from jax.experimental import pallas as pl
from jax.experimental.pallas import tpu as pltpu
from jax.sharding import PartitionSpec as P

norm_eps = 1e-05
MESH = pl.DeviceIdType.MESH
BF16, F32 = jnp.bfloat16, jnp.float32


def dot(left, right):
    return jnp.dot(left, right, preferred_element_type=F32)


def dot_right_t(left, right):
    return lax.dot_general(left, right, (((1,), (1,)), ((), ())), preferred_element_type=F32)


def inner_rows(left, right):
    return lax.dot_general(left, right, (((0,), (0,)), ((), ())), preferred_element_type=F32)


def sigmoid(argument):
    return 0.5 * jnp.tanh(0.5 * argument) + 0.5


def row_mean(values):
    return jnp.sum(values, axis=-1, keepdims=True) * (1.0 / values.shape[-1])


def plane_of(loop_size):
    plane = 8 if loop_size % 8 == 0 and loop_size > 8 else 2
    return plane, loop_size // plane


def copy_all(buffer, sem):
    return pltpu.make_async_copy(buffer, buffer, sem)


def slot_order(key_col, key_row, cols):
    shape = (32, 128)
    slot = lax.broadcasted_iota(jnp.int32, shape, 0)
    lane = lax.broadcasted_iota(jnp.int32, shape, 1)
    ahead = (key_row < key_col) | ((key_row == key_col) & (lane < slot))
    rank = jnp.sum(jnp.where(ahead & (lane < 24), 1, 0), axis=1, keepdims=True)
    placed = (rank == lane) & (slot < 24)
    rows = [
        jnp.sum(jnp.where(placed, col, 0), axis=0, keepdims=True) for col in (slot, *cols, key_col)
    ]
    before = pltpu.roll(rows[-1], 1, 1)
    keep = jnp.where((rows[-1] == before) & (lane[:1] > 0), 1, 0)
    last = jnp.sum(jnp.where((key_col <= lane) & (slot < 24), 1, 0), axis=0, keepdims=True) - 1
    last = jnp.maximum(last, 0)
    return [*rows[:-1], keep, last]


def silu_and_slope(pre):
    gate = sigmoid(pre)
    value = pre * gate
    return value.astype(BF16), gate + value * (1.0 - gate)


def remote(source, target, send_sem, recv_sem, device):
    pltpu.make_async_remote_copy(
        source, target, send_sem, recv_sem, device_id=device, device_id_type=MESH
    ).start()


def greet(device):
    pl.semaphore_signal(pltpu.get_barrier_semaphore(), inc=1, device_id=device, device_id_type=MESH)


def halo_kernel(
    reps, loop_size,
    nf_hbm, index_ref, count_ref, rows_ref, kept_ref,
    hin, meta,
    nf_ref, flat, hout, load_sem, send_sem, recv_sem,
):
    node_rows = nf_ref.shape[0]
    blocks = node_rows // 128
    peers = 2 + reps
    loop_at, rep_at = lax.axis_index("loop"), lax.axis_index("rep")
    loop_up = {"loop": lax.rem(loop_at + 1, loop_size), "rep": rep_at}
    loop_down = {"loop": lax.rem(loop_at + loop_size - 1, loop_size), "rep": rep_at}

    load = pltpu.make_async_copy(nf_hbm, nf_ref, load_sem)
    load.start()
    greet(loop_up)
    greet(loop_down)
    for step in range(1, reps):
        greet({"loop": loop_at, "rep": lax.rem(rep_at + step, reps)})
    flat[...] = jnp.zeros(flat.shape, jnp.int32)
    flat[0:2, 0:24] = index_ref[...]
    for k in range(peers):
        flat[8 + k : 9 + k, :] = rows_ref[k]
    turned = jnp.transpose(flat[...])
    lane_rows = lax.broadcasted_iota(jnp.int32, (128, node_rows), 1)
    sub_rows = lax.broadcasted_iota(jnp.int32, (128, node_rows), 0)
    load.wait()

    def pick(k):
        live = (lane_rows == turned[:, 8 + k : 9 + k]) & (sub_rows < kept_ref[0, k])
        picker = jnp.where(live, 1.0, 0.0).astype(BF16)
        hout[k] = dot(picker, nf_ref[...]).astype(BF16)

    pick(0)
    pick(1)
    pl.semaphore_wait(pltpu.get_barrier_semaphore(), 1 + reps)
    remote(hout.at[0], hin.at[0], send_sem, recv_sem, loop_up)
    remote(hout.at[1], hin.at[1], send_sem, recv_sem, loop_down)
    for k in range(2, peers):
        pick(k)
    for step in range(1, reps):
        r_to = lax.rem(rep_at + step, reps)
        remote(
            hout.at[2 + r_to], hin.at[2 + rep_at], send_sem, recv_sem, {"loop": loop_at, "rep": r_to}
        )
    own = pltpu.make_async_copy(hout.at[2 + rep_at], hin.at[2 + rep_at], load_sem)
    own.start()

    live_total = count_ref[0, 0]
    slot_col = lax.broadcasted_iota(jnp.int32, (32, 1), 0)
    slot_row = lax.broadcasted_iota(jnp.int32, (1, 128), 1)
    dest_col, source_col = turned[0:32, 0:1], turned[0:32, 1:2]
    dest_row, source_row = flat[0:1, :], flat[1:2, :]

    def keyed(value, iota):
        return jnp.where(iota < live_total, value, 64)

    def halo_first(value):
        return jnp.where(value >= blocks, value - blocks, value + peers)

    forward = slot_order(keyed(dest_col, slot_col), keyed(dest_row, slot_row), (source_col,))
    backward = slot_order(
        keyed(halo_first(source_col), slot_col), keyed(halo_first(source_row), slot_row), (dest_col,)
    )
    meta[...] = jnp.concatenate(forward + backward, axis=0)

    own.wait()
    copy_all(hin.at[1:], recv_sem).wait()
    copy_all(hin.at[1:], send_sem).wait()


def layer_kernel(
    plane, depth, reps, scale,
    nf_hbm, wm_hbm, wi_hbm, hin_hbm, meta_hbm, adj_hbm, cot_hbm, wo_hbm,
    rows_ref, kept_ref, bias_ref, gain_ref,
    new_hbm, grad_hbm, mw_hbm, iw_hbm, grad_bias_hbm, ow_hbm, grad_gain_hbm,
    nf_ref, wm_ref, wi_ref, hin, meta_s, adj_ref, cot_ref, wo_ref,
    out_new, out_grad, out_mw, out_iw, out_bias, out_ow, out_gain,
    rout, rin, table, own_slope, halo_slope, pre_part, spread, run,
    agg, hidden, outer_grad, pre_grad, agg_grad, norm_rows, own_grad, halo_grad,
    stage_e, land_e, psend, pland, epiece, eland, gpiece_e, gather_e,
    stage_l, land_l, lpiece, lland, gpiece_l, gather_l,
    load_sem, store_sem, send_sem, recv_sem,
):
    sub = 8 // plane
    node_rows = nf_ref.shape[0]
    blocks = node_rows // 128
    peers = 2 + reps
    loop_size = plane * depth
    loop_at, rep_at = lax.axis_index("loop"), lax.axis_index("rep")
    z_at, g_at = loop_at // plane, lax.rem(loop_at, plane)
    team = reps * plane
    team_at = rep_at * plane + g_at
    loop_up = {"loop": lax.rem(loop_at + 1, loop_size), "rep": rep_at}
    loop_down = {"loop": lax.rem(loop_at + loop_size - 1, loop_size), "rep": rep_at}

    def mate(step):
        other = lax.rem(team_at + step, team)
        r_to, g_to = other // plane, lax.rem(other, plane)
        return other, {"loop": z_at * plane + g_to, "rep": r_to}

    def above(step):
        z_to = lax.rem(z_at + step, depth)
        return z_to, {"loop": z_to * plane + g_at, "rep": rep_at}

    parity = lax.rem(z_at, 2)
    z_pair = z_at + 1 - 2 * parity

    def twin(step):
        other = lax.rem(parity * plane + g_at + step, 2 * plane)
        z_to, g_to = z_at - parity + other // plane, lax.rem(other, plane)
        return {"loop": z_to * plane + g_to, "rep": rep_at}

    def send(source, target, sem, device):
        remote(source, target, send_sem.at[sem], recv_sem.at[sem], device)

    def to_team(stage, land, sem):
        land[team_at] = stage[team_at]

        @pl.loop(1, team)
        def _(step):
            other, device = mate(step)
            send(stage.at[other], land.at[team_at], sem, device)

    def to_plane(piece, gather, sem):
        gather[g_at] = piece[...]

        @pl.loop(1, plane)
        def _(step):
            g_to = lax.rem(g_at + step, plane)
            send(piece, gather.at[g_at], sem, {"loop": z_at * plane + g_to, "rep": rep_at})

    def arrived(land, sem):
        if land.shape[0] > 1:
            copy_all(land.at[1:], recv_sem.at[sem]).wait()

    def added(land, count):
        total = land[0].astype(F32)
        return lax.fori_loop(1, count, lambda slot, total: total + land[slot].astype(F32), total)

    loads = [
        pltpu.make_async_copy(source, target, load_sem.at[i])
        for i, (source, target) in enumerate(
            (
                (nf_hbm, nf_ref), (wm_hbm, wm_ref), (wi_hbm, wi_ref), (hin_hbm, hin),
                (meta_hbm, meta_s), (adj_hbm, adj_ref), (cot_hbm, cot_ref), (wo_hbm, wo_ref),
            )
        )
    ]
    for load in loads:
        load.start()
    stores = [
        pltpu.make_async_copy(source, target, store_sem.at[i])
        for i, (source, target) in enumerate(
            (
                (out_new, new_hbm), (out_grad, grad_hbm), (out_mw, mw_hbm), (out_iw, iw_hbm),
                (out_bias, grad_bias_hbm), (out_ow, ow_hbm), (out_gain, grad_gain_hbm),
            )
        )
    ]

    @pl.loop(1, depth)
    def _(step):
        greet(above(step)[1])

    @pl.loop(1, team)
    def _(step):
        greet(mate(step)[1])

    @pl.loop(1, plane)
    def _(step):
        greet({"loop": z_pair * plane + lax.rem(g_at + step, plane), "rep": rep_at})

    greet(loop_up)
    greet(loop_down)

    for load in loads[:3]:
        load.wait()

    @pl.loop(0, node_rows // 256, unroll=2)
    def _(c):
        at = pl.ds(pl.multiple_of(c * 256, 256), 256)
        features = nf_ref[at, :]
        message, own_slope[at, :] = silu_and_slope(dot(features, wm_ref[...]))
        table[pl.ds(2 * c, 2)] = message.reshape(2, 128, 256)
        pre_part[at, :] = dot(features, wi_ref[0:256, :]) + bias_ref[...]

    loads[3].wait()
    half_peers = peers // 2
    for first in range(0, peers, half_peers):
        some = slice(first, first + half_peers)
        message, gate = silu_and_slope(dot(hin[some].reshape(half_peers * 128, 256), wm_ref[...]))
        table[blocks + first : blocks + first + half_peers] = message.reshape(half_peers, 128, 256)
        halo_slope[some] = gate.reshape(half_peers, 128, 256)

    loads[4].wait()
    loads[5].wait()

    def forward_slots(c, total):
        for lap in range(4):
            i = c * 4 + lap
            product = dot(adj_ref[meta_s[0, i]], table[meta_s[1, i]])
            total = product + total * meta_s[2, i].astype(F32)
            run[i] = total
        return total

    lax.fori_loop(0, 6, forward_slots, jnp.zeros((128, 256), F32), unroll=6)

    loads[6].wait()
    loads[7].wait()

    def node_update(c, gain_sum):
        at = pl.ds(pl.multiple_of(c * 256, 256), 256)
        gathered = jnp.concatenate(
            [run[meta_s[3, 2 * c]], run[meta_s[3, 2 * c + 1]]], axis=0
        ).astype(BF16)
        agg[at, :] = gathered
        hid, hid_slope = silu_and_slope(pre_part[at, :] + dot(gathered, wi_ref[256:512, :]))
        hidden[at, :] = hid
        outer = dot(hid, wo_ref[...])
        centered = outer - row_mean(outer)
        inv_std = lax.rsqrt(row_mean(centered * centered) + norm_eps)
        normed = centered * inv_std
        norm_rows[at, :] = normed
        upstream = cot_ref[at, :].astype(F32)
        gained = upstream * gain_ref[...]
        back = ((gained - row_mean(gained) - normed * row_mean(gained * normed)) * inv_std).astype(BF16)
        outer_grad[at, :] = back
        pre_grad[at, :] = (dot_right_t(back, wo_ref[...]) * hid_slope).astype(BF16)
        return gain_sum + jnp.sum(upstream * normed, axis=0, keepdims=True)

    gain_sum = lax.fori_loop(
        0, node_rows // 256, node_update, jnp.zeros((1, 256), F32), unroll=2
    )

    def deal(stage, first, tall, value):
        for rep in range(reps):
            for tile in range(8):
                start, half = (64 * rep + 16 * (tile // 2)) * tall, 128 * (tile % 2)
                slot, place = rep * plane + tile // sub, stage.shape[1] // sub * (tile % sub)
                stage[slot, place + first : place + first + 16 * tall, :] = value[
                    start : start + 16 * tall, half : half + 128
                ].astype(BF16)

    deal(stage_e, 0, 1, inner_rows(hidden[...], outer_grad[...]))
    back_all = pre_grad[...]
    bias_sum = dot(jnp.ones((16, node_rows), BF16), back_all)[0:1]
    deal(
        stage_e, 16, 2,
        jnp.concatenate([inner_rows(nf_ref[...], back_all), inner_rows(agg[...], back_all)], axis=0),
    )
    low_lane = lax.broadcasted_iota(jnp.int32, (1, 128), 1) < 64
    for rep in range(reps):
        at = slice(128 * (rep // 2), 128 * (rep // 2) + 128)
        left, right = bias_sum[:, at], gain_sum[:, at]
        if rep % 2:
            left = pltpu.roll(left, 64, 1)
        else:
            right = pltpu.roll(right, 64, 1)
        both = jnp.broadcast_to(jnp.where(low_lane, left, right), (16, 128)).astype(BF16)
        for g in range(plane):
            stage_e[rep * plane + g, 48:64, :] = both

    pl.semaphore_wait(pltpu.get_barrier_semaphore(), team + depth + plane - 1)
    to_team(stage_e, land_e, 0)

    @pl.loop(0, node_rows // 256, unroll=2)
    def _(c):
        at = pl.ds(pl.multiple_of(c * 256, 256), 256)
        back = dot_right_t(pre_grad[at, :], wi_ref[256:512, :])
        agg_grad[pl.ds(2 * c, 2)] = back.astype(BF16).reshape(2, 128, 256)

    def backward_slots(c, total):
        for lap in range(4):
            i = c * 4 + lap
            product = inner_rows(adj_ref[meta_s[4, i]], agg_grad[meta_s[5, i]])
            total = product + total * meta_s[6, i].astype(F32)
            run[i] = total
        return total

    lax.fori_loop(0, 6, backward_slots, jnp.zeros((128, 256), F32), unroll=6)

    for k in range(peers):
        halo_grad[k] = (run[meta_s[7, k]] * halo_slope[k]).astype(BF16)
    @pl.loop(0, blocks, unroll=4)
    def _(b):
        at = pl.ds(pl.multiple_of(b * 128, 128), 128)
        own_grad[at, :] = (run[meta_s[7, peers + b]] * own_slope[at, :]).astype(BF16)

    message_grad = inner_rows(nf_ref[...], own_grad[...])
    message_grad += inner_rows(hin[...].reshape(peers * 128, 256), halo_grad[...].reshape(peers * 128, 256))
    deal(stage_l, 0, 1, message_grad)
    to_team(stage_l, land_l, 2)

    halo_back = halo_grad[...].reshape(peers * 128, 256)
    rout[...] = dot_right_t(halo_back, wm_ref[...]).astype(BF16).reshape(peers, 128, 256)

    rin[2 + rep_at] = rout[2 + rep_at]
    send(rout.at[0], rin.at[0], 1, loop_down)
    send(rout.at[1], rin.at[1], 1, loop_up)
    for step in range(1, reps):
        r_to = lax.rem(rep_at + step, reps)
        send(rout.at[2 + r_to], rin.at[2 + rep_at], 1, {"loop": loop_at, "rep": r_to})

    row_at = lax.broadcasted_iota(jnp.int32, (node_rows, 128), 0)
    lane_at = lax.broadcasted_iota(jnp.int32, (node_rows, 128), 1)
    for k in range(peers):
        live = (row_at == rows_ref[k]) & (lane_at < kept_ref[0, k])
        spread[:, 128 * k : 128 * k + 128] = jnp.where(live, 1.0, 0.0).astype(BF16)

    arrived(land_e, 0)
    total = added(land_e, team)
    vec_rows = jnp.broadcast_to(total[48:49], (8, 128))
    total = jnp.concatenate([total[64 * tile : 64 * tile + 48] for tile in range(sub)], axis=0)
    rows = 24 * sub
    for part in range(2):
        psend[part, 0:rows, :] = total[part * rows : (part + 1) * rows]
        psend[part, rows:, :] = vec_rows
    send(psend.at[1 - parity], pland, 3, {"loop": z_pair * plane + g_at, "rep": rep_at})

    arrived(land_l, 2)
    lpiece[...] = added(land_l, team).astype(BF16)
    lland[z_at] = lpiece[...]

    @pl.loop(1, depth)
    def _(step):
        send(lpiece, lland.at[z_at], 5, above(step)[1])

    copy_all(pland, recv_sem.at[3]).wait()
    total = psend[parity] + pland[...]
    filler = jnp.zeros((epiece.shape[0] - total.shape[0], 128), F32)
    epiece[...] = (jnp.concatenate([total, filler], axis=0) if filler.shape[0] else total).astype(BF16)
    eland[z_at // 2] = epiece[...]

    @pl.loop(1, depth // 2)
    def _(step):
        send(epiece, eland.at[z_at // 2], 4, above(2 * step)[1])

    arrived(rin, 1)
    returned = rin[...].reshape(peers * 128, 256)

    @pl.loop(0, node_rows // 256, unroll=2)
    def _(c):
        at = pl.ds(pl.multiple_of(c * 256, 256), 256)
        out_new[at, :] = (nf_ref[at, :].astype(F32) + norm_rows[at, :] * gain_ref[...]).astype(BF16)
        total = cot_ref[at, :].astype(F32) + dot_right_t(pre_grad[at, :], wi_ref[0:256, :])
        total += dot_right_t(own_grad[at, :], wm_ref[...])
        out_grad[at, :] = (total + dot(spread[at, :], returned)).astype(BF16)

    stores[0].start()
    stores[1].start()

    arrived(lland, 5)
    gpiece_l[...] = (added(lland, depth) * scale).astype(BF16)
    to_plane(gpiece_l, gather_l, 6)

    arrived(eland, 4)
    total = added(eland, depth // 2) * scale
    vec_row = total[rows : rows + 1]
    half = out_bias.shape[1]
    out_bias[...] = vec_row[:, 0:half]
    out_gain[...] = pltpu.roll(vec_row, half, 1)[:, 0:half]
    stores[4].start()
    stores[6].start()
    gpiece_e[...] = total.astype(BF16)
    gather_e[parity * plane + g_at] = gpiece_e[...]

    @pl.loop(1, 2 * plane)
    def _(step):
        send(gpiece_e, gather_e.at[parity * plane + g_at], 7, twin(step))

    def collect(out, owned, first, tall):
        for tile in range(8):
            row, half = 16 * tall * (tile // 2), 128 * (tile % 2)
            block = owned[tile // sub]
            place = block.shape[0] // sub * (tile % sub) + first
            out[row : row + 16 * tall, half : half + 128] = block[place : place + 16 * tall]

    arrived(gather_l, 6)
    collect(out_mw, [gather_l[g].astype(F32) for g in range(plane)], 0, 1)
    stores[2].start()
    arrived(gather_e, 7)
    owned = [
        jnp.concatenate([gather_e[part * plane + g].astype(F32)[0:rows] for part in range(2)], axis=0)
        for g in range(plane)
    ]
    collect(out_ow, owned, 0, 1)
    stores[5].start()
    collect(out_iw, owned, 16, 2)
    stores[3].start()

    for sem, land in ((0, land_e), (1, rin), (2, land_l), (4, eland), (5, lland), (6, gather_l), (7, gather_e)):
        if land.shape[0] > 1:
            copy_all(land.at[1:], send_sem.at[sem]).wait()
    copy_all(pland, send_sem.at[3]).wait()
    for store in stores:
        store.wait()


def finish_kernel(*refs):
    sources, targets, held, (load_sem, store_sem) = refs[:7], refs[7:14], refs[14:21], refs[21:]
    pieces = []
    for source, target, buffer in zip(sources, targets, held):
        step = min(256, source.shape[0])
        for first in range(0, source.shape[0], step):
            at = pl.ds(first, step)
            i = len(pieces)
            pieces.append(
                (
                    pltpu.make_async_copy(source.at[at], buffer.at[at], load_sem.at[i]),
                    pltpu.make_async_copy(buffer.at[at], target.at[at], store_sem.at[i]),
                )
            )
    for load, _ in pieces:
        load.start()
    for load, store in pieces:
        load.wait()
        store.start()
    for _, store in pieces:
        store.wait()


def shards(
    node_features,
    cotangent,
    adjacency,
    block_index,
    block_count,
    send_rows,
    row_counts,
    message_weight,
    input_weight,
    input_bias,
    output_weight,
    norm_gain,
):
    loop_size, reps = lax.axis_size("loop"), lax.axis_size("rep")
    plane, depth = plane_of(loop_size)
    sub = 8 // plane
    peers = 2 + reps
    node_rows, width = node_features.shape
    blocks = node_rows // 128
    slots = adjacency.shape[2]
    half_rows = -(-(24 * sub + 8) // 16) * 16
    scale = 1.0 / math.sqrt(node_rows * loop_size * reps)
    vmem, smem = pl.BlockSpec(memory_space=pltpu.VMEM), pl.BlockSpec(memory_space=pltpu.SMEM)
    hbm = pl.BlockSpec(memory_space=pltpu.HBM)
    shape = jax.ShapeDtypeStruct
    wide = (node_rows, width)
    mega = 1024 * 1024
    rows_in = send_rows.reshape(peers, 1, 128)
    hin, meta = pl.pallas_call(
        functools.partial(halo_kernel, reps, loop_size),
        out_shape=(shape((peers, 128, width), BF16), shape((8, 128), jnp.int32)),
        in_specs=[hbm, vmem, smem, vmem, smem],
        out_specs=[hbm, vmem],
        scratch_shapes=[
            pltpu.VMEM(wide, BF16),
            pltpu.VMEM((128, 128), jnp.int32),
            pltpu.VMEM((peers, 128, width), BF16),
            pltpu.SemaphoreType.DMA,
            pltpu.SemaphoreType.DMA,
            pltpu.SemaphoreType.DMA,
        ],
        compiler_params=pltpu.CompilerParams(
            collective_id=0, has_side_effects=True, vmem_limit_bytes=56 * mega
        ),
        name="halo_rows",
    )(node_features, block_index[0, 0], block_count, rows_in, row_counts[0])
    small = pltpu.VMEM(wide, BF16)
    half = width // reps
    results = (
        shape(wide, BF16),
        shape(wide, BF16),
        shape((half, width), F32),
        shape((2 * half, width), F32),
        shape((1, half), F32),
        shape((half, width), F32),
        shape((1, half), F32),
    )
    outs = pl.pallas_call(
        functools.partial(layer_kernel, plane, depth, reps, scale),
        out_shape=results,
        in_specs=[hbm] * 8 + [vmem, smem, vmem, vmem],
        out_specs=[hbm] * 7,
        scratch_shapes=[
            small,
            pltpu.VMEM((width, width), BF16),
            pltpu.VMEM((2 * width, width), BF16),
            pltpu.VMEM((peers, 128, width), BF16),
            pltpu.SMEM((8, 128), jnp.int32),
            pltpu.VMEM((slots, 128, 128), BF16),
            small,
            pltpu.VMEM((width, width), BF16),
            *(pltpu.VMEM(result.shape, result.dtype) for result in results),
            pltpu.VMEM((peers, 128, width), BF16),
            pltpu.VMEM((peers, 128, width), BF16),
            pltpu.VMEM((blocks + peers, 128, width), BF16),
            pltpu.VMEM(wide, F32),
            pltpu.VMEM((peers, 128, width), F32),
            pltpu.VMEM(wide, F32),
            pltpu.VMEM((node_rows, peers * 128), BF16),
            pltpu.VMEM((slots, 128, width), F32),
            small, small, small, small,
            pltpu.VMEM((blocks, 128, width), BF16),
            pltpu.VMEM(wide, F32),
            small,
            pltpu.VMEM((peers, 128, width), BF16),
            pltpu.VMEM((reps * plane, 64 * sub, 128), BF16),
            pltpu.VMEM((reps * plane, 64 * sub, 128), BF16),
            pltpu.VMEM((2, 24 * sub + 8, 128), F32),
            pltpu.VMEM((24 * sub + 8, 128), F32),
            pltpu.VMEM((half_rows, 128), BF16),
            pltpu.VMEM((depth // 2, half_rows, 128), BF16),
            pltpu.VMEM((half_rows, 128), BF16),
            pltpu.VMEM((2 * plane, half_rows, 128), BF16),
            pltpu.VMEM((reps * plane, 16 * sub, 128), BF16),
            pltpu.VMEM((reps * plane, 16 * sub, 128), BF16),
            pltpu.VMEM((16 * sub, 128), BF16),
            pltpu.VMEM((depth, 16 * sub, 128), BF16),
            pltpu.VMEM((16 * sub, 128), BF16),
            pltpu.VMEM((plane, 16 * sub, 128), BF16),
            pltpu.SemaphoreType.DMA((8,)),
            pltpu.SemaphoreType.DMA((7,)),
            pltpu.SemaphoreType.DMA((8,)),
            pltpu.SemaphoreType.DMA((8,)),
        ],
        compiler_params=pltpu.CompilerParams(
            collective_id=1, has_side_effects=True, vmem_limit_bytes=56 * mega
        ),
        name="message_layer",
    )(
        node_features,
        message_weight,
        input_weight,
        hin,
        meta,
        adjacency[0, 0],
        cotangent,
        output_weight,
        rows_in,
        row_counts[0],
        input_bias[None, :],
        norm_gain[None, :],
    )
    new_features, grad_features, grad_mw, grad_iw, grad_bias, grad_ow, grad_gain = pl.pallas_call(
        finish_kernel,
        out_shape=results,
        in_specs=[hbm] * 7,
        out_specs=[hbm] * 7,
        scratch_shapes=[
            *(pltpu.VMEM(result.shape, result.dtype) for result in results),
            pltpu.SemaphoreType.DMA((16,)),
            pltpu.SemaphoreType.DMA((16,)),
        ],
        compiler_params=pltpu.CompilerParams(has_side_effects=True, vmem_limit_bytes=56 * mega),
        name="write_results",
    )(*outs)
    return (
        new_features, grad_features, grad_mw, grad_iw,
        grad_bias.reshape(half), grad_ow, grad_gain.reshape(half),
    )


def solution(mesh):
    in_specs = (
        P(("loop", "rep"), None),
        P(("loop", "rep"), None),
        P("loop", "rep", None, None, None),
        P("loop", "rep", None, None),
        P("loop", "rep"),
        P("loop", "rep", None, None),
        P("loop", "rep", None),
        P(),
        P(),
        P(),
        P(),
        P(),
    )
    out_specs = (
        P(("loop", "rep"), None),
        P(("loop", "rep"), None),
        P("rep", None),
        P("rep", None),
        P("rep"),
        P("rep", None),
        P("rep"),
    )
    return jax.shard_map(shards, mesh=mesh, in_specs=in_specs, out_specs=out_specs, check_vma=False)
```

```python
import functools
import math

import jax
import jax.numpy as jnp
from jax import lax
from jax.experimental import pallas as pl
from jax.experimental.pallas import tpu as pltpu
from jax.sharding import PartitionSpec as P

norm_eps = 1e-05
MESH = pl.DeviceIdType.MESH
BF16, F32 = jnp.bfloat16, jnp.float32


def dot(left, right):
    return jnp.dot(left, right, preferred_element_type=F32)


def dot_right_t(left, right):
    return lax.dot_general(left, right, (((1,), (1,)), ((), ())), preferred_element_type=F32)


def inner_rows(left, right):
    return lax.dot_general(left, right, (((0,), (0,)), ((), ())), preferred_element_type=F32)


def sigmoid(argument):
    return 0.5 * jnp.tanh(0.5 * argument) + 0.5


def row_mean(values):
    return jnp.sum(values, axis=-1, keepdims=True) * (1.0 / values.shape[-1])


def plane_of(loop_size):
    plane = 8 if loop_size % 8 == 0 and loop_size > 8 else 2
    return plane, loop_size // plane


def copy_all(buffer, sem):
    return pltpu.make_async_copy(buffer, buffer, sem)


def slot_order(key_col, key_row, cols):
    shape = (32, 128)
    slot = lax.broadcasted_iota(jnp.int32, shape, 0)
    lane = lax.broadcasted_iota(jnp.int32, shape, 1)
    ahead = (key_row < key_col) | ((key_row == key_col) & (lane < slot))
    rank = jnp.sum(jnp.where(ahead & (lane < 24), 1, 0), axis=1, keepdims=True)
    placed = (rank == lane) & (slot < 24)
    rows = [
        jnp.sum(jnp.where(placed, col, 0), axis=0, keepdims=True) for col in (slot, *cols, key_col)
    ]
    before = pltpu.roll(rows[-1], 1, 1)
    keep = jnp.where((rows[-1] == before) & (lane[:1] > 0), 1, 0)
    last = jnp.sum(jnp.where((key_col <= lane) & (slot < 24), 1, 0), axis=0, keepdims=True) - 1
    last = jnp.maximum(last, 0)
    return [*rows[:-1], keep, last]


def silu_and_slope(pre):
    gate = sigmoid(pre)
    value = pre * gate
    return value.astype(BF16), gate + value * (1.0 - gate)


def remote(source, target, send_sem, recv_sem, device):
    pltpu.make_async_remote_copy(
        source, target, send_sem, recv_sem, device_id=device, device_id_type=MESH
    ).start()


def greet(device):
    pl.semaphore_signal(pltpu.get_barrier_semaphore(), inc=1, device_id=device, device_id_type=MESH)


def halo_kernel(
    reps, loop_size,
    nf_hbm, wm_hbm, index_ref, count_ref, rows_ref, kept_ref,
    hin, messages, meta,
    nf_ref, wm_ref, flat, hout, held, load_sem, send_sem, recv_sem,
):
    node_rows = nf_ref.shape[0]
    blocks = node_rows // 128
    peers = 2 + reps
    loop_at, rep_at = lax.axis_index("loop"), lax.axis_index("rep")
    loop_up = {"loop": lax.rem(loop_at + 1, loop_size), "rep": rep_at}
    loop_down = {"loop": lax.rem(loop_at + loop_size - 1, loop_size), "rep": rep_at}

    load = pltpu.make_async_copy(nf_hbm, nf_ref, load_sem.at[0])
    load.start()
    load_wm = pltpu.make_async_copy(wm_hbm, wm_ref, load_sem.at[1])
    load_wm.start()
    greet(loop_up)
    greet(loop_down)
    for step in range(1, reps):
        greet({"loop": loop_at, "rep": lax.rem(rep_at + step, reps)})
    flat[...] = jnp.zeros(flat.shape, jnp.int32)
    flat[0:2, 0:24] = index_ref[...]
    for k in range(peers):
        flat[8 + k : 9 + k, :] = rows_ref[k]
    turned = jnp.transpose(flat[...])
    lane_rows = lax.broadcasted_iota(jnp.int32, (128, node_rows), 1)
    sub_rows = lax.broadcasted_iota(jnp.int32, (128, node_rows), 0)
    load.wait()

    def pick(k):
        live = (lane_rows == turned[:, 8 + k : 9 + k]) & (sub_rows < kept_ref[0, k])
        picker = jnp.where(live, 1.0, 0.0).astype(BF16)
        hout[k] = dot(picker, nf_ref[...]).astype(BF16)

    pick(0)
    pick(1)
    pl.semaphore_wait(pltpu.get_barrier_semaphore(), 1 + reps)
    remote(hout.at[0], hin.at[0], send_sem, recv_sem, loop_up)
    remote(hout.at[1], hin.at[1], send_sem, recv_sem, loop_down)
    for k in range(2, peers):
        pick(k)
    for step in range(1, reps):
        r_to = lax.rem(rep_at + step, reps)
        remote(
            hout.at[2 + r_to], hin.at[2 + rep_at], send_sem, recv_sem, {"loop": loop_at, "rep": r_to}
        )
    own = pltpu.make_async_copy(hout.at[2 + rep_at], hin.at[2 + rep_at], load_sem.at[2])
    own.start()

    load_wm.wait()
    value, _ = silu_and_slope(dot(nf_ref[...], wm_ref[...]))
    held[...] = value.reshape(blocks, 128, 256)
    store = pltpu.make_async_copy(held, messages, load_sem.at[3])
    store.start()

    live_total = count_ref[0, 0]
    slot_col = lax.broadcasted_iota(jnp.int32, (32, 1), 0)
    slot_row = lax.broadcasted_iota(jnp.int32, (1, 128), 1)
    dest_col, source_col = turned[0:32, 0:1], turned[0:32, 1:2]
    dest_row, source_row = flat[0:1, :], flat[1:2, :]

    def keyed(value, iota):
        return jnp.where(iota < live_total, value, 64)

    def halo_first(value):
        return jnp.where(value >= blocks, value - blocks, value + peers)

    forward = slot_order(keyed(dest_col, slot_col), keyed(dest_row, slot_row), (source_col,))
    backward = slot_order(
        keyed(halo_first(source_col), slot_col), keyed(halo_first(source_row), slot_row), (dest_col,)
    )
    meta[...] = jnp.concatenate(forward + backward, axis=0)

    own.wait()
    store.wait()
    copy_all(hin.at[1:], recv_sem).wait()
    copy_all(hin.at[1:], send_sem).wait()


def layer_kernel(
    plane, depth, reps, scale,
    messages_hbm, hin_hbm, wm_hbm, meta_hbm, adj_hbm, nf_hbm, wi_hbm, wo_hbm, cot_hbm,
    rows_ref, kept_ref, bias_ref, gain_ref,
    new_hbm, grad_hbm, mw_hbm, iw_hbm, grad_bias_hbm, ow_hbm, grad_gain_hbm,
    table, hin, wm_ref, meta_s, adj_ref, nf_ref, wi_ref, wo_ref, cot_ref,
    out_new, out_grad, out_mw, out_iw, out_bias, out_ow, out_gain,
    rout, rin, halo_slope, spread, run,
    agg, hidden, outer_grad, pre_grad, agg_grad, norm_rows, own_grad, halo_grad,
    stage_e, land_e, psend, pland, epiece, eland, gpiece_e, gather_e,
    stage_l, land_l, lpiece, lland, gpiece_l, gather_l,
    load_sem, store_sem, send_sem, recv_sem,
):
    sub = 8 // plane
    node_rows = nf_ref.shape[0]
    blocks = node_rows // 128
    peers = 2 + reps
    loop_size = plane * depth
    loop_at, rep_at = lax.axis_index("loop"), lax.axis_index("rep")
    z_at, g_at = loop_at // plane, lax.rem(loop_at, plane)
    team = reps * plane
    team_at = rep_at * plane + g_at
    loop_up = {"loop": lax.rem(loop_at + 1, loop_size), "rep": rep_at}
    loop_down = {"loop": lax.rem(loop_at + loop_size - 1, loop_size), "rep": rep_at}

    def mate(step):
        other = lax.rem(team_at + step, team)
        r_to, g_to = other // plane, lax.rem(other, plane)
        return other, {"loop": z_at * plane + g_to, "rep": r_to}

    def above(step):
        z_to = lax.rem(z_at + step, depth)
        return z_to, {"loop": z_to * plane + g_at, "rep": rep_at}

    parity = lax.rem(z_at, 2)
    z_pair = z_at + 1 - 2 * parity

    def twin(step):
        other = lax.rem(parity * plane + g_at + step, 2 * plane)
        z_to, g_to = z_at - parity + other // plane, lax.rem(other, plane)
        return {"loop": z_to * plane + g_to, "rep": rep_at}

    def send(source, target, sem, device):
        remote(source, target, send_sem.at[sem], recv_sem.at[sem], device)

    def to_team(stage, land, sem):
        land[team_at] = stage[team_at]

        @pl.loop(1, team)
        def _(step):
            other, device = mate(step)
            send(stage.at[other], land.at[team_at], sem, device)

    def to_plane(piece, gather, sem):
        gather[g_at] = piece[...]

        @pl.loop(1, plane)
        def _(step):
            g_to = lax.rem(g_at + step, plane)
            send(piece, gather.at[g_at], sem, {"loop": z_at * plane + g_to, "rep": rep_at})

    def arrived(land, sem):
        if land.shape[0] > 1:
            copy_all(land.at[1:], recv_sem.at[sem]).wait()

    def added(land, count):
        total = land[0].astype(F32)
        return lax.fori_loop(1, count, lambda slot, total: total + land[slot].astype(F32), total)

    loads = [
        pltpu.make_async_copy(source, target, load_sem.at[i])
        for i, (source, target) in enumerate(
            (
                (messages_hbm, table.at[0:blocks]), (hin_hbm, hin), (wm_hbm, wm_ref),
                (meta_hbm, meta_s), (adj_hbm, adj_ref), (nf_hbm, nf_ref), (wi_hbm, wi_ref),
                (wo_hbm, wo_ref), (cot_hbm, cot_ref),
            )
        )
    ]
    for load in loads:
        load.start()
    stores = [
        pltpu.make_async_copy(source, target, store_sem.at[i])
        for i, (source, target) in enumerate(
            (
                (out_new, new_hbm), (out_grad, grad_hbm), (out_mw, mw_hbm), (out_iw, iw_hbm),
                (out_bias, grad_bias_hbm), (out_ow, ow_hbm), (out_gain, grad_gain_hbm),
            )
        )
    ]

    @pl.loop(1, depth)
    def _(step):
        greet(above(step)[1])

    @pl.loop(1, team)
    def _(step):
        greet(mate(step)[1])

    @pl.loop(1, plane)
    def _(step):
        greet({"loop": z_pair * plane + lax.rem(g_at + step, plane), "rep": rep_at})

    greet(loop_up)
    greet(loop_down)

    loads[1].wait()
    loads[2].wait()
    half_peers = peers // 2
    for first in range(0, peers, half_peers):
        some = slice(first, first + half_peers)
        message, gate = silu_and_slope(dot(hin[some].reshape(half_peers * 128, 256), wm_ref[...]))
        table[blocks + first : blocks + first + half_peers] = message.reshape(half_peers, 128, 256)
        halo_slope[some] = gate.reshape(half_peers, 128, 256)

    for load in (loads[0], loads[3], loads[4]):
        load.wait()

    def forward_slots(c, total):
        for lap in range(4):
            i = c * 4 + lap
            product = dot(adj_ref[meta_s[0, i]], table[meta_s[1, i]])
            total = product + total * meta_s[2, i].astype(F32)
            run[i] = total
        return total

    lax.fori_loop(0, 6, forward_slots, jnp.zeros((128, 256), F32), unroll=6)

    for load in loads[5:]:
        load.wait()

    def node_update(c, gain_sum):
        at = pl.ds(pl.multiple_of(c * 256, 256), 256)
        gathered = jnp.concatenate(
            [run[meta_s[3, 2 * c]], run[meta_s[3, 2 * c + 1]]], axis=0
        ).astype(BF16)
        agg[at, :] = gathered
        pre = dot(nf_ref[at, :], wi_ref[0:256, :]) + bias_ref[...]
        hid, hid_slope = silu_and_slope(pre + dot(gathered, wi_ref[256:512, :]))
        hidden[at, :] = hid
        outer = dot(hid, wo_ref[...])
        centered = outer - row_mean(outer)
        inv_std = lax.rsqrt(row_mean(centered * centered) + norm_eps)
        normed = centered * inv_std
        norm_rows[at, :] = normed
        upstream = cot_ref[at, :].astype(F32)
        gained = upstream * gain_ref[...]
        back = ((gained - row_mean(gained) - normed * row_mean(gained * normed)) * inv_std).astype(BF16)
        outer_grad[at, :] = back
        pre_grad[at, :] = (dot_right_t(back, wo_ref[...]) * hid_slope).astype(BF16)
        return gain_sum + jnp.sum(upstream * normed, axis=0, keepdims=True)

    gain_sum = lax.fori_loop(
        0, node_rows // 256, node_update, jnp.zeros((1, 256), F32), unroll=2
    )

    def deal(stage, first, tall, value):
        for rep in range(reps):
            for tile in range(8):
                start, half = (64 * rep + 16 * (tile // 2)) * tall, 128 * (tile % 2)
                slot, place = rep * plane + tile // sub, stage.shape[1] // sub * (tile % sub)
                stage[slot, place + first : place + first + 16 * tall, :] = value[
                    start : start + 16 * tall, half : half + 128
                ].astype(BF16)

    deal(stage_e, 0, 1, inner_rows(hidden[...], outer_grad[...]))
    back_all = pre_grad[...]
    bias_sum = dot(jnp.ones((16, node_rows), BF16), back_all)[0:1]
    deal(
        stage_e, 16, 2,
        jnp.concatenate([inner_rows(nf_ref[...], back_all), inner_rows(agg[...], back_all)], axis=0),
    )
    low_lane = lax.broadcasted_iota(jnp.int32, (1, 128), 1) < 64
    for rep in range(reps):
        at = slice(128 * (rep // 2), 128 * (rep // 2) + 128)
        left, right = bias_sum[:, at], gain_sum[:, at]
        if rep % 2:
            left = pltpu.roll(left, 64, 1)
        else:
            right = pltpu.roll(right, 64, 1)
        both = jnp.broadcast_to(jnp.where(low_lane, left, right), (16, 128)).astype(BF16)
        for g in range(plane):
            stage_e[rep * plane + g, 48:64, :] = both

    pl.semaphore_wait(pltpu.get_barrier_semaphore(), team + depth + plane - 1)
    to_team(stage_e, land_e, 0)

    @pl.loop(0, node_rows // 256, unroll=2)
    def _(c):
        at = pl.ds(pl.multiple_of(c * 256, 256), 256)
        back = dot_right_t(pre_grad[at, :], wi_ref[256:512, :])
        agg_grad[pl.ds(2 * c, 2)] = back.astype(BF16).reshape(2, 128, 256)

    def backward_slots(c, total):
        for lap in range(4):
            i = c * 4 + lap
            product = inner_rows(adj_ref[meta_s[4, i]], agg_grad[meta_s[5, i]])
            total = product + total * meta_s[6, i].astype(F32)
            run[i] = total
        return total

    lax.fori_loop(0, 6, backward_slots, jnp.zeros((128, 256), F32), unroll=6)

    for k in range(peers):
        halo_grad[k] = (run[meta_s[7, k]] * halo_slope[k]).astype(BF16)
    @pl.loop(0, blocks, unroll=4)
    def _(b):
        at = pl.ds(pl.multiple_of(b * 128, 128), 128)
        _, own_slope = silu_and_slope(dot(nf_ref[at, :], wm_ref[...]))
        own_grad[at, :] = (run[meta_s[7, peers + b]] * own_slope).astype(BF16)

    message_grad = inner_rows(nf_ref[...], own_grad[...])
    message_grad += inner_rows(hin[...].reshape(peers * 128, 256), halo_grad[...].reshape(peers * 128, 256))
    deal(stage_l, 0, 1, message_grad)
    to_team(stage_l, land_l, 2)

    row_at = lax.broadcasted_iota(jnp.int32, (node_rows, 128), 0)
    lane_at = lax.broadcasted_iota(jnp.int32, (node_rows, 128), 1)
    for k in range(peers):
        live = (row_at == rows_ref[k]) & (lane_at < kept_ref[0, k])
        spread[:, 128 * k : 128 * k + 128] = jnp.where(live, 1.0, 0.0).astype(BF16)

    arrived(land_e, 0)
    total = added(land_e, team)
    vec_rows = jnp.broadcast_to(total[48:49], (8, 128))
    total = jnp.concatenate([total[64 * tile : 64 * tile + 48] for tile in range(sub)], axis=0)
    rows = 24 * sub
    for part in range(2):
        psend[part, 0:rows, :] = total[part * rows : (part + 1) * rows]
        psend[part, rows:, :] = vec_rows
    send(psend.at[1 - parity], pland, 3, {"loop": z_pair * plane + g_at, "rep": rep_at})

    arrived(land_l, 2)
    lpiece[...] = added(land_l, team).astype(BF16)
    lland[z_at] = lpiece[...]

    @pl.loop(1, depth)
    def _(step):
        send(lpiece, lland.at[z_at], 5, above(step)[1])

    halo_back = halo_grad[...].reshape(peers * 128, 256)
    rout[...] = dot_right_t(halo_back, wm_ref[...]).astype(BF16).reshape(peers, 128, 256)

    rin[2 + rep_at] = rout[2 + rep_at]
    send(rout.at[0], rin.at[0], 1, loop_down)
    send(rout.at[1], rin.at[1], 1, loop_up)
    for step in range(1, reps):
        r_to = lax.rem(rep_at + step, reps)
        send(rout.at[2 + r_to], rin.at[2 + rep_at], 1, {"loop": loop_at, "rep": r_to})

    copy_all(pland, recv_sem.at[3]).wait()
    total = psend[parity] + pland[...]
    filler = jnp.zeros((epiece.shape[0] - total.shape[0], 128), F32)
    epiece[...] = (jnp.concatenate([total, filler], axis=0) if filler.shape[0] else total).astype(BF16)
    eland[z_at // 2] = epiece[...]

    @pl.loop(1, depth // 2)
    def _(step):
        send(epiece, eland.at[z_at // 2], 4, above(2 * step)[1])

    arrived(rin, 1)
    returned = rin[...].reshape(peers * 128, 256)

    @pl.loop(0, node_rows // 256, unroll=2)
    def _(c):
        at = pl.ds(pl.multiple_of(c * 256, 256), 256)
        out_new[at, :] = (nf_ref[at, :].astype(F32) + norm_rows[at, :] * gain_ref[...]).astype(BF16)
        total = cot_ref[at, :].astype(F32) + dot_right_t(pre_grad[at, :], wi_ref[0:256, :])
        total += dot_right_t(own_grad[at, :], wm_ref[...])
        out_grad[at, :] = (total + dot(spread[at, :], returned)).astype(BF16)

    stores[0].start()
    stores[1].start()

    arrived(lland, 5)
    gpiece_l[...] = (added(lland, depth) * scale).astype(BF16)
    to_plane(gpiece_l, gather_l, 6)

    arrived(eland, 4)
    total = added(eland, depth // 2) * scale
    vec_row = total[rows : rows + 1]
    half = out_bias.shape[1]
    out_bias[...] = vec_row[:, 0:half]
    out_gain[...] = pltpu.roll(vec_row, half, 1)[:, 0:half]
    stores[4].start()
    stores[6].start()
    gpiece_e[...] = total.astype(BF16)
    gather_e[parity * plane + g_at] = gpiece_e[...]

    @pl.loop(1, 2 * plane)
    def _(step):
        send(gpiece_e, gather_e.at[parity * plane + g_at], 7, twin(step))

    def collect(out, owned, first, tall):
        for tile in range(8):
            row, half = 16 * tall * (tile // 2), 128 * (tile % 2)
            block = owned[tile // sub]
            place = block.shape[0] // sub * (tile % sub) + first
            out[row : row + 16 * tall, half : half + 128] = block[place : place + 16 * tall]

    arrived(gather_l, 6)
    collect(out_mw, [gather_l[g].astype(F32) for g in range(plane)], 0, 1)
    stores[2].start()
    arrived(gather_e, 7)
    owned = [
        jnp.concatenate([gather_e[part * plane + g].astype(F32)[0:rows] for part in range(2)], axis=0)
        for g in range(plane)
    ]
    collect(out_ow, owned, 0, 1)
    stores[5].start()
    collect(out_iw, owned, 16, 2)
    stores[3].start()

    for sem, land in ((0, land_e), (1, rin), (2, land_l), (4, eland), (5, lland), (6, gather_l), (7, gather_e)):
        if land.shape[0] > 1:
            copy_all(land.at[1:], send_sem.at[sem]).wait()
    copy_all(pland, send_sem.at[3]).wait()
    for store in stores:
        store.wait()


def finish_kernel(*refs):
    sources, targets, held, (load_sem, store_sem) = refs[:7], refs[7:14], refs[14:21], refs[21:]
    pieces = []
    for source, target, buffer in zip(sources, targets, held):
        step = min(256, source.shape[0])
        for first in range(0, source.shape[0], step):
            at = pl.ds(first, step)
            i = len(pieces)
            pieces.append(
                (
                    pltpu.make_async_copy(source.at[at], buffer.at[at], load_sem.at[i]),
                    pltpu.make_async_copy(buffer.at[at], target.at[at], store_sem.at[i]),
                )
            )
    for load, _ in pieces:
        load.start()
    for load, store in pieces:
        load.wait()
        store.start()
    for _, store in pieces:
        store.wait()


def shards(
    node_features,
    cotangent,
    adjacency,
    block_index,
    block_count,
    send_rows,
    row_counts,
    message_weight,
    input_weight,
    input_bias,
    output_weight,
    norm_gain,
):
    loop_size, reps = lax.axis_size("loop"), lax.axis_size("rep")
    plane, depth = plane_of(loop_size)
    sub = 8 // plane
    peers = 2 + reps
    node_rows, width = node_features.shape
    blocks = node_rows // 128
    slots = adjacency.shape[2]
    half_rows = -(-(24 * sub + 8) // 16) * 16
    scale = 1.0 / math.sqrt(node_rows * loop_size * reps)
    vmem, smem = pl.BlockSpec(memory_space=pltpu.VMEM), pl.BlockSpec(memory_space=pltpu.SMEM)
    hbm = pl.BlockSpec(memory_space=pltpu.HBM)
    shape = jax.ShapeDtypeStruct
    wide = (node_rows, width)
    mega = 1024 * 1024
    rows_in = send_rows.reshape(peers, 1, 128)
    hin, messages, meta = pl.pallas_call(
        functools.partial(halo_kernel, reps, loop_size),
        out_shape=(
            shape((peers, 128, width), BF16),
            shape((blocks, 128, width), BF16),
            shape((8, 128), jnp.int32),
        ),
        in_specs=[hbm, hbm, vmem, smem, vmem, smem],
        out_specs=[hbm, hbm, vmem],
        scratch_shapes=[
            pltpu.VMEM(wide, BF16),
            pltpu.VMEM((width, width), BF16),
            pltpu.VMEM((128, 128), jnp.int32),
            pltpu.VMEM((peers, 128, width), BF16),
            pltpu.VMEM((blocks, 128, width), BF16),
            pltpu.SemaphoreType.DMA((4,)),
            pltpu.SemaphoreType.DMA,
            pltpu.SemaphoreType.DMA,
        ],
        compiler_params=pltpu.CompilerParams(
            collective_id=0, has_side_effects=True, vmem_limit_bytes=56 * mega
        ),
        name="halo_rows",
    )(node_features, message_weight, block_index[0, 0], block_count, rows_in, row_counts[0])
    small = pltpu.VMEM(wide, BF16)
    half = width // reps
    results = (
        shape(wide, BF16),
        shape(wide, BF16),
        shape((half, width), F32),
        shape((2 * half, width), F32),
        shape((1, half), F32),
        shape((half, width), F32),
        shape((1, half), F32),
    )
    outs = pl.pallas_call(
        functools.partial(layer_kernel, plane, depth, reps, scale),
        out_shape=results,
        in_specs=[hbm] * 9 + [vmem, smem, vmem, vmem],
        out_specs=[hbm] * 7,
        scratch_shapes=[
            pltpu.VMEM((blocks + peers, 128, width), BF16),
            pltpu.VMEM((peers, 128, width), BF16),
            pltpu.VMEM((width, width), BF16),
            pltpu.SMEM((8, 128), jnp.int32),
            pltpu.VMEM((slots, 128, 128), BF16),
            small,
            pltpu.VMEM((2 * width, width), BF16),
            pltpu.VMEM((width, width), BF16),
            small,
            *(pltpu.VMEM(result.shape, result.dtype) for result in results),
            pltpu.VMEM((peers, 128, width), BF16),
            pltpu.VMEM((peers, 128, width), BF16),
            pltpu.VMEM((peers, 128, width), F32),
            pltpu.VMEM((node_rows, peers * 128), BF16),
            pltpu.VMEM((slots, 128, width), F32),
            small, small, small, small,
            pltpu.VMEM((blocks, 128, width), BF16),
            pltpu.VMEM(wide, F32),
            small,
            pltpu.VMEM((peers, 128, width), BF16),
            pltpu.VMEM((reps * plane, 64 * sub, 128), BF16),
            pltpu.VMEM((reps * plane, 64 * sub, 128), BF16),
            pltpu.VMEM((2, 24 * sub + 8, 128), F32),
            pltpu.VMEM((24 * sub + 8, 128), F32),
            pltpu.VMEM((half_rows, 128), BF16),
            pltpu.VMEM((depth // 2, half_rows, 128), BF16),
            pltpu.VMEM((half_rows, 128), BF16),
            pltpu.VMEM((2 * plane, half_rows, 128), BF16),
            pltpu.VMEM((reps * plane, 16 * sub, 128), BF16),
            pltpu.VMEM((reps * plane, 16 * sub, 128), BF16),
            pltpu.VMEM((16 * sub, 128), BF16),
            pltpu.VMEM((depth, 16 * sub, 128), BF16),
            pltpu.VMEM((16 * sub, 128), BF16),
            pltpu.VMEM((plane, 16 * sub, 128), BF16),
            pltpu.SemaphoreType.DMA((9,)),
            pltpu.SemaphoreType.DMA((7,)),
            pltpu.SemaphoreType.DMA((8,)),
            pltpu.SemaphoreType.DMA((8,)),
        ],
        compiler_params=pltpu.CompilerParams(
            collective_id=1, has_side_effects=True, vmem_limit_bytes=56 * mega
        ),
        name="message_layer",
    )(
        messages,
        hin,
        message_weight,
        meta,
        adjacency[0, 0],
        node_features,
        input_weight,
        output_weight,
        cotangent,
        rows_in,
        row_counts[0],
        input_bias[None, :],
        norm_gain[None, :],
    )
    new_features, grad_features, grad_mw, grad_iw, grad_bias, grad_ow, grad_gain = pl.pallas_call(
        finish_kernel,
        out_shape=results,
        in_specs=[hbm] * 7,
        out_specs=[hbm] * 7,
        scratch_shapes=[
            *(pltpu.VMEM(result.shape, result.dtype) for result in results),
            pltpu.SemaphoreType.DMA((16,)),
            pltpu.SemaphoreType.DMA((16,)),
        ],
        compiler_params=pltpu.CompilerParams(has_side_effects=True, vmem_limit_bytes=56 * mega),
        name="write_results",
    )(*outs)
    return (
        new_features, grad_features, grad_mw, grad_iw,
        grad_bias.reshape(half), grad_ow, grad_gain.reshape(half),
    )


def solution(mesh):
    in_specs = (
        P(("loop", "rep"), None),
        P(("loop", "rep"), None),
        P("loop", "rep", None, None, None),
        P("loop", "rep", None, None),
        P("loop", "rep"),
        P("loop", "rep", None, None),
        P("loop", "rep", None),
        P(),
        P(),
        P(),
        P(),
        P(),
    )
    out_specs = (
        P(("loop", "rep"), None),
        P(("loop", "rep"), None),
        P("rep", None),
        P("rep", None),
        P("rep"),
        P("rep", None),
        P("rep"),
    )
    return jax.shard_map(shards, mesh=mesh, in_specs=in_specs, out_specs=out_specs, check_vma=False)
```

```python
import functools
import math

import jax
import jax.numpy as jnp
from jax import lax
from jax.experimental import pallas as pl
from jax.experimental.pallas import tpu as pltpu
from jax.sharding import PartitionSpec as P

norm_eps = 1e-05
MESH = pl.DeviceIdType.MESH
BF16, F32 = jnp.bfloat16, jnp.float32


def dot(left, right):
    return jnp.dot(left, right, preferred_element_type=F32)


def dot_right_t(left, right):
    return lax.dot_general(left, right, (((1,), (1,)), ((), ())), preferred_element_type=F32)


def inner_rows(left, right):
    return lax.dot_general(left, right, (((0,), (0,)), ((), ())), preferred_element_type=F32)


def sigmoid(argument):
    return 0.5 * jnp.tanh(0.5 * argument) + 0.5


def row_mean(values):
    return jnp.sum(values, axis=-1, keepdims=True) * (1.0 / values.shape[-1])


def plane_of(loop_size):
    plane = 8 if loop_size % 8 == 0 and loop_size > 8 else 2
    return plane, loop_size // plane


def copy_all(buffer, sem):
    return pltpu.make_async_copy(buffer, buffer, sem)


def slot_order(key_col, key_row, cols):
    shape = (32, 128)
    slot = lax.broadcasted_iota(jnp.int32, shape, 0)
    lane = lax.broadcasted_iota(jnp.int32, shape, 1)
    ahead = (key_row < key_col) | ((key_row == key_col) & (lane < slot))
    rank = jnp.sum(jnp.where(ahead & (lane < 24), 1, 0), axis=1, keepdims=True)
    placed = (rank == lane) & (slot < 24)
    rows = [
        jnp.sum(jnp.where(placed, col, 0), axis=0, keepdims=True) for col in (slot, *cols, key_col)
    ]
    before = pltpu.roll(rows[-1], 1, 1)
    keep = jnp.where((rows[-1] == before) & (lane[:1] > 0), 1, 0)
    last = jnp.sum(jnp.where((key_col <= lane) & (slot < 24), 1, 0), axis=0, keepdims=True) - 1
    last = jnp.maximum(last, 0)
    return [*rows[:-1], keep, last]


def silu_and_slope(pre):
    gate = sigmoid(pre)
    value = pre * gate
    return value.astype(BF16), gate + value * (1.0 - gate)


def remote(source, target, send_sem, recv_sem, device):
    pltpu.make_async_remote_copy(
        source, target, send_sem, recv_sem, device_id=device, device_id_type=MESH
    ).start()


def greet(device):
    pl.semaphore_signal(pltpu.get_barrier_semaphore(), inc=1, device_id=device, device_id_type=MESH)


def layer_kernel(
    plane, depth, reps, scale,
    nf_hbm, wm_hbm, adj_hbm, wi_hbm, wo_hbm, cot_hbm,
    index_ref, count_ref, rows_ref, kept_ref, bias_ref, gain_ref,
    new_hbm, grad_hbm, mw_hbm, iw_hbm, grad_bias_hbm, ow_hbm, grad_gain_hbm,
    nf_ref, wm_ref, adj_ref, wi_ref, wo_ref, cot_ref,
    flat, meta_v, meta_s, hout, hin, table,
    out_new, out_grad, out_mw, out_iw, out_bias, out_ow, out_gain,
    rout, rin, halo_slope, spread, run,
    agg, hidden, outer_grad, pre_grad, agg_grad, norm_rows, own_grad, halo_grad,
    stage_e, land_e, psend, pland, epiece, eland, gpiece_e, gather_e,
    stage_l, land_l, lpiece, lland, gpiece_l, gather_l,
    load_sem, store_sem, meta_sem, relay_sem, send_sem, recv_sem,
):
    sub = 8 // plane
    node_rows = nf_ref.shape[0]
    blocks = node_rows // 128
    peers = 2 + reps
    loop_size = plane * depth
    loop_at, rep_at = lax.axis_index("loop"), lax.axis_index("rep")
    z_at, g_at = loop_at // plane, lax.rem(loop_at, plane)
    team = reps * plane
    team_at = rep_at * plane + g_at
    loop_up = {"loop": lax.rem(loop_at + 1, loop_size), "rep": rep_at}
    loop_down = {"loop": lax.rem(loop_at + loop_size - 1, loop_size), "rep": rep_at}

    def mate(step):
        other = lax.rem(team_at + step, team)
        r_to, g_to = other // plane, lax.rem(other, plane)
        return other, {"loop": z_at * plane + g_to, "rep": r_to}

    def above(step):
        z_to = lax.rem(z_at + step, depth)
        return z_to, {"loop": z_to * plane + g_at, "rep": rep_at}

    near = max(1, depth // 4)
    near_steps = sorted({side for k in range(1, near + 1) for side in (k, depth - k)})
    relay_steps = sorted({near, depth - near})
    parity = lax.rem(z_at, 2)
    z_pair = z_at + 1 - 2 * parity

    def twin(step):
        other = lax.rem(parity * plane + g_at + step, 2 * plane)
        z_to, g_to = z_at - parity + other // plane, lax.rem(other, plane)
        return {"loop": z_to * plane + g_to, "rep": rep_at}

    def send(source, target, sem, device):
        remote(source, target, send_sem.at[sem], recv_sem.at[sem], device)

    def to_team(stage, land, sem):
        land[team_at] = stage[team_at]

        @pl.loop(1, team)
        def _(step):
            other, device = mate(step)
            send(stage.at[other], land.at[team_at], sem, device)

    def to_plane(piece, gather, sem):
        gather[g_at] = piece[...]

        @pl.loop(1, plane)
        def _(step):
            g_to = lax.rem(g_at + step, plane)
            send(piece, gather.at[g_at], sem, {"loop": z_at * plane + g_to, "rep": rep_at})

    def arrived(land, sem):
        if land.shape[0] > 1:
            copy_all(land.at[1:], recv_sem.at[sem]).wait()

    def added(land, count):
        total = land[0].astype(F32)
        return lax.fori_loop(1, count, lambda slot, total: total + land[slot].astype(F32), total)

    loads = [
        pltpu.make_async_copy(source, target, load_sem.at[i])
        for i, (source, target) in enumerate(
            (
                (nf_hbm, nf_ref), (wm_hbm, wm_ref), (adj_hbm, adj_ref),
                (wi_hbm, wi_ref), (wo_hbm, wo_ref), (cot_hbm, cot_ref),
            )
        )
    ]
    for load in loads:
        load.start()
    stores = [
        pltpu.make_async_copy(source, target, store_sem.at[i])
        for i, (source, target) in enumerate(
            (
                (out_new, new_hbm), (out_grad, grad_hbm), (out_mw, mw_hbm), (out_iw, iw_hbm),
                (out_bias, grad_bias_hbm), (out_ow, ow_hbm), (out_gain, grad_gain_hbm),
            )
        )
    ]

    greet(loop_up)
    greet(loop_down)
    for step in near_steps:
        greet(above(step)[1])

    @pl.loop(1, team)
    def _(step):
        greet(mate(step)[1])

    flat[...] = jnp.zeros(flat.shape, jnp.int32)
    flat[0:2, 0:24] = index_ref[...]
    for k in range(peers):
        flat[8 + k : 9 + k, :] = rows_ref[k]
    turned = jnp.transpose(flat[...])
    lane_rows = lax.broadcasted_iota(jnp.int32, (128, node_rows), 1)
    sub_rows = lax.broadcasted_iota(jnp.int32, (128, node_rows), 0)
    loads[0].wait()

    for k in range(peers):
        live = (lane_rows == turned[:, 8 + k : 9 + k]) & (sub_rows < kept_ref[0, k])
        picker = jnp.where(live, 1.0, 0.0).astype(BF16)
        hout[k] = dot(picker, nf_ref[...]).astype(BF16)

    pl.semaphore_wait(pltpu.get_barrier_semaphore(), team - 1 + 2 + len(near_steps))
    send(hout.at[0], hin.at[0], 8, loop_up)
    send(hout.at[1], hin.at[1], 8, loop_down)
    for step in range(1, reps):
        r_to = lax.rem(rep_at + step, reps)
        send(hout.at[2 + r_to], hin.at[2 + rep_at], 8, {"loop": loop_at, "rep": r_to})
    hin[2 + rep_at] = hout[2 + rep_at]

    for step in relay_steps:
        pl.semaphore_signal(relay_sem, inc=1, device_id=above(step)[1], device_id_type=MESH)

    loads[1].wait()
    message, _ = silu_and_slope(dot(nf_ref[...], wm_ref[...]))
    table[0:blocks] = message.reshape(blocks, 128, 256)

    live_total = count_ref[0, 0]
    slot_col = lax.broadcasted_iota(jnp.int32, (32, 1), 0)
    slot_row = lax.broadcasted_iota(jnp.int32, (1, 128), 1)
    dest_col, source_col = turned[0:32, 0:1], turned[0:32, 1:2]
    dest_row, source_row = flat[0:1, :], flat[1:2, :]

    def keyed(value, iota):
        return jnp.where(iota < live_total, value, 64)

    def halo_first(value):
        return jnp.where(value >= blocks, value - blocks, value + peers)

    forward = slot_order(keyed(dest_col, slot_col), keyed(dest_row, slot_row), (source_col,))
    backward = slot_order(
        keyed(halo_first(source_col), slot_col), keyed(halo_first(source_row), slot_row), (dest_col,)
    )
    meta_v[...] = jnp.concatenate(forward + backward, axis=0)
    meta_copy = pltpu.make_async_copy(meta_v, meta_s, meta_sem)
    meta_copy.start()

    row_at = lax.broadcasted_iota(jnp.int32, (node_rows, 128), 0)
    lane_at = lax.broadcasted_iota(jnp.int32, (node_rows, 128), 1)
    for k in range(peers):
        live = (row_at == rows_ref[k]) & (lane_at < kept_ref[0, k])
        spread[:, 128 * k : 128 * k + 128] = jnp.where(live, 1.0, 0.0).astype(BF16)

    meta_copy.wait()
    for load in loads[2:]:
        load.wait()
    arrived(hin, 8)
    half_peers = peers // 2
    for first in range(0, peers, half_peers):
        some = slice(first, first + half_peers)
        message, gate = silu_and_slope(dot(hin[some].reshape(half_peers * 128, 256), wm_ref[...]))
        table[blocks + first : blocks + first + half_peers] = message.reshape(half_peers, 128, 256)
        halo_slope[some] = gate.reshape(half_peers, 128, 256)


    def forward_slots(c, total):
        for lap in range(4):
            i = c * 4 + lap
            product = dot(adj_ref[meta_s[0, i]], table[meta_s[1, i]])
            total = product + total * meta_s[2, i].astype(F32)
            run[i] = total
        return total

    lax.fori_loop(0, 6, forward_slots, jnp.zeros((128, 256), F32), unroll=6)


    def node_update(c, gain_sum):
        at = pl.ds(pl.multiple_of(c * 256, 256), 256)
        gathered = jnp.concatenate(
            [run[meta_s[3, 2 * c]], run[meta_s[3, 2 * c + 1]]], axis=0
        ).astype(BF16)
        agg[at, :] = gathered
        pre = dot(nf_ref[at, :], wi_ref[0:256, :]) + bias_ref[...]
        hid, hid_slope = silu_and_slope(pre + dot(gathered, wi_ref[256:512, :]))
        hidden[at, :] = hid
        outer = dot(hid, wo_ref[...])
        centered = outer - row_mean(outer)
        inv_std = lax.rsqrt(row_mean(centered * centered) + norm_eps)
        normed = centered * inv_std
        norm_rows[at, :] = normed
        upstream = cot_ref[at, :].astype(F32)
        gained = upstream * gain_ref[...]
        back = ((gained - row_mean(gained) - normed * row_mean(gained * normed)) * inv_std).astype(BF16)
        outer_grad[at, :] = back
        pre_grad[at, :] = (dot_right_t(back, wo_ref[...]) * hid_slope).astype(BF16)
        return gain_sum + jnp.sum(upstream * normed, axis=0, keepdims=True)

    gain_sum = lax.fori_loop(
        0, node_rows // 256, node_update, jnp.zeros((1, 256), F32), unroll=2
    )

    def deal(stage, first, tall, value):
        for rep in range(reps):
            for tile in range(8):
                start, half = (64 * rep + 16 * (tile // 2)) * tall, 128 * (tile % 2)
                slot, place = rep * plane + tile // sub, stage.shape[1] // sub * (tile % sub)
                stage[slot, place + first : place + first + 16 * tall, :] = value[
                    start : start + 16 * tall, half : half + 128
                ].astype(BF16)

    deal(stage_e, 0, 1, inner_rows(hidden[...], outer_grad[...]))
    back_all = pre_grad[...]
    bias_sum = dot(jnp.ones((16, node_rows), BF16), back_all)[0:1]
    deal(
        stage_e, 16, 2,
        jnp.concatenate([inner_rows(nf_ref[...], back_all), inner_rows(agg[...], back_all)], axis=0),
    )
    low_lane = lax.broadcasted_iota(jnp.int32, (1, 128), 1) < 64
    for rep in range(reps):
        at = slice(128 * (rep // 2), 128 * (rep // 2) + 128)
        left, right = bias_sum[:, at], gain_sum[:, at]
        if rep % 2:
            left = pltpu.roll(left, 64, 1)
        else:
            right = pltpu.roll(right, 64, 1)
        both = jnp.broadcast_to(jnp.where(low_lane, left, right), (16, 128)).astype(BF16)
        for g in range(plane):
            stage_e[rep * plane + g, 48:64, :] = both

    to_team(stage_e, land_e, 0)

    @pl.loop(0, node_rows // 256, unroll=2)
    def _(c):
        at = pl.ds(pl.multiple_of(c * 256, 256), 256)
        back = dot_right_t(pre_grad[at, :], wi_ref[256:512, :])
        agg_grad[pl.ds(2 * c, 2)] = back.astype(BF16).reshape(2, 128, 256)

    def backward_slots(c, total):
        for lap in range(4):
            i = c * 4 + lap
            product = inner_rows(adj_ref[meta_s[4, i]], agg_grad[meta_s[5, i]])
            total = product + total * meta_s[6, i].astype(F32)
            run[i] = total
        return total

    lax.fori_loop(0, 6, backward_slots, jnp.zeros((128, 256), F32), unroll=6)

    for k in range(peers):
        halo_grad[k] = (run[meta_s[7, k]] * halo_slope[k]).astype(BF16)
    @pl.loop(0, blocks, unroll=4)
    def _(b):
        at = pl.ds(pl.multiple_of(b * 128, 128), 128)
        _, own_slope = silu_and_slope(dot(nf_ref[at, :], wm_ref[...]))
        own_grad[at, :] = (run[meta_s[7, peers + b]] * own_slope).astype(BF16)

    message_grad = inner_rows(nf_ref[...], own_grad[...])
    message_grad += inner_rows(hin[...].reshape(peers * 128, 256), halo_grad[...].reshape(peers * 128, 256))
    deal(stage_l, 0, 1, message_grad)
    to_team(stage_l, land_l, 2)

    arrived(land_e, 0)
    total = added(land_e, team)
    vec_rows = jnp.broadcast_to(total[48:49], (8, 128))
    total = jnp.concatenate([total[64 * tile : 64 * tile + 48] for tile in range(sub)], axis=0)
    rows = 24 * sub
    for part in range(2):
        psend[part, 0:rows, :] = total[part * rows : (part + 1) * rows]
        psend[part, rows:, :] = vec_rows
    send(psend.at[1 - parity], pland, 3, {"loop": z_pair * plane + g_at, "rep": rep_at})

    arrived(land_l, 2)
    lpiece[...] = added(land_l, team).astype(BF16)
    lland[z_at] = lpiece[...]

    pl.semaphore_wait(relay_sem, len(relay_steps))

    @pl.loop(1, depth)
    def _(step):
        send(lpiece, lland.at[z_at], 5, above(step)[1])

    halo_back = halo_grad[...].reshape(peers * 128, 256)
    rout[...] = dot_right_t(halo_back, wm_ref[...]).astype(BF16).reshape(peers, 128, 256)

    rin[2 + rep_at] = rout[2 + rep_at]
    send(rout.at[0], rin.at[0], 1, loop_down)
    send(rout.at[1], rin.at[1], 1, loop_up)
    for step in range(1, reps):
        r_to = lax.rem(rep_at + step, reps)
        send(rout.at[2 + r_to], rin.at[2 + rep_at], 1, {"loop": loop_at, "rep": r_to})

    copy_all(pland, recv_sem.at[3]).wait()
    total = psend[parity] + pland[...]
    filler = jnp.zeros((epiece.shape[0] - total.shape[0], 128), F32)
    epiece[...] = (jnp.concatenate([total, filler], axis=0) if filler.shape[0] else total).astype(BF16)
    eland[z_at // 2] = epiece[...]

    @pl.loop(1, depth // 2)
    def _(step):
        send(epiece, eland.at[z_at // 2], 4, above(2 * step)[1])

    arrived(rin, 1)
    returned = rin[...].reshape(peers * 128, 256)

    @pl.loop(0, node_rows // 256, unroll=2)
    def _(c):
        at = pl.ds(pl.multiple_of(c * 256, 256), 256)
        out_new[at, :] = (nf_ref[at, :].astype(F32) + norm_rows[at, :] * gain_ref[...]).astype(BF16)
        total = cot_ref[at, :].astype(F32) + dot_right_t(pre_grad[at, :], wi_ref[0:256, :])
        total += dot_right_t(own_grad[at, :], wm_ref[...])
        out_grad[at, :] = (total + dot(spread[at, :], returned)).astype(BF16)

    stores[0].start()
    stores[1].start()

    arrived(lland, 5)
    gpiece_l[...] = (added(lland, depth) * scale).astype(BF16)
    to_plane(gpiece_l, gather_l, 6)

    arrived(eland, 4)
    total = added(eland, depth // 2) * scale
    vec_row = total[rows : rows + 1]
    half = out_bias.shape[1]
    out_bias[...] = vec_row[:, 0:half]
    out_gain[...] = pltpu.roll(vec_row, half, 1)[:, 0:half]
    stores[4].start()
    stores[6].start()
    gpiece_e[...] = total.astype(BF16)
    gather_e[parity * plane + g_at] = gpiece_e[...]

    @pl.loop(1, 2 * plane)
    def _(step):
        send(gpiece_e, gather_e.at[parity * plane + g_at], 7, twin(step))

    def collect(out, owned, first, tall):
        for tile in range(8):
            row, half = 16 * tall * (tile // 2), 128 * (tile % 2)
            block = owned[tile // sub]
            place = block.shape[0] // sub * (tile % sub) + first
            out[row : row + 16 * tall, half : half + 128] = block[place : place + 16 * tall]

    arrived(gather_l, 6)
    collect(out_mw, [gather_l[g].astype(F32) for g in range(plane)], 0, 1)
    stores[2].start()
    arrived(gather_e, 7)
    owned = [
        jnp.concatenate([gather_e[part * plane + g].astype(F32)[0:rows] for part in range(2)], axis=0)
        for g in range(plane)
    ]
    collect(out_ow, owned, 0, 1)
    stores[5].start()
    collect(out_iw, owned, 16, 2)
    stores[3].start()

    for sem, land in ((0, land_e), (1, rin), (2, land_l), (4, eland), (5, lland), (6, gather_l), (7, gather_e), (8, hin)):
        if land.shape[0] > 1:
            copy_all(land.at[1:], send_sem.at[sem]).wait()
    copy_all(pland, send_sem.at[3]).wait()
    for store in stores:
        store.wait()


def finish_kernel(*refs):
    sources, targets, held, (load_sem, store_sem) = refs[:7], refs[7:14], refs[14:21], refs[21:]
    pieces = []
    for source, target, buffer in zip(sources, targets, held):
        step = min(256, source.shape[0])
        for first in range(0, source.shape[0], step):
            at = pl.ds(first, step)
            i = len(pieces)
            pieces.append(
                (
                    pltpu.make_async_copy(source.at[at], buffer.at[at], load_sem.at[i]),
                    pltpu.make_async_copy(buffer.at[at], target.at[at], store_sem.at[i]),
                )
            )
    for load, _ in pieces:
        load.start()
    for load, store in pieces:
        load.wait()
        store.start()
    for _, store in pieces:
        store.wait()


def shards(
    node_features,
    cotangent,
    adjacency,
    block_index,
    block_count,
    send_rows,
    row_counts,
    message_weight,
    input_weight,
    input_bias,
    output_weight,
    norm_gain,
):
    loop_size, reps = lax.axis_size("loop"), lax.axis_size("rep")
    plane, depth = plane_of(loop_size)
    sub = 8 // plane
    peers = 2 + reps
    node_rows, width = node_features.shape
    blocks = node_rows // 128
    slots = adjacency.shape[2]
    half_rows = -(-(24 * sub + 8) // 16) * 16
    scale = 1.0 / math.sqrt(node_rows * loop_size * reps)
    vmem, smem = pl.BlockSpec(memory_space=pltpu.VMEM), pl.BlockSpec(memory_space=pltpu.SMEM)
    hbm = pl.BlockSpec(memory_space=pltpu.HBM)
    shape = jax.ShapeDtypeStruct
    wide = (node_rows, width)
    mega = 1024 * 1024
    rows_in = send_rows.reshape(peers, 1, 128)
    small = pltpu.VMEM(wide, BF16)
    half = width // reps
    results = (
        shape(wide, BF16),
        shape(wide, BF16),
        shape((half, width), F32),
        shape((2 * half, width), F32),
        shape((1, half), F32),
        shape((half, width), F32),
        shape((1, half), F32),
    )
    outs = pl.pallas_call(
        functools.partial(layer_kernel, plane, depth, reps, scale),
        out_shape=results,
        in_specs=[hbm] * 6 + [vmem, smem, vmem, smem, vmem, vmem],
        out_specs=[hbm] * 7,
        scratch_shapes=[
            small,
            pltpu.VMEM((width, width), BF16),
            pltpu.VMEM((slots, 128, 128), BF16),
            pltpu.VMEM((2 * width, width), BF16),
            pltpu.VMEM((width, width), BF16),
            small,
            pltpu.VMEM((128, 128), jnp.int32),
            pltpu.VMEM((8, 128), jnp.int32),
            pltpu.SMEM((8, 128), jnp.int32),
            pltpu.VMEM((peers, 128, width), BF16),
            pltpu.VMEM((peers, 128, width), BF16),
            pltpu.VMEM((blocks + peers, 128, width), BF16),
            *(pltpu.VMEM(result.shape, result.dtype) for result in results),
            pltpu.VMEM((peers, 128, width), BF16),
            pltpu.VMEM((peers, 128, width), BF16),
            pltpu.VMEM((peers, 128, width), F32),
            pltpu.VMEM((node_rows, peers * 128), BF16),
            pltpu.VMEM((slots, 128, width), F32),
            small, small, small, small,
            pltpu.VMEM((blocks, 128, width), BF16),
            pltpu.VMEM(wide, F32),
            small,
            pltpu.VMEM((peers, 128, width), BF16),
            pltpu.VMEM((reps * plane, 64 * sub, 128), BF16),
            pltpu.VMEM((reps * plane, 64 * sub, 128), BF16),
            pltpu.VMEM((2, 24 * sub + 8, 128), F32),
            pltpu.VMEM((24 * sub + 8, 128), F32),
            pltpu.VMEM((half_rows, 128), BF16),
            pltpu.VMEM((depth // 2, half_rows, 128), BF16),
            pltpu.VMEM((half_rows, 128), BF16),
            pltpu.VMEM((2 * plane, half_rows, 128), BF16),
            pltpu.VMEM((reps * plane, 16 * sub, 128), BF16),
            pltpu.VMEM((reps * plane, 16 * sub, 128), BF16),
            pltpu.VMEM((16 * sub, 128), BF16),
            pltpu.VMEM((depth, 16 * sub, 128), BF16),
            pltpu.VMEM((16 * sub, 128), BF16),
            pltpu.VMEM((plane, 16 * sub, 128), BF16),
            pltpu.SemaphoreType.DMA((6,)),
            pltpu.SemaphoreType.DMA((7,)),
            pltpu.SemaphoreType.DMA,
            pltpu.SemaphoreType.REGULAR,
            pltpu.SemaphoreType.DMA((9,)),
            pltpu.SemaphoreType.DMA((9,)),
        ],
        compiler_params=pltpu.CompilerParams(
            collective_id=0, has_side_effects=True, vmem_limit_bytes=56 * mega
        ),
        name="message_layer",
    )(
        node_features,
        message_weight,
        adjacency[0, 0],
        input_weight,
        output_weight,
        cotangent,
        block_index[0, 0],
        block_count,
        send_rows.reshape(peers, 1, 128),
        row_counts[0],
        input_bias[None, :],
        norm_gain[None, :],
    )
    new_features, grad_features, grad_mw, grad_iw, grad_bias, grad_ow, grad_gain = pl.pallas_call(
        finish_kernel,
        out_shape=results,
        in_specs=[hbm] * 7,
        out_specs=[hbm] * 7,
        scratch_shapes=[
            *(pltpu.VMEM(result.shape, result.dtype) for result in results),
            pltpu.SemaphoreType.DMA((16,)),
            pltpu.SemaphoreType.DMA((16,)),
        ],
        compiler_params=pltpu.CompilerParams(has_side_effects=True, vmem_limit_bytes=56 * mega),
        name="write_results",
    )(*outs)
    return (
        new_features, grad_features, grad_mw, grad_iw,
        grad_bias.reshape(half), grad_ow, grad_gain.reshape(half),
    )


def solution(mesh):
    in_specs = (
        P(("loop", "rep"), None),
        P(("loop", "rep"), None),
        P("loop", "rep", None, None, None),
        P("loop", "rep", None, None),
        P("loop", "rep"),
        P("loop", "rep", None, None),
        P("loop", "rep", None),
        P(),
        P(),
        P(),
        P(),
        P(),
    )
    out_specs = (
        P(("loop", "rep"), None),
        P(("loop", "rep"), None),
        P("rep", None),
        P("rep", None),
        P("rep"),
        P("rep", None),
        P("rep"),
    )
    return jax.shard_map(shards, mesh=mesh, in_specs=in_specs, out_specs=out_specs, check_vma=False)
```

```python
import functools
import math

import jax
import jax.numpy as jnp
from jax import lax
from jax.experimental import pallas as pl
from jax.experimental.pallas import tpu as pltpu
from jax.sharding import PartitionSpec as P

norm_eps = 1e-05
MESH = pl.DeviceIdType.MESH
BF16, F32 = jnp.bfloat16, jnp.float32


def dot(left, right):
    return jnp.dot(left, right, preferred_element_type=F32)


def dot_right_t(left, right):
    return lax.dot_general(left, right, (((1,), (1,)), ((), ())), preferred_element_type=F32)


def inner_rows(left, right):
    return lax.dot_general(left, right, (((0,), (0,)), ((), ())), preferred_element_type=F32)


def sigmoid(argument):
    return 0.5 * jnp.tanh(0.5 * argument) + 0.5


def row_mean(values):
    return jnp.sum(values, axis=-1, keepdims=True) * (1.0 / values.shape[-1])


def plane_of(loop_size):
    plane = 8 if loop_size % 8 == 0 and loop_size > 8 else 2
    return plane, loop_size // plane


def copy_all(buffer, sem):
    return pltpu.make_async_copy(buffer, buffer, sem)


def slot_order(key_col, key_row, cols):
    shape = (32, 128)
    slot = lax.broadcasted_iota(jnp.int32, shape, 0)
    lane = lax.broadcasted_iota(jnp.int32, shape, 1)
    ahead = (key_row < key_col) | ((key_row == key_col) & (lane < slot))
    rank = jnp.sum(jnp.where(ahead & (lane < 24), 1, 0), axis=1, keepdims=True)
    placed = (rank == lane) & (slot < 24)
    rows = [
        jnp.sum(jnp.where(placed, col, 0), axis=0, keepdims=True) for col in (slot, *cols, key_col)
    ]
    before = pltpu.roll(rows[-1], 1, 1)
    keep = jnp.where((rows[-1] == before) & (lane[:1] > 0), 1, 0)
    last = jnp.sum(jnp.where((key_col <= lane) & (slot < 24), 1, 0), axis=0, keepdims=True) - 1
    last = jnp.maximum(last, 0)
    return [*rows[:-1], keep, last]


def silu_and_slope(pre):
    gate = sigmoid(pre)
    value = pre * gate
    return value.astype(BF16), gate + value * (1.0 - gate)


def remote(source, target, send_sem, recv_sem, device):
    pltpu.make_async_remote_copy(
        source, target, send_sem, recv_sem, device_id=device, device_id_type=MESH
    ).start()


def greet(device):
    pl.semaphore_signal(pltpu.get_barrier_semaphore(), inc=1, device_id=device, device_id_type=MESH)


def layer_kernel(
    plane, depth, reps, scale,
    nf_hbm, wm_hbm, adj_hbm, wi_hbm, wo_hbm, cot_hbm,
    index_ref, count_ref, rows_ref, kept_ref, bias_ref, gain_ref,
    new_hbm, grad_hbm, mw_hbm, iw_hbm, grad_bias_hbm, ow_hbm, grad_gain_hbm,
    nf_ref, wm_ref, adj_ref, wi_ref, wo_ref, cot_ref,
    flat, meta_v, meta_s, hout, hin, table,
    out_new, out_grad, out_mw, out_iw, out_bias, out_ow, out_gain,
    rout, rin, halo_slope, spread, run,
    agg, hidden, outer_grad, pre_grad, agg_grad, norm_rows, own_grad, halo_grad,
    stage_e, core_land, stage_p, land_e, epiece, eland, gpiece_e, gather_e,
    stage_l, land_l, lpiece, lland, gpiece_l, gather_l,
    load_sem, store_sem, meta_sem, relay_sem, pair_sem, send_sem, recv_sem,
):
    sub = 8 // plane
    node_rows = nf_ref.shape[0]
    blocks = node_rows // 128
    peers = 2 + reps
    loop_size = plane * depth
    loop_at, rep_at = lax.axis_index("loop"), lax.axis_index("rep")
    z_at, g_at = loop_at // plane, lax.rem(loop_at, plane)
    team = reps * plane
    team_at = rep_at * plane + g_at
    loop_up = {"loop": lax.rem(loop_at + 1, loop_size), "rep": rep_at}
    loop_down = {"loop": lax.rem(loop_at + loop_size - 1, loop_size), "rep": rep_at}

    def mate(step):
        other = lax.rem(team_at + step, team)
        r_to, g_to = other // plane, lax.rem(other, plane)
        return other, {"loop": z_at * plane + g_to, "rep": r_to}

    def above(step):
        z_to = lax.rem(z_at + step, depth)
        return z_to, {"loop": z_to * plane + g_at, "rep": rep_at}

    near = max(1, depth // 4)
    near_steps = sorted({side for k in range(1, near + 1) for side in (k, depth - k)})
    relay_steps = sorted({near, depth - near})
    parity = lax.rem(z_at, 2)
    z_pair = z_at + 1 - 2 * parity

    core = lax.rem(rep_at, 2)
    squad = reps * plane
    squad_at = ((rep_at // 2) * plane + g_at) * 2 + parity

    def comrade(step):
        other = lax.rem(squad_at + step, squad)
        z_to = z_at - parity + lax.rem(other, 2)
        g_to = lax.rem(other // 2, plane)
        return other, {"loop": z_to * plane + g_to, "rep": other // (2 * plane) * 2 + core}

    def twin(step):
        other = lax.rem(parity * plane + g_at + step, 2 * plane)
        z_to, g_to = z_at - parity + other // plane, lax.rem(other, plane)
        return {"loop": z_to * plane + g_to, "rep": rep_at}

    def send(source, target, sem, device):
        remote(source, target, send_sem.at[sem], recv_sem.at[sem], device)

    def to_team(stage, land, sem):
        land[team_at] = stage[team_at]

        @pl.loop(1, team)
        def _(step):
            other, device = mate(step)
            send(stage.at[other], land.at[team_at], sem, device)

    def to_plane(piece, gather, sem):
        gather[g_at] = piece[...]

        @pl.loop(1, plane)
        def _(step):
            g_to = lax.rem(g_at + step, plane)
            send(piece, gather.at[g_at], sem, {"loop": z_at * plane + g_to, "rep": rep_at})

    def arrived(land, sem):
        if land.shape[0] > 1:
            copy_all(land.at[1:], recv_sem.at[sem]).wait()

    def added(land, count):
        total = land[0].astype(F32)
        for slot in range(1, count):
            total = total + land[slot].astype(F32)
        return total

    loads = [
        pltpu.make_async_copy(source, target, load_sem.at[i])
        for i, (source, target) in enumerate(
            (
                (nf_hbm, nf_ref), (wm_hbm, wm_ref), (adj_hbm, adj_ref),
                (wi_hbm, wi_ref), (wo_hbm, wo_ref), (cot_hbm, cot_ref),
            )
        )
    ]
    for load in loads:
        load.start()
    stores = [
        pltpu.make_async_copy(source, target, store_sem.at[i])
        for i, (source, target) in enumerate(
            (
                (out_new, new_hbm), (out_grad, grad_hbm), (out_mw, mw_hbm), (out_iw, iw_hbm),
                (out_bias, grad_bias_hbm), (out_ow, ow_hbm), (out_gain, grad_gain_hbm),
            )
        )
    ]

    greet(loop_up)
    greet(loop_down)
    for step in near_steps:
        greet(above(step)[1])

    @pl.loop(1, team)
    def _(step):
        greet(mate(step)[1])

    flat[...] = jnp.zeros(flat.shape, jnp.int32)
    flat[0:2, 0:24] = index_ref[...]
    for k in range(peers):
        flat[8 + k : 9 + k, :] = rows_ref[k]
    turned = jnp.transpose(flat[...])
    lane_rows = lax.broadcasted_iota(jnp.int32, (128, node_rows), 1)
    sub_rows = lax.broadcasted_iota(jnp.int32, (128, node_rows), 0)
    loads[0].wait()

    for k in range(peers):
        live = (lane_rows == turned[:, 8 + k : 9 + k]) & (sub_rows < kept_ref[0, k])
        picker = jnp.where(live, 1.0, 0.0).astype(BF16)
        hout[k] = dot(picker, nf_ref[...]).astype(BF16)

    pl.semaphore_wait(pltpu.get_barrier_semaphore(), team - 1 + 2 + len(near_steps))
    send(hout.at[0], hin.at[0], 8, loop_up)
    send(hout.at[1], hin.at[1], 8, loop_down)
    for step in range(1, reps):
        r_to = lax.rem(rep_at + step, reps)
        send(hout.at[2 + r_to], hin.at[2 + rep_at], 8, {"loop": loop_at, "rep": r_to})
    hin[2 + rep_at] = hout[2 + rep_at]

    for step in relay_steps:
        pl.semaphore_signal(relay_sem, inc=1, device_id=above(step)[1], device_id_type=MESH)
    pl.semaphore_signal(
        pair_sem, inc=1, device_id={"loop": z_pair * plane + g_at, "rep": rep_at}, device_id_type=MESH
    )

    loads[1].wait()
    message, _ = silu_and_slope(dot(nf_ref[...], wm_ref[...]))
    table[0:blocks] = message.reshape(blocks, 128, 256)

    live_total = count_ref[0, 0]
    slot_col = lax.broadcasted_iota(jnp.int32, (32, 1), 0)
    slot_row = lax.broadcasted_iota(jnp.int32, (1, 128), 1)
    dest_col, source_col = turned[0:32, 0:1], turned[0:32, 1:2]
    dest_row, source_row = flat[0:1, :], flat[1:2, :]

    def keyed(value, iota):
        return jnp.where(iota < live_total, value, 64)

    def halo_first(value):
        return jnp.where(value >= blocks, value - blocks, value + peers)

    forward = slot_order(keyed(dest_col, slot_col), keyed(dest_row, slot_row), (source_col,))
    backward = slot_order(
        keyed(halo_first(source_col), slot_col), keyed(halo_first(source_row), slot_row), (dest_col,)
    )
    meta_v[...] = jnp.concatenate(forward + backward, axis=0)
    meta_copy = pltpu.make_async_copy(meta_v, meta_s, meta_sem)
    meta_copy.start()

    row_at = lax.broadcasted_iota(jnp.int32, (node_rows, 128), 0)
    lane_at = lax.broadcasted_iota(jnp.int32, (node_rows, 128), 1)
    for k in range(peers):
        live = (row_at == rows_ref[k]) & (lane_at < kept_ref[0, k])
        spread[:, 128 * k : 128 * k + 128] = jnp.where(live, 1.0, 0.0).astype(BF16)

    meta_copy.wait()
    for load in loads[2:]:
        load.wait()
    arrived(hin, 8)
    half_peers = peers // 2
    for first in range(0, peers, half_peers):
        some = slice(first, first + half_peers)
        message, gate = silu_and_slope(dot(hin[some].reshape(half_peers * 128, 256), wm_ref[...]))
        table[blocks + first : blocks + first + half_peers] = message.reshape(half_peers, 128, 256)
        halo_slope[some] = gate.reshape(half_peers, 128, 256)


    def forward_slots(c, total):
        for lap in range(4):
            i = c * 4 + lap
            product = dot(adj_ref[meta_s[0, i]], table[meta_s[1, i]])
            total = product + total * meta_s[2, i].astype(F32)
            run[i] = total
        return total

    lax.fori_loop(0, 6, forward_slots, jnp.zeros((128, 256), F32), unroll=6)


    def node_update(c, gain_sum):
        at = pl.ds(pl.multiple_of(c * 256, 256), 256)
        gathered = jnp.concatenate(
            [run[meta_s[3, 2 * c]], run[meta_s[3, 2 * c + 1]]], axis=0
        ).astype(BF16)
        agg[at, :] = gathered
        pre = dot(nf_ref[at, :], wi_ref[0:256, :]) + bias_ref[...]
        hid, hid_slope = silu_and_slope(pre + dot(gathered, wi_ref[256:512, :]))
        hidden[at, :] = hid
        outer = dot(hid, wo_ref[...])
        centered = outer - row_mean(outer)
        inv_std = lax.rsqrt(row_mean(centered * centered) + norm_eps)
        normed = centered * inv_std
        norm_rows[at, :] = normed
        upstream = cot_ref[at, :].astype(F32)
        gained = upstream * gain_ref[...]
        back = ((gained - row_mean(gained) - normed * row_mean(gained * normed)) * inv_std).astype(BF16)
        outer_grad[at, :] = back
        pre_grad[at, :] = (dot_right_t(back, wo_ref[...]) * hid_slope).astype(BF16)
        return gain_sum + jnp.sum(upstream * normed, axis=0, keepdims=True)

    gain_sum = lax.fori_loop(
        0, node_rows // 256, node_update, jnp.zeros((1, 256), F32), unroll=2
    )

    def deal(stage, first, tall, value):
        for rep in range(reps):
            for tile in range(8):
                start, half = (64 * rep + 16 * (tile // 2)) * tall, 128 * (tile % 2)
                slot, place = rep * plane + tile // sub, stage.shape[1] // sub * (tile % sub)
                stage[slot, place + first : place + first + 16 * tall, :] = value[
                    start : start + 16 * tall, half : half + 128
                ].astype(BF16)

    outer_weight = inner_rows(hidden[...], outer_grad[...])
    back_all = pre_grad[...]
    bias_sum = dot(jnp.ones((16, node_rows), BF16), back_all)[0:1]
    inner_weight = jnp.concatenate(
        [inner_rows(nf_ref[...], back_all), inner_rows(agg[...], back_all)], axis=0
    )
    low_lane = lax.broadcasted_iota(jnp.int32, (1, 128), 1) < 64
    rows = 24 * sub
    for rep in range(reps):
        at = slice(128 * (rep // 2), 128 * (rep // 2) + 128)
        left, right = bias_sum[:, at], gain_sum[:, at]
        if rep % 2:
            left = pltpu.roll(left, 64, 1)
        else:
            right = pltpu.roll(right, 64, 1)
        both = jnp.broadcast_to(jnp.where(low_lane, left, right), (stage_e.shape[2] - rows, 128))
        for g in range(plane):
            tiles = []
            for tile in range(g * sub, (g + 1) * sub):
                row, half = 16 * (tile // 2), slice(128 * (tile % 2), 128 * (tile % 2) + 128)
                tiles.append(outer_weight[64 * rep + row : 64 * rep + row + 16, half])
                tiles.append(inner_weight[128 * rep + 2 * row : 128 * rep + 2 * row + 32, half])
            block = jnp.concatenate(tiles, axis=0)
            for part in range(2):
                slot = ((rep // 2) * plane + g) * 2 + part
                piece = jnp.concatenate([block[part * rows : (part + 1) * rows], both], axis=0)
                stage_e[rep % 2, slot] = piece.astype(BF16)
    send(stage_e.at[1 - core], core_land, 0, {"loop": loop_at, "rep": rep_at + 1 - 2 * core})

    @pl.loop(0, node_rows // 256, unroll=2)
    def _(c):
        at = pl.ds(pl.multiple_of(c * 256, 256), 256)
        back = dot_right_t(pre_grad[at, :], wi_ref[256:512, :])
        agg_grad[pl.ds(2 * c, 2)] = back.astype(BF16).reshape(2, 128, 256)

    def backward_slots(c, total):
        for lap in range(4):
            i = c * 4 + lap
            product = inner_rows(adj_ref[meta_s[4, i]], agg_grad[meta_s[5, i]])
            total = product + total * meta_s[6, i].astype(F32)
            run[i] = total
        return total

    lax.fori_loop(0, 6, backward_slots, jnp.zeros((128, 256), F32), unroll=6)

    copy_all(core_land, recv_sem.at[0]).wait()
    stage_p[...] = (stage_e[core].astype(F32) + core_land[...].astype(F32)).astype(BF16)
    land_e[squad_at] = stage_p[squad_at]
    pl.semaphore_wait(pair_sem, 1)

    @pl.loop(1, squad)
    def _(step):
        other, device = comrade(step)
        send(stage_p.at[other], land_e.at[squad_at], 3, device)


    for k in range(peers):
        halo_grad[k] = (run[meta_s[7, k]] * halo_slope[k]).astype(BF16)
    @pl.loop(0, blocks, unroll=4)
    def _(b):
        at = pl.ds(pl.multiple_of(b * 128, 128), 128)
        _, own_slope = silu_and_slope(dot(nf_ref[at, :], wm_ref[...]))
        own_grad[at, :] = (run[meta_s[7, peers + b]] * own_slope).astype(BF16)

    message_grad = inner_rows(nf_ref[...], own_grad[...])
    message_grad += inner_rows(hin[...].reshape(peers * 128, 256), halo_grad[...].reshape(peers * 128, 256))
    deal(stage_l, 0, 1, message_grad)
    to_team(stage_l, land_l, 2)

    arrived(land_e, 3)
    pl.semaphore_wait(relay_sem, len(relay_steps))
    epiece[...] = added(land_e, squad).astype(BF16)
    eland[z_at // 2] = epiece[...]

    @pl.loop(1, depth // 2)
    def _(step):
        send(epiece, eland.at[z_at // 2], 4, above(2 * step)[1])

    arrived(land_l, 2)
    lpiece[...] = added(land_l, team).astype(BF16)
    lland[z_at] = lpiece[...]

    @pl.loop(1, depth)
    def _(step):
        send(lpiece, lland.at[z_at], 5, above(step)[1])

    halo_back = halo_grad[...].reshape(peers * 128, 256)
    rout[...] = dot_right_t(halo_back, wm_ref[...]).astype(BF16).reshape(peers, 128, 256)

    rin[2 + rep_at] = rout[2 + rep_at]
    send(rout.at[0], rin.at[0], 1, loop_down)
    send(rout.at[1], rin.at[1], 1, loop_up)
    for step in range(1, reps):
        r_to = lax.rem(rep_at + step, reps)
        send(rout.at[2 + r_to], rin.at[2 + rep_at], 1, {"loop": loop_at, "rep": r_to})

    arrived(rin, 1)
    returned = rin[...].reshape(peers * 128, 256)

    @pl.loop(0, node_rows // 256, unroll=2)
    def _(c):
        at = pl.ds(pl.multiple_of(c * 256, 256), 256)
        out_new[at, :] = (nf_ref[at, :].astype(F32) + norm_rows[at, :] * gain_ref[...]).astype(BF16)
        total = cot_ref[at, :].astype(F32) + dot_right_t(pre_grad[at, :], wi_ref[0:256, :])
        total += dot_right_t(own_grad[at, :], wm_ref[...])
        out_grad[at, :] = (total + dot(spread[at, :], returned)).astype(BF16)

    stores[0].start()
    stores[1].start()

    arrived(lland, 5)
    gpiece_l[...] = (added(lland, depth) * scale).astype(BF16)
    to_plane(gpiece_l, gather_l, 6)

    arrived(eland, 4)
    total = added(eland, depth // 2) * scale
    vec_row = total[rows : rows + 1]
    half = out_bias.shape[1]
    out_bias[...] = vec_row[:, 0:half]
    out_gain[...] = pltpu.roll(vec_row, half, 1)[:, 0:half]
    stores[4].start()
    stores[6].start()
    gpiece_e[...] = total.astype(BF16)
    gather_e[parity * plane + g_at] = gpiece_e[...]

    @pl.loop(1, 2 * plane)
    def _(step):
        send(gpiece_e, gather_e.at[parity * plane + g_at], 7, twin(step))

    def collect(out, owned, first, tall):
        for tile in range(8):
            row, half = 16 * tall * (tile // 2), 128 * (tile % 2)
            block = owned[tile // sub]
            place = block.shape[0] // sub * (tile % sub) + first
            out[row : row + 16 * tall, half : half + 128] = block[place : place + 16 * tall]

    arrived(gather_l, 6)
    collect(out_mw, [gather_l[g].astype(F32) for g in range(plane)], 0, 1)
    stores[2].start()
    arrived(gather_e, 7)
    owned = [
        jnp.concatenate([gather_e[part * plane + g].astype(F32)[0:rows] for part in range(2)], axis=0)
        for g in range(plane)
    ]
    collect(out_ow, owned, 0, 1)
    stores[5].start()
    collect(out_iw, owned, 16, 2)
    stores[3].start()

    for sem, land in ((1, rin), (2, land_l), (3, land_e), (4, eland), (5, lland), (6, gather_l), (7, gather_e), (8, hin)):
        if land.shape[0] > 1:
            copy_all(land.at[1:], send_sem.at[sem]).wait()
    copy_all(core_land, send_sem.at[0]).wait()
    for store in stores:
        store.wait()


def finish_kernel(*refs):
    sources, targets, held, (load_sem, store_sem) = refs[:7], refs[7:14], refs[14:21], refs[21:]
    pieces = []
    for source, target, buffer in zip(sources, targets, held):
        step = min(256, source.shape[0])
        for first in range(0, source.shape[0], step):
            at = pl.ds(first, step)
            i = len(pieces)
            pieces.append(
                (
                    pltpu.make_async_copy(source.at[at], buffer.at[at], load_sem.at[i]),
                    pltpu.make_async_copy(buffer.at[at], target.at[at], store_sem.at[i]),
                )
            )
    for load, _ in pieces:
        load.start()
    for load, store in pieces:
        load.wait()
        store.start()
    for _, store in pieces:
        store.wait()


def shards(
    node_features,
    cotangent,
    adjacency,
    block_index,
    block_count,
    send_rows,
    row_counts,
    message_weight,
    input_weight,
    input_bias,
    output_weight,
    norm_gain,
):
    loop_size, reps = lax.axis_size("loop"), lax.axis_size("rep")
    plane, depth = plane_of(loop_size)
    sub = 8 // plane
    peers = 2 + reps
    node_rows, width = node_features.shape
    blocks = node_rows // 128
    slots = adjacency.shape[2]
    half_rows = -(-(24 * sub + 8) // 16) * 16
    scale = 1.0 / math.sqrt(node_rows * loop_size * reps)
    vmem, smem = pl.BlockSpec(memory_space=pltpu.VMEM), pl.BlockSpec(memory_space=pltpu.SMEM)
    hbm = pl.BlockSpec(memory_space=pltpu.HBM)
    shape = jax.ShapeDtypeStruct
    wide = (node_rows, width)
    mega = 1024 * 1024
    rows_in = send_rows.reshape(peers, 1, 128)
    small = pltpu.VMEM(wide, BF16)
    half = width // reps
    results = (
        shape(wide, BF16),
        shape(wide, BF16),
        shape((half, width), F32),
        shape((2 * half, width), F32),
        shape((1, half), F32),
        shape((half, width), F32),
        shape((1, half), F32),
    )
    outs = pl.pallas_call(
        functools.partial(layer_kernel, plane, depth, reps, scale),
        out_shape=results,
        in_specs=[hbm] * 6 + [vmem, smem, vmem, smem, vmem, vmem],
        out_specs=[hbm] * 7,
        scratch_shapes=[
            small,
            pltpu.VMEM((width, width), BF16),
            pltpu.VMEM((slots, 128, 128), BF16),
            pltpu.VMEM((2 * width, width), BF16),
            pltpu.VMEM((width, width), BF16),
            small,
            pltpu.VMEM((128, 128), jnp.int32),
            pltpu.VMEM((8, 128), jnp.int32),
            pltpu.SMEM((8, 128), jnp.int32),
            pltpu.VMEM((peers, 128, width), BF16),
            pltpu.VMEM((peers, 128, width), BF16),
            pltpu.VMEM((blocks + peers, 128, width), BF16),
            *(pltpu.VMEM(result.shape, result.dtype) for result in results),
            pltpu.VMEM((peers, 128, width), BF16),
            pltpu.VMEM((peers, 128, width), BF16),
            pltpu.VMEM((peers, 128, width), F32),
            pltpu.VMEM((node_rows, peers * 128), BF16),
            pltpu.VMEM((slots, 128, width), F32),
            small, small, small, small,
            pltpu.VMEM((blocks, 128, width), BF16),
            pltpu.VMEM(wide, F32),
            small,
            pltpu.VMEM((peers, 128, width), BF16),
            pltpu.VMEM((2, reps * plane, half_rows, 128), BF16),
            pltpu.VMEM((reps * plane, half_rows, 128), BF16),
            pltpu.VMEM((reps * plane, half_rows, 128), BF16),
            pltpu.VMEM((reps * plane, half_rows, 128), BF16),
            pltpu.VMEM((half_rows, 128), BF16),
            pltpu.VMEM((depth // 2, half_rows, 128), BF16),
            pltpu.VMEM((half_rows, 128), BF16),
            pltpu.VMEM((2 * plane, half_rows, 128), BF16),
            pltpu.VMEM((reps * plane, 16 * sub, 128), BF16),
            pltpu.VMEM((reps * plane, 16 * sub, 128), BF16),
            pltpu.VMEM((16 * sub, 128), BF16),
            pltpu.VMEM((depth, 16 * sub, 128), BF16),
            pltpu.VMEM((16 * sub, 128), BF16),
            pltpu.VMEM((plane, 16 * sub, 128), BF16),
            pltpu.SemaphoreType.DMA((6,)),
            pltpu.SemaphoreType.DMA((7,)),
            pltpu.SemaphoreType.DMA,
            pltpu.SemaphoreType.REGULAR,
            pltpu.SemaphoreType.REGULAR,
            pltpu.SemaphoreType.DMA((9,)),
            pltpu.SemaphoreType.DMA((9,)),
        ],
        compiler_params=pltpu.CompilerParams(
            collective_id=0, has_side_effects=True, vmem_limit_bytes=56 * mega
        ),
        name="message_layer",
    )(
        node_features,
        message_weight,
        adjacency[0, 0],
        input_weight,
        output_weight,
        cotangent,
        block_index[0, 0],
        block_count,
        send_rows.reshape(peers, 1, 128),
        row_counts[0],
        input_bias[None, :],
        norm_gain[None, :],
    )
    new_features, grad_features, grad_mw, grad_iw, grad_bias, grad_ow, grad_gain = pl.pallas_call(
        finish_kernel,
        out_shape=results,
        in_specs=[hbm] * 7,
        out_specs=[hbm] * 7,
        scratch_shapes=[
            *(pltpu.VMEM(result.shape, result.dtype) for result in results),
            pltpu.SemaphoreType.DMA((16,)),
            pltpu.SemaphoreType.DMA((16,)),
        ],
        compiler_params=pltpu.CompilerParams(has_side_effects=True, vmem_limit_bytes=56 * mega),
        name="write_results",
    )(*outs)
    return (
        new_features, grad_features, grad_mw, grad_iw,
        grad_bias.reshape(half), grad_ow, grad_gain.reshape(half),
    )


def solution(mesh):
    in_specs = (
        P(("loop", "rep"), None),
        P(("loop", "rep"), None),
        P("loop", "rep", None, None, None),
        P("loop", "rep", None, None),
        P("loop", "rep"),
        P("loop", "rep", None, None),
        P("loop", "rep", None),
        P(),
        P(),
        P(),
        P(),
        P(),
    )
    out_specs = (
        P(("loop", "rep"), None),
        P(("loop", "rep"), None),
        P("rep", None),
        P("rep", None),
        P("rep"),
        P("rep", None),
        P("rep"),
    )
    return jax.shard_map(shards, mesh=mesh, in_specs=in_specs, out_specs=out_specs, check_vma=False)
```

```python
import functools
import math

import jax
import jax.numpy as jnp
from jax import lax
from jax.experimental import pallas as pl
from jax.experimental.pallas import tpu as pltpu
from jax.sharding import PartitionSpec as P

norm_eps = 1e-05
MESH = pl.DeviceIdType.MESH
BF16, F32 = jnp.bfloat16, jnp.float32


def dot(left, right):
    return jnp.dot(left, right, preferred_element_type=F32)


def dot_right_t(left, right):
    return lax.dot_general(left, right, (((1,), (1,)), ((), ())), preferred_element_type=F32)


def inner_rows(left, right):
    return lax.dot_general(left, right, (((0,), (0,)), ((), ())), preferred_element_type=F32)


def sigmoid(argument):
    return 0.5 * jnp.tanh(0.5 * argument) + 0.5


def row_mean(values):
    return jnp.sum(values, axis=-1, keepdims=True) * (1.0 / values.shape[-1])


def plane_of(loop_size):
    plane = 8 if loop_size % 8 == 0 and loop_size > 8 else 2
    return plane, loop_size // plane


def copy_all(buffer, sem):
    return pltpu.make_async_copy(buffer, buffer, sem)


def slot_order(key_col, key_row, cols):
    shape = (32, 128)
    slot = lax.broadcasted_iota(jnp.int32, shape, 0)
    lane = lax.broadcasted_iota(jnp.int32, shape, 1)
    ahead = (key_row < key_col) | ((key_row == key_col) & (lane < slot))
    rank = jnp.sum(jnp.where(ahead & (lane < 24), 1, 0), axis=1, keepdims=True)
    placed = (rank == lane) & (slot < 24)
    rows = [
        jnp.sum(jnp.where(placed, col, 0), axis=0, keepdims=True) for col in (slot, *cols, key_col)
    ]
    before = pltpu.roll(rows[-1], 1, 1)
    keep = jnp.where((rows[-1] == before) & (lane[:1] > 0), 1, 0)
    last = jnp.sum(jnp.where((key_col <= lane) & (slot < 24), 1, 0), axis=0, keepdims=True) - 1
    last = jnp.maximum(last, 0)
    return [*rows[:-1], keep, last]


def silu_and_slope(pre):
    gate = sigmoid(pre)
    value = pre * gate
    return value.astype(BF16), gate + value * (1.0 - gate)


def remote(source, target, send_sem, recv_sem, device):
    pltpu.make_async_remote_copy(
        source, target, send_sem, recv_sem, device_id=device, device_id_type=MESH
    ).start()


def greet(device):
    pl.semaphore_signal(pltpu.get_barrier_semaphore(), inc=1, device_id=device, device_id_type=MESH)


def layer_kernel(
    plane, depth, reps, scale,
    nf_hbm, wm_hbm, adj_hbm, wi_hbm, wo_hbm, cot_hbm,
    index_ref, count_ref, rows_ref, kept_ref, bias_ref, gain_ref,
    new_hbm, grad_hbm, mw_hbm, iw_hbm, grad_bias_hbm, ow_hbm, grad_gain_hbm,
    nf_ref, wm_ref, adj_ref, wi_ref, wo_ref, cot_ref,
    flat, meta_v, meta_s, hout, hin, table,
    out_new, out_grad, out_mw, out_iw, out_bias, out_ow, out_gain,
    rout, rin, halo_slope, spread, run,
    agg, hidden, outer_grad, pre_grad, agg_grad, norm_rows, own_grad, halo_grad,
    stage_e, core_land, stage_p, land_e, epiece, eland, gpiece_e, gather_e,
    stage_l, land_l, lpiece, lland, gpiece_l, gather_l,
    load_sem, store_sem, meta_sem, relay_sem, pair_sem, send_sem, recv_sem,
):
    sub = 8 // plane
    node_rows = nf_ref.shape[0]
    blocks = node_rows // 128
    peers = 2 + reps
    loop_size = plane * depth
    loop_at, rep_at = lax.axis_index("loop"), lax.axis_index("rep")
    z_at, g_at = loop_at // plane, lax.rem(loop_at, plane)
    team = reps * plane
    team_at = rep_at * plane + g_at
    loop_up = {"loop": lax.rem(loop_at + 1, loop_size), "rep": rep_at}
    loop_down = {"loop": lax.rem(loop_at + loop_size - 1, loop_size), "rep": rep_at}

    def mate(step):
        other = lax.rem(team_at + step, team)
        r_to, g_to = other // plane, lax.rem(other, plane)
        return other, {"loop": z_at * plane + g_to, "rep": r_to}

    def above(step):
        z_to = lax.rem(z_at + step, depth)
        return z_to, {"loop": z_to * plane + g_at, "rep": rep_at}

    near = max(1, depth // 4)
    near_steps = sorted({side for k in range(1, near + 1) for side in (k, depth - k)})
    relay_steps = sorted({near, depth - near})
    parity = lax.rem(z_at, 2)
    z_pair = z_at + 1 - 2 * parity

    core = lax.rem(rep_at, 2)
    squad = reps * plane
    squad_at = ((rep_at // 2) * plane + g_at) * 2 + parity

    def comrade(step):
        other = lax.rem(squad_at + step, squad)
        z_to = z_at - parity + lax.rem(other, 2)
        g_to = lax.rem(other // 2, plane)
        return other, {"loop": z_to * plane + g_to, "rep": other // (2 * plane) * 2 + core}

    def twin(step):
        other = lax.rem(parity * plane + g_at + step, 2 * plane)
        z_to, g_to = z_at - parity + other // plane, lax.rem(other, plane)
        return {"loop": z_to * plane + g_to, "rep": rep_at}

    def send(source, target, sem, device):
        remote(source, target, send_sem.at[sem], recv_sem.at[sem], device)

    def to_team(stage, land, sem):
        land[team_at] = stage[team_at]

        @pl.loop(1, team)
        def _(step):
            other, device = mate(step)
            send(stage.at[other], land.at[team_at], sem, device)

    def to_plane(piece, gather, sem):
        gather[g_at] = piece[...]

        @pl.loop(1, plane)
        def _(step):
            g_to = lax.rem(g_at + step, plane)
            send(piece, gather.at[g_at], sem, {"loop": z_at * plane + g_to, "rep": rep_at})

    def arrived(land, sem):
        if land.shape[0] > 1:
            copy_all(land.at[1:], recv_sem.at[sem]).wait()

    def added(land, count):
        total = land[0].astype(F32)
        for slot in range(1, count):
            total = total + land[slot].astype(F32)
        return total

    loads = [
        pltpu.make_async_copy(source, target, load_sem.at[i])
        for i, (source, target) in enumerate(
            (
                (nf_hbm, nf_ref), (wm_hbm, wm_ref), (adj_hbm, adj_ref),
                (wi_hbm, wi_ref), (wo_hbm, wo_ref), (cot_hbm, cot_ref),
            )
        )
    ]
    for load in loads:
        load.start()
    stores = [
        pltpu.make_async_copy(source, target, store_sem.at[i])
        for i, (source, target) in enumerate(
            (
                (out_new, new_hbm), (out_grad, grad_hbm), (out_mw, mw_hbm), (out_iw, iw_hbm),
                (out_bias, grad_bias_hbm), (out_ow, ow_hbm), (out_gain, grad_gain_hbm),
            )
        )
    ]

    greet(loop_up)
    greet(loop_down)
    for step in near_steps:
        greet(above(step)[1])

    @pl.loop(1, team)
    def _(step):
        greet(mate(step)[1])

    flat[...] = jnp.zeros(flat.shape, jnp.int32)
    flat[0:2, 0:24] = index_ref[...]
    for k in range(peers):
        flat[8 + k : 9 + k, :] = rows_ref[k]
    turned = jnp.transpose(flat[...])
    lane_rows = lax.broadcasted_iota(jnp.int32, (128, node_rows), 1)
    sub_rows = lax.broadcasted_iota(jnp.int32, (128, node_rows), 0)
    loads[0].wait()

    for k in range(peers):
        live = (lane_rows == turned[:, 8 + k : 9 + k]) & (sub_rows < kept_ref[0, k])
        picker = jnp.where(live, 1.0, 0.0).astype(BF16)
        hout[k] = dot(picker, nf_ref[...]).astype(BF16)

    pl.semaphore_wait(pltpu.get_barrier_semaphore(), team - 1 + 2 + len(near_steps))
    send(hout.at[0], hin.at[0], 8, loop_up)
    send(hout.at[1], hin.at[1], 8, loop_down)
    for step in range(1, reps):
        r_to = lax.rem(rep_at + step, reps)
        send(hout.at[2 + r_to], hin.at[2 + rep_at], 8, {"loop": loop_at, "rep": r_to})
    hin[2 + rep_at] = hout[2 + rep_at]

    for step in relay_steps:
        pl.semaphore_signal(relay_sem, inc=1, device_id=above(step)[1], device_id_type=MESH)
    pl.semaphore_signal(
        pair_sem, inc=1, device_id={"loop": z_pair * plane + g_at, "rep": rep_at}, device_id_type=MESH
    )

    loads[1].wait()
    message, _ = silu_and_slope(dot(nf_ref[...], wm_ref[...]))
    table[0:blocks] = message.reshape(blocks, 128, 256)

    live_total = count_ref[0, 0]
    slot_col = lax.broadcasted_iota(jnp.int32, (32, 1), 0)
    slot_row = lax.broadcasted_iota(jnp.int32, (1, 128), 1)
    dest_col, source_col = turned[0:32, 0:1], turned[0:32, 1:2]
    dest_row, source_row = flat[0:1, :], flat[1:2, :]

    def keyed(value, iota):
        return jnp.where(iota < live_total, value, 64)

    def halo_first(value):
        return jnp.where(value >= blocks, value - blocks, value + peers)

    forward = slot_order(keyed(dest_col, slot_col), keyed(dest_row, slot_row), (source_col,))
    backward = slot_order(
        keyed(halo_first(source_col), slot_col), keyed(halo_first(source_row), slot_row), (dest_col,)
    )
    meta_v[...] = jnp.concatenate(forward + backward, axis=0)
    meta_copy = pltpu.make_async_copy(meta_v, meta_s, meta_sem)
    meta_copy.start()

    row_at = lax.broadcasted_iota(jnp.int32, (node_rows, 128), 0)
    lane_at = lax.broadcasted_iota(jnp.int32, (node_rows, 128), 1)
    for k in range(peers):
        live = (row_at == rows_ref[k]) & (lane_at < kept_ref[0, k])
        spread[:, 128 * k : 128 * k + 128] = jnp.where(live, 1.0, 0.0).astype(BF16)

    meta_copy.wait()
    for load in loads[2:]:
        load.wait()
    arrived(hin, 8)
    half_peers = peers // 2
    for first in range(0, peers, half_peers):
        some = slice(first, first + half_peers)
        message, gate = silu_and_slope(dot(hin[some].reshape(half_peers * 128, 256), wm_ref[...]))
        table[blocks + first : blocks + first + half_peers] = message.reshape(half_peers, 128, 256)
        halo_slope[some] = gate.reshape(half_peers, 128, 256)


    def forward_slots(c, total):
        for lap in range(4):
            i = c * 4 + lap
            product = dot(adj_ref[meta_s[0, i]], table[meta_s[1, i]])
            total = product + total * meta_s[2, i].astype(F32)
            run[i] = total
        return total

    lax.fori_loop(0, 6, forward_slots, jnp.zeros((128, 256), F32), unroll=6)


    def node_update(c, gain_sum):
        at = pl.ds(pl.multiple_of(c * 256, 256), 256)
        gathered = jnp.concatenate(
            [run[meta_s[3, 2 * c]], run[meta_s[3, 2 * c + 1]]], axis=0
        ).astype(BF16)
        agg[at, :] = gathered
        pre = dot(nf_ref[at, :], wi_ref[0:256, :]) + bias_ref[...]
        hid, hid_slope = silu_and_slope(pre + dot(gathered, wi_ref[256:512, :]))
        hidden[at, :] = hid
        outer = dot(hid, wo_ref[...])
        centered = outer - row_mean(outer)
        inv_std = lax.rsqrt(row_mean(centered * centered) + norm_eps)
        normed = centered * inv_std
        norm_rows[at, :] = normed
        upstream = cot_ref[at, :].astype(F32)
        gained = upstream * gain_ref[...]
        back = ((gained - row_mean(gained) - normed * row_mean(gained * normed)) * inv_std).astype(BF16)
        outer_grad[at, :] = back
        pre_grad[at, :] = (dot_right_t(back, wo_ref[...]) * hid_slope).astype(BF16)
        return gain_sum + jnp.sum(upstream * normed, axis=0, keepdims=True)

    gain_sum = lax.fori_loop(
        0, node_rows // 256, node_update, jnp.zeros((1, 256), F32), unroll=2
    )

    def deal(stage, first, tall, value):
        for rep in range(reps):
            for tile in range(8):
                start, half = (64 * rep + 16 * (tile // 2)) * tall, 128 * (tile % 2)
                slot, place = rep * plane + tile // sub, stage.shape[1] // sub * (tile % sub)
                stage[slot, place + first : place + first + 16 * tall, :] = value[
                    start : start + 16 * tall, half : half + 128
                ].astype(BF16)

    outer_weight = inner_rows(hidden[...], outer_grad[...])
    back_all = pre_grad[...]
    bias_sum = dot(jnp.ones((16, node_rows), BF16), back_all)[0:1]
    inner_weight = jnp.concatenate(
        [inner_rows(nf_ref[...], back_all), inner_rows(agg[...], back_all)], axis=0
    )
    low_lane = lax.broadcasted_iota(jnp.int32, (1, 128), 1) < 64
    rows = 24 * sub
    for rep in range(reps):
        at = slice(128 * (rep // 2), 128 * (rep // 2) + 128)
        left, right = bias_sum[:, at], gain_sum[:, at]
        if rep % 2:
            left = pltpu.roll(left, 64, 1)
        else:
            right = pltpu.roll(right, 64, 1)
        both = jnp.broadcast_to(jnp.where(low_lane, left, right), (stage_e.shape[2] - rows, 128))
        for g in range(plane):
            tiles = []
            for tile in range(g * sub, (g + 1) * sub):
                row, half = 16 * (tile // 2), slice(128 * (tile % 2), 128 * (tile % 2) + 128)
                tiles.append(outer_weight[64 * rep + row : 64 * rep + row + 16, half])
                tiles.append(inner_weight[128 * rep + 2 * row : 128 * rep + 2 * row + 32, half])
            block = jnp.concatenate(tiles, axis=0)
            for part in range(2):
                slot = ((rep // 2) * plane + g) * 2 + part
                piece = jnp.concatenate([block[part * rows : (part + 1) * rows], both], axis=0)
                stage_e[rep % 2, slot] = piece.astype(BF16)
    send(stage_e.at[1 - core], core_land, 0, {"loop": loop_at, "rep": rep_at + 1 - 2 * core})

    @pl.loop(0, node_rows // 256, unroll=2)
    def _(c):
        at = pl.ds(pl.multiple_of(c * 256, 256), 256)
        back = dot_right_t(pre_grad[at, :], wi_ref[256:512, :])
        agg_grad[pl.ds(2 * c, 2)] = back.astype(BF16).reshape(2, 128, 256)

    def backward_slots(c, total):
        for lap in range(4):
            i = c * 4 + lap
            product = inner_rows(adj_ref[meta_s[4, i]], agg_grad[meta_s[5, i]])
            total = product + total * meta_s[6, i].astype(F32)
            run[i] = total
        return total

    lax.fori_loop(0, 6, backward_slots, jnp.zeros((128, 256), F32), unroll=6)

    copy_all(core_land, recv_sem.at[0]).wait()
    stage_p[...] = (stage_e[core].astype(F32) + core_land[...].astype(F32)).astype(BF16)
    land_e[squad_at] = stage_p[squad_at]
    pl.semaphore_wait(pair_sem, 1)

    @pl.loop(1, squad)
    def _(step):
        other, device = comrade(step)
        send(stage_p.at[other], land_e.at[squad_at], 3, device)


    for k in range(peers):
        halo_grad[k] = (run[meta_s[7, k]] * halo_slope[k]).astype(BF16)
    @pl.loop(0, blocks, unroll=4)
    def _(b):
        at = pl.ds(pl.multiple_of(b * 128, 128), 128)
        _, own_slope = silu_and_slope(dot(nf_ref[at, :], wm_ref[...]))
        own_grad[at, :] = (run[meta_s[7, peers + b]] * own_slope).astype(BF16)

    message_grad = inner_rows(nf_ref[...], own_grad[...])
    message_grad += inner_rows(hin[...].reshape(peers * 128, 256), halo_grad[...].reshape(peers * 128, 256))
    deal(stage_l, 0, 1, message_grad)
    to_team(stage_l, land_l, 2)

    arrived(land_e, 3)
    pl.semaphore_wait(relay_sem, len(relay_steps))
    epiece[...] = added(land_e, squad).astype(BF16)
    eland[z_at // 2] = epiece[...]

    @pl.loop(1, depth // 2)
    def _(step):
        send(epiece, eland.at[z_at // 2], 4, above(2 * step)[1])

    arrived(land_l, 2)
    lpiece[...] = added(land_l, team).astype(BF16)
    lland[z_at] = lpiece[...]

    @pl.loop(1, depth)
    def _(step):
        send(lpiece, lland.at[z_at], 5, above(step)[1])

    halo_back = halo_grad[...].reshape(peers * 128, 256)
    rout[...] = dot_right_t(halo_back, wm_ref[...]).astype(BF16).reshape(peers, 128, 256)

    rin[2 + rep_at] = rout[2 + rep_at]
    send(rout.at[0], rin.at[0], 1, loop_down)
    send(rout.at[1], rin.at[1], 1, loop_up)
    for step in range(1, reps):
        r_to = lax.rem(rep_at + step, reps)
        send(rout.at[2 + r_to], rin.at[2 + rep_at], 1, {"loop": loop_at, "rep": r_to})

    @pl.loop(0, node_rows // 256, unroll=2)
    def _(c):
        at = pl.ds(pl.multiple_of(c * 256, 256), 256)
        out_new[at, :] = (nf_ref[at, :].astype(F32) + norm_rows[at, :] * gain_ref[...]).astype(BF16)
        total = cot_ref[at, :].astype(F32) + dot_right_t(pre_grad[at, :], wi_ref[0:256, :])
        norm_rows[at, :] = total + dot_right_t(own_grad[at, :], wm_ref[...])

    stores[0].start()

    arrived(eland, 4)
    total = added(eland, depth // 2) * scale
    vec_row = total[rows : rows + 1]
    half = out_bias.shape[1]
    out_bias[...] = vec_row[:, 0:half]
    out_gain[...] = pltpu.roll(vec_row, half, 1)[:, 0:half]
    stores[4].start()
    stores[6].start()
    gpiece_e[...] = total.astype(BF16)
    gather_e[parity * plane + g_at] = gpiece_e[...]

    @pl.loop(1, 2 * plane)
    def _(step):
        send(gpiece_e, gather_e.at[parity * plane + g_at], 7, twin(step))

    arrived(lland, 5)
    gpiece_l[...] = (added(lland, depth) * scale).astype(BF16)
    to_plane(gpiece_l, gather_l, 6)

    arrived(rin, 1)
    returned = rin[...].reshape(peers * 128, 256)

    @pl.loop(0, node_rows // 256, unroll=2)
    def _(c):
        at = pl.ds(pl.multiple_of(c * 256, 256), 256)
        out_grad[at, :] = (norm_rows[at, :] + dot(spread[at, :], returned)).astype(BF16)

    stores[1].start()

    def collect(out, owned, first, tall):
        for tile in range(8):
            row, half = 16 * tall * (tile // 2), 128 * (tile % 2)
            block = owned[tile // sub]
            place = block.shape[0] // sub * (tile % sub) + first
            out[row : row + 16 * tall, half : half + 128] = block[place : place + 16 * tall]

    arrived(gather_l, 6)
    collect(out_mw, [gather_l[g].astype(F32) for g in range(plane)], 0, 1)
    stores[2].start()
    arrived(gather_e, 7)
    owned = [
        jnp.concatenate([gather_e[part * plane + g].astype(F32)[0:rows] for part in range(2)], axis=0)
        for g in range(plane)
    ]
    collect(out_ow, owned, 0, 1)
    stores[5].start()
    collect(out_iw, owned, 16, 2)
    stores[3].start()

    for sem, land in ((1, rin), (2, land_l), (3, land_e), (4, eland), (5, lland), (6, gather_l), (7, gather_e), (8, hin)):
        if land.shape[0] > 1:
            copy_all(land.at[1:], send_sem.at[sem]).wait()
    copy_all(core_land, send_sem.at[0]).wait()
    for store in stores:
        store.wait()


def finish_kernel(*refs):
    sources, targets, held, (load_sem, store_sem) = refs[:7], refs[7:14], refs[14:21], refs[21:]
    pieces = []
    for source, target, buffer in zip(sources, targets, held):
        step = min(256, source.shape[0])
        for first in range(0, source.shape[0], step):
            at = pl.ds(first, step)
            i = len(pieces)
            pieces.append(
                (
                    pltpu.make_async_copy(source.at[at], buffer.at[at], load_sem.at[i]),
                    pltpu.make_async_copy(buffer.at[at], target.at[at], store_sem.at[i]),
                )
            )
    for load, _ in pieces:
        load.start()
    for load, store in pieces:
        load.wait()
        store.start()
    for _, store in pieces:
        store.wait()


def shards(
    node_features,
    cotangent,
    adjacency,
    block_index,
    block_count,
    send_rows,
    row_counts,
    message_weight,
    input_weight,
    input_bias,
    output_weight,
    norm_gain,
):
    loop_size, reps = lax.axis_size("loop"), lax.axis_size("rep")
    plane, depth = plane_of(loop_size)
    sub = 8 // plane
    peers = 2 + reps
    node_rows, width = node_features.shape
    blocks = node_rows // 128
    slots = adjacency.shape[2]
    half_rows = -(-(24 * sub + 8) // 16) * 16
    scale = 1.0 / math.sqrt(node_rows * loop_size * reps)
    vmem, smem = pl.BlockSpec(memory_space=pltpu.VMEM), pl.BlockSpec(memory_space=pltpu.SMEM)
    hbm = pl.BlockSpec(memory_space=pltpu.HBM)
    shape = jax.ShapeDtypeStruct
    wide = (node_rows, width)
    mega = 1024 * 1024
    rows_in = send_rows.reshape(peers, 1, 128)
    small = pltpu.VMEM(wide, BF16)
    half = width // reps
    results = (
        shape(wide, BF16),
        shape(wide, BF16),
        shape((half, width), F32),
        shape((2 * half, width), F32),
        shape((1, half), F32),
        shape((half, width), F32),
        shape((1, half), F32),
    )
    outs = pl.pallas_call(
        functools.partial(layer_kernel, plane, depth, reps, scale),
        out_shape=results,
        in_specs=[hbm] * 6 + [vmem, smem, vmem, smem, vmem, vmem],
        out_specs=[hbm] * 7,
        scratch_shapes=[
            small,
            pltpu.VMEM((width, width), BF16),
            pltpu.VMEM((slots, 128, 128), BF16),
            pltpu.VMEM((2 * width, width), BF16),
            pltpu.VMEM((width, width), BF16),
            small,
            pltpu.VMEM((128, 128), jnp.int32),
            pltpu.VMEM((8, 128), jnp.int32),
            pltpu.SMEM((8, 128), jnp.int32),
            pltpu.VMEM((peers, 128, width), BF16),
            pltpu.VMEM((peers, 128, width), BF16),
            pltpu.VMEM((blocks + peers, 128, width), BF16),
            *(pltpu.VMEM(result.shape, result.dtype) for result in results),
            pltpu.VMEM((peers, 128, width), BF16),
            pltpu.VMEM((peers, 128, width), BF16),
            pltpu.VMEM((peers, 128, width), F32),
            pltpu.VMEM((node_rows, peers * 128), BF16),
            pltpu.VMEM((slots, 128, width), F32),
            small, small, small, small,
            pltpu.VMEM((blocks, 128, width), BF16),
            pltpu.VMEM(wide, F32),
            small,
            pltpu.VMEM((peers, 128, width), BF16),
            pltpu.VMEM((2, reps * plane, half_rows, 128), BF16),
            pltpu.VMEM((reps * plane, half_rows, 128), BF16),
            pltpu.VMEM((reps * plane, half_rows, 128), BF16),
            pltpu.VMEM((reps * plane, half_rows, 128), BF16),
            pltpu.VMEM((half_rows, 128), BF16),
            pltpu.VMEM((depth // 2, half_rows, 128), BF16),
            pltpu.VMEM((half_rows, 128), BF16),
            pltpu.VMEM((2 * plane, half_rows, 128), BF16),
            pltpu.VMEM((reps * plane, 16 * sub, 128), BF16),
            pltpu.VMEM((reps * plane, 16 * sub, 128), BF16),
            pltpu.VMEM((16 * sub, 128), BF16),
            pltpu.VMEM((depth, 16 * sub, 128), BF16),
            pltpu.VMEM((16 * sub, 128), BF16),
            pltpu.VMEM((plane, 16 * sub, 128), BF16),
            pltpu.SemaphoreType.DMA((6,)),
            pltpu.SemaphoreType.DMA((7,)),
            pltpu.SemaphoreType.DMA,
            pltpu.SemaphoreType.REGULAR,
            pltpu.SemaphoreType.REGULAR,
            pltpu.SemaphoreType.DMA((9,)),
            pltpu.SemaphoreType.DMA((9,)),
        ],
        compiler_params=pltpu.CompilerParams(
            collective_id=0, has_side_effects=True, vmem_limit_bytes=56 * mega
        ),
        name="message_layer",
    )(
        node_features,
        message_weight,
        adjacency[0, 0],
        input_weight,
        output_weight,
        cotangent,
        block_index[0, 0],
        block_count,
        send_rows.reshape(peers, 1, 128),
        row_counts[0],
        input_bias[None, :],
        norm_gain[None, :],
    )
    new_features, grad_features, grad_mw, grad_iw, grad_bias, grad_ow, grad_gain = pl.pallas_call(
        finish_kernel,
        out_shape=results,
        in_specs=[hbm] * 7,
        out_specs=[hbm] * 7,
        scratch_shapes=[
            *(pltpu.VMEM(result.shape, result.dtype) for result in results),
            pltpu.SemaphoreType.DMA((16,)),
            pltpu.SemaphoreType.DMA((16,)),
        ],
        compiler_params=pltpu.CompilerParams(has_side_effects=True, vmem_limit_bytes=56 * mega),
        name="write_results",
    )(*outs)
    return (
        new_features, grad_features, grad_mw, grad_iw,
        grad_bias.reshape(half), grad_ow, grad_gain.reshape(half),
    )


def solution(mesh):
    in_specs = (
        P(("loop", "rep"), None),
        P(("loop", "rep"), None),
        P("loop", "rep", None, None, None),
        P("loop", "rep", None, None),
        P("loop", "rep"),
        P("loop", "rep", None, None),
        P("loop", "rep", None),
        P(),
        P(),
        P(),
        P(),
        P(),
    )
    out_specs = (
        P(("loop", "rep"), None),
        P(("loop", "rep"), None),
        P("rep", None),
        P("rep", None),
        P("rep"),
        P("rep", None),
        P("rep"),
    )
    return jax.shard_map(shards, mesh=mesh, in_specs=in_specs, out_specs=out_specs, check_vma=False)
```
